32 devices in a mesh: wide: 8 (over z, x), batch: 4 (over y, core).
Axes of the slice: x: 2, y: 2, z: 4, core: 2. Of those that a mesh axis runs over, the one named last changes fastest.
Arguments:
- pooled: bfloat16 [2, 9216, 4096], P(None, 'wide', 'batch'), may hold values from -6 to 6
- weight: bfloat16 [2, 9216, 4096], P(None, 'wide'), may hold values from -0.09375 to 0.09375
- fc_bias: float32 [2, 4096], P(None, 'wide'), may hold values from -3 to 3
- stitch: float32 [2, 2, 4096], P(None, None, 'wide'), as said below
- cotangent: bfloat16 [2, 4096, 4096], P(None, 'wide', 'batch'), may hold values from -6 to 6
- valid_mask: int32 [9216], P('wide'), may hold values from 0 to 1, as said below
- image_group: int32 [4096], P('batch'), may hold values 0 or 1
- step_rate: float32 [1], replicated, may hold values from 0.004 to 0.02
Outputs:
- stitched: bfloat16 [2, 4096, 4096], P(None, 'wide', 'batch')
- pooled_grad: bfloat16 [2, 9216, 4096], P(None, 'wide', 'batch')
- weight_grad: float32 [2, 9216, 4096], P(None, 'wide', 'batch')
- bias_grad: float32 [2, 4096], P(None, ('wide', 'batch'))
- stitch_grad: float32 [2, 2, 4096], P(None, None, ('wide', 'batch'))
- stitch_new: float32 [2, 2, 4096], P(None, None, ('wide', 'batch'))
The draws below stay inside these ranges and needn't reach their ends.
Inputs may be any that keep to these rules, and one draw needn't show every extreme that they name: valid_mask[k] depends only on k mod 36: it is 1 at 25 of the 36 pooled positions and 0 at the others. `stitch`: diagonal values lie in 0.6 to 1.2, off-diagonal ones in 0 to 0.4.
All inputs are finite; a program needn't handle non-finite values. No bound on the sum of `image_group` on one device may be relied on, other than what follows from the above.
Results may differ from the reference program's by a relative error of at most 0.0049.
Values may be sent and summed in bfloat16 or wider, within the bound.
A program may use at most 192 MiB of HBM per device.

```python
import math
import jax
import jax.numpy as jnp
from jax import lax

FEATURES = 9216
CHANNELS = 4096
TOWERS = 2
IMAGES = 4096


def draw_stitch(key, part):
    key = jax.random.fold_in(key, 11)
    uniform_vals = jax.random.uniform(key, (TOWERS, TOWERS, CHANNELS), jnp.float32)
    diagonal = jnp.eye(TOWERS, dtype=jnp.float32)[:, :, None]
    return diagonal * (0.6 + 0.6 * uniform_vals) + (1.0 - diagonal) * (0.4 * uniform_vals)


def draw_valid_mask(key, part):
    key = jax.random.fold_in(key, 23)
    order = jax.random.permutation(key, 36)
    chosen = (order < 25).astype(jnp.int32)
    position = jnp.arange(FEATURES, dtype=jnp.int32) % 36
    return chosen[position]


def plant(drawn, stream_key, low, high):
    shape = drawn.shape
    spot = [jax.random.randint(jax.random.fold_in(stream_key, axis), (), 0, shape[axis]) for axis in range(len(shape))]
    drawn = drawn.at[tuple(spot)].set(low)
    longest = shape.index(max(shape))
    spot[longest] = (spot[longest] + 1) % shape[longest]
    return drawn.at[tuple(spot)].set(high)


def spiked(entries, stream_key, source, target, shards_of, factor):
    owner, partner = [(jnp.arange(entries.shape[axis_at]) // (entries.shape[axis_at] // shards_of)).reshape([-1 if axis == axis_at else 1 for axis in range(entries.ndim)]) for axis_at in (source, target)]
    chosen = jax.random.permutation(stream_key, shards_of)[partner]
    strong = (owner == chosen) | (owner == (partner + shards_of // 2) % shards_of)
    return jnp.where(strong, factor * entries, entries)


def block_scale(key, shape, shards, least, top_value):
    def one(dim, parts):
        steps = jax.random.uniform(jax.random.fold_in(jax.random.fold_in(key, 6), dim), (parts,), jnp.float32, least / len(shards), top_value / len(shards))
        return jnp.repeat(jnp.exp(steps), shape[dim] // parts).reshape((-1,) + (1,) * (len(shape) - dim - 1))

    loudness = one(*shards[0])
    for cut in shards[1:]:
        loudness = loudness * one(*cut)
    return loudness


def scatter_about(rng, extent, width, limit, pieces=(), kind=jnp.bfloat16):
    array = jax.random.normal(rng, extent, jnp.float32) * width
    if len(pieces) > 0:
        array = block_scale(rng, extent, pieces, -0.22, 0.18) * array
    return jnp.clip(array, min=-limit, max=limit).astype(kind)


def heavy_noise(own_key, shape, scale, limit, pieces, heavy, held_as=jnp.bfloat16):
    entries = scale * jax.random.normal(own_key, shape, jnp.float32)
    if pieces:
        entries = entries * block_scale(own_key, shape, pieces, -0.22, 0.18)
    return jnp.clip(spiked(entries, jax.random.fold_in(own_key, 3), *heavy), -limit, limit).astype(held_as)


def setup_inputs(seed: int = 0) -> dict:
    arg_keys = jax.random.split(jax.random.key(seed), 9)
    pooled = scatter_about(arg_keys[0], (TOWERS, FEATURES, IMAGES), 1.0, 6.0, ((1, 8), (2, 4)))
    weight = heavy_noise(arg_keys[1], (TOWERS, FEATURES, CHANNELS), FEATURES ** -0.5, 0.09375, ((1, 8),), (1, 2, 8, 2.0))
    fc_bias = scatter_about(arg_keys[2], (TOWERS, CHANNELS), 0.5, 3.0, ((1, 8),), jnp.float32)
    stitch = draw_stitch(jax.random.fold_in(arg_keys[8], 71), 0)
    cotangent = scatter_about(arg_keys[4], (TOWERS, CHANNELS, IMAGES), 1.0, 6.0, ((1, 8), (2, 4)))
    valid_mask = draw_valid_mask(jax.random.fold_in(arg_keys[8], 71), 0)
    image_group = plant((jax.random.randint(arg_keys[6], (IMAGES,), 0, 8) < 3).astype(jnp.int32), jax.random.fold_in(arg_keys[6], 1), 0, 1)
    step_rate = jnp.clip(jnp.exp(jax.random.uniform(arg_keys[7], (1,), jnp.float32, math.log(0.004), math.log(0.02))), 0.004, 0.02)
    return {"pooled": pooled, "weight": weight, "fc_bias": fc_bias, "stitch": stitch, "cotangent": cotangent, "valid_mask": valid_mask, "image_group": image_group, "step_rate": step_rate}


@jax.custom_vjp
def low(v):
    return lax.optimization_barrier(v.astype(jnp.bfloat16)).astype(jnp.float32)

@jax.custom_vjp
def low_back(v):
    return v

def low_keep(v):
    return (low(v), None)

def low_pass(kept, grad):
    return (grad,)

def back_keep(v):
    return (v, None)

def back_low(kept, grad):
    return (low(grad),)
low.defvjp(low_keep, low_pass)
low_back.defvjp(back_keep, back_low)

def reference(pooled, weight, fc_bias, stitch, cotangent, valid_mask, image_group, step_rate):
    highest = lax.Precision.HIGHEST
    factor = 1.0 - image_group[None, :].astype(jnp.float32) * (1.0 - valid_mask[:, None].astype(jnp.float32))

    def forward_pass(pooled_f, weight_f, bias_f, stitch_f):
        masked = pooled_f * factor[None]
        product = jnp.einsum('tkc,tkb->tcb', weight_f, masked, precision=highest)
        product = low_back(product)
        hidden = jax.nn.gelu(product + bias_f[:, :, None], approximate=True)
        return jnp.einsum('ijc,jcb->icb', stitch_f, hidden, precision=highest)
    outputs, pull_back = jax.vjp(forward_pass, pooled.astype(jnp.float32), weight.astype(jnp.float32), fc_bias, stitch)
    pooled_g, weight_g, bias_g, stitch_g = pull_back(cotangent.astype(jnp.float32))
    stitch_new = stitch - step_rate[0] * stitch_g
    return (outputs.astype(jnp.bfloat16), pooled_g.astype(jnp.bfloat16), weight_g, bias_g, stitch_g, stitch_new)
```

```python
import functools
import math

import jax
import jax.numpy as jnp
from jax import lax
from jax.experimental import pallas as pl
from jax.experimental.pallas import tpu as pltpu
from jax.sharding import PartitionSpec as P

MESH = pl.DeviceIdType.MESH
BLK = 128
NZ, NX = 4, 2
F32, BF16 = jnp.float32, jnp.bfloat16
NT = (((1,), (1,)), ((), ()))
ROOT = math.sqrt(2.0 / math.pi)
CUBE = 0.044715
PIECES = 3


class Dims:
    def __init__(self, pooled, weight, cotangent):
        self.towers, self.feats, self.images = pooled.shape
        self.chans = weight.shape[2]
        self.own = cotangent.shape[1]
        self.subs = self.own // BLK
        self.parts = 2
        self.rows = self.images // self.parts
        self.rx = (self.rows * 19 // 32) // 16 * 16
        self.rz = self.rows - self.rx
        self.units = self.towers * self.subs * self.parts
        self.cols = NZ * NX * BLK
        self.third = self.feats // PIECES


def chunks(count, size=64):
    return [(r, min(size, count - r)) for r in range(0, count, size)]


def kernel(
    dm,
    step_ref, w_hbm, xm_hbm, xt_hbm, cot, bias, st, st8,
    out_s, pg_hbm, wg_hbm, out_small, xp_hbm,
    wb, xt, xb, xpb, acc, fwd, gat, gatp,
    x1_s, x1_r, xr_s, xr_r, zr_s, zr_r, zown, z2_s, z2_r,
    own, y_s, y_r, hid0, htmp, pgb, sacc, sum_s, sum_r,
    m_w, m_ld, m_x1s, m_x1r, m_xrs, m_xrr, m_zrs, m_zrr, m_z2s, m_z2r, m_z4s, m_z4r,
    m_gxs, m_gxr, m_gzs, m_gzr, m_x5s, m_x5r, m_cs, m_cr, m_ys, m_yr, m_ss, m_sr, m_xps, m_xpr, m_own, m_pg,
):
    n_units, rows, rx, rz = dm.units, dm.rows, dm.rx, dm.rz
    wi, bi = lax.axis_index("wide"), lax.axis_index("batch")
    z, x = wi // NX, wi % NX
    y, core = bi // 2, bi % 2
    x_dev = (z * NX + 1 - x, bi)
    c_dev = (wi, y * 2 + 1 - core)
    y_dev = (wi, (1 - y) * 2 + core)

    def z_dev(d):
        return (wi + NX, bi) if d == 0 else (wi - NX, bi)

    def far(d):
        return z if d == 0 else NZ - 1 - z

    def rc(src, dst, ss, rs, dev):
        return pltpu.make_async_remote_copy(src, dst, ss, rs, device_id=dev, device_id_type=MESH)

    def al(v, k=BLK):
        return pl.multiple_of(v, k)

    def tower(n):
        return n // (dm.subs * dm.parts)

    def sub(n):
        return (n // dm.parts) % dm.subs

    def part(n):
        return n % dm.parts

    def gpair(n):
        return (n // dm.parts) % 2

    def col(o, xx):
        return al((o * NX + xx) * BLK)

    def w_load(p, w):
        t, u = p // dm.subs, p % dm.subs
        return pltpu.make_async_copy(
            w_hbm.at[t, :, pl.ds(al(w * dm.own + u * BLK), BLK)], wb.at[p % 4, :, pl.ds(w * BLK, BLK)], m_w.at[p % 4, w]
        )

    def xt_load(t):
        return pltpu.make_async_copy(xt_hbm.at[t], xt.at[t], m_ld.at[t])

    def xb_load(t):
        return pltpu.make_async_copy(xm_hbm.at[t], xb, m_ld.at[2])

    def xpb_load(t):
        return pltpu.make_async_copy(xp_hbm.at[t], xpb, m_ld.at[3])

    def x1_copy(n, o):
        return rc(x1_s.at[o], x1_r.at[n % 2, o], m_x1s.at[o], m_x1r.at[n % 2, o], x_dev)

    def xr_copy(n, d, h):
        return rc(xr_s.at[d, h], xr_r.at[n % 2, d, h], m_xrs.at[d, h], m_xrr.at[n % 2, d, h], z_dev(d))

    def zr_copy(n, d, h):
        return rc(zr_s.at[d, h], zr_r.at[n % 2, d, h], m_zrs.at[d, h], m_zrr.at[n % 2, d, h], z_dev(d))

    def z2_copy(n):
        return rc(z2_s, z2_r.at[n % 2], m_z2s, m_z2r.at[n % 2], x_dev)

    def g_x(n, o, xx):
        return gat.at[gpair(n), pl.ds(al(part(n) * rows, 16), rx), pl.ds(col(o, xx), BLK)]

    def g_z(n, o, xx, width):
        return gat.at[gpair(n), pl.ds(al(part(n) * rows + rx, 16), rz), pl.ds(col(o, xx), width)]

    def z4_copy(n):
        return rc(g_z(n, z, x, BLK), g_z(n, z, x, BLK), m_z4s, m_z4r.at[n % 2], x_dev)

    def gx_copy(n, d, h):
        o = z - h if d == 0 else z + h
        return rc(g_x(n, o, x), g_x(n, o, x), m_gxs.at[d, h], m_gxr.at[n % 2, d, h], z_dev(d))

    def gz_copy(n, d, h):
        o = z - h if d == 0 else z + h
        blk = g_z(n, o, 0, NX * BLK)
        return rc(blk, blk, m_gzs.at[d, h], m_gzr.at[n % 2, d, h], z_dev(d))

    def x5_copy(n, o, xx):
        return rc(g_x(n, o, xx), g_x(n, o, xx), m_x5s.at[o], m_x5r.at[n % 2, o], x_dev)

    def c_copy(n, e):
        r = pl.ds(al(part(n) * rows, 16), rows)
        return rc(
            gat.at[gpair(n), r, pl.ds(col(2 * e + 1 - core, 0), NX * BLK)],
            gatp.at[gpair(n), r, pl.ds(e * NX * BLK, NX * BLK)],
            m_cs.at[e], m_cr.at[n % 4, e], c_dev,
        )

    def y_copy(p, q):
        k = pl.ds(q * dm.third, dm.third)
        return rc(y_s.at[k], y_r.at[p % 2, k], m_ys.at[q], m_yr.at[p % 2, q], y_dev)

    def own_copy(p, q, e):
        t, u = p // dm.subs, p % dm.subs
        k = pl.ds(q * dm.third, dm.third)
        return pltpu.make_async_copy(
            own.at[p % 2, k, pl.ds(e * BLK, BLK)],
            wg_hbm.at[t, k, pl.ds(al(e * dm.own + u * BLK), BLK)],
            m_own.at[p % 2, q, e],
        )

    def pg_copy(t, s):
        return pltpu.make_async_copy(pgb, pg_hbm.at[t, :, pl.ds(al(s * rows), rows)], m_pg)

    def sum_copy(k):
        to = lax.rem(bi + k, 4)
        return rc(sum_s.at[to], sum_r.at[k - 1], m_ss.at[k - 1], m_sr.at[k - 1], (wi, to))

    xp_copy = rc(xm_hbm, xp_hbm, m_xps, m_xpr, c_dev)

    def forward(n, k):
        fwd[n % 2, :, pl.ds(k * 256, 256)] = jnp.dot(
            xt[tower(n), pl.ds(al(part(n) * rows, 16), rows), :],
            wb[(n // dm.parts) % 4, :, pl.ds(k * 256, 256)],
            preferred_element_type=F32,
        )

    def x1_send(n, q):
        o = (
            jnp.where(z < 2, 3, 0),
            jnp.where(z < 2, 2, 1),
            jnp.where(z < 2, 1 - z, 5 - z),
            z,
        )[q]

        @pl.when(n >= 1)
        def _():
            x1_copy(n, o).wait_send()

        for r, m in chunks(rx):
            x1_s[o, r : r + m] = fwd[n % 2, r : r + m, pl.ds(col(o, 1 - x), BLK)].astype(BF16)
        x1_copy(n, o).start()

    def xr_hop(n, h):
        for d in (0, 1):
            o = 3 - h + z if d == 0 else h - 3 + z

            @pl.when(far(d) <= h)
            def _():
                x1_copy(n, o).wait_recv()
                if h:
                    @pl.when(far(d) >= 1)
                    def _():
                        xr_copy(n, d, h - 1).wait_recv()

                @pl.when(n >= 1)
                def _():
                    xr_copy(n, d, h).wait_send()

                for r, m in chunks(rx):
                    v = fwd[n % 2, r : r + m, pl.ds(col(o, x), BLK)] + x1_r[n % 2, o, r : r + m].astype(F32)
                    if h:
                        v = v + xr_r[n % 2, d, h - 1, r : r + m].astype(F32)
                    xr_s[d, h, r : r + m] = v.astype(BF16)
                xr_copy(n, d, h).start()

    def zr_hop(n, h):
        for d in (0, 1):
            o = 3 - h + z if d == 0 else h - 3 + z

            @pl.when(far(d) <= h)
            def _():
                if h:
                    @pl.when(far(d) >= 1)
                    def _():
                        zr_copy(n, d, h - 1).wait_recv()

                @pl.when(n >= 1)
                def _():
                    zr_copy(n, d, h).wait_send()

                for r, m in chunks(rz):
                    v = fwd[n % 2, rx + r : rx + r + m, pl.ds(col(o, 0), NX * BLK)]
                    if h:
                        v = v + zr_r[n % 2, d, h - 1, r : r + m].astype(F32)
                    zr_s[d, h, r : r + m] = v.astype(BF16)
                zr_copy(n, d, h).start()

    def z_sum(n):
        for d in (0, 1):
            @pl.when(far(d) >= 1)
            def _():
                zr_copy(n, d, 2).wait_recv()

        @pl.when(n >= 1)
        def _():
            z2_copy(n).wait_send()

        for xx in (1 - x, x):
            for r, m in chunks(rz):
                lanes = pl.ds(al(xx * BLK), BLK)
                v = (
                    fwd[n % 2, rx + r : rx + r + m, pl.ds(col(z, xx), BLK)]
                    + zr_r[n % 2, 0, 2, r : r + m, lanes].astype(F32)
                    + zr_r[n % 2, 1, 2, r : r + m, lanes].astype(F32)
                )
                if xx is x:
                    zown[r : r + m] = v
                else:
                    z2_s[r : r + m] = v.astype(BF16)
            if xx is not x:
                z2_copy(n).start()

    def finish(n, row0, count, total):
        t, u = tower(n), sub(n)
        lanes = pl.ds(al(u * BLK), BLK)
        base = part(n) * rows + row0
        b_row = bias[t, :, lanes]
        from0, from1 = st[t, :, lanes], st[2 + t, :, lanes]
        for r, m in chunks(count):
            at = pl.ds(al(base + r, 16), m)
            v = total(r, m) + b_row
            sq = v * v
            th = jnp.tanh(ROOT * v * (1.0 + CUBE * sq))
            half = 0.5 * (1.0 + th)
            htmp[r : r + m] = v * half
            slope = half + 0.5 * v * (1.0 - th * th) * (ROOT * (1.0 + 3.0 * CUBE * sq))
            up0, up1 = cot[0, at, lanes].astype(F32), cot[1, at, lanes].astype(F32)
            grad = (from0 * up0 + from1 * up1) * slope
            sacc[u, t] += jnp.sum(grad.reshape(m // 8, 8, BLK), axis=0)
            gat[gpair(n), at, pl.ds(col(z, x), BLK)] = grad.astype(BF16)

    def mix(n, row0, count):
        t, u = tower(n), sub(n)
        lanes = pl.ds(al(u * BLK), BLK)
        base = part(n) * rows + row0

        @pl.when(t == 0)
        def _():
            for r, m in chunks(count):
                hid0[pl.ds(al(base + r, 16), m), lanes] = htmp[r : r + m]

        @pl.when(t == 1)
        def _():
            for r, m in chunks(count):
                at = pl.ds(al(base + r, 16), m)
                h = hid0[at, lanes], htmp[r : r + m]
                for i in (0, 1):
                    up = cot[i, at, lanes].astype(F32)
                    out_s[i, at, lanes] = (st[2 * i, :, lanes] * h[0] + st[2 * i + 1, :, lanes] * h[1]).astype(BF16)
                    for j in (0, 1):
                        sacc[u, 2 + 2 * i + j] += jnp.sum((up * h[j]).reshape(m // 8, 8, BLK), axis=0)

    def z_final(n):
        z2_copy(n).wait_recv()
        finish(n, rx, rz, lambda r, m: zown[r : r + m] + z2_r[n % 2, r : r + m].astype(F32))

        @pl.when(n >= 1)
        def _():
            z4_copy(n).wait_send()

        z4_copy(n).start()
        mix(n, rx, rz)

    def x_final(n):
        x1_copy(n, z).wait_recv()
        for d in (0, 1):
            @pl.when(far(d) >= 1)
            def _():
                xr_copy(n, d, 2).wait_recv()

        def total(r, m):
            return (
                fwd[n % 2, r : r + m, pl.ds(col(z, x), BLK)]
                + x1_r[n % 2, z, r : r + m].astype(F32)
                + xr_r[n % 2, 0, 2, r : r + m].astype(F32)
                + xr_r[n % 2, 1, 2, r : r + m].astype(F32)
            )

        finish(n, 0, rx, total)
        for d in (0, 1):
            gather_hop(gx_copy, n, d, 0)
        x5_send(n, z)
        mix(n, 0, rx)

    def gather_hop(copy, n, d, h):
        @pl.when((far(d) >= h) & (far(d) <= 2))
        def _():
            @pl.when(n >= 1)
            def _():
                copy(n, d, h).wait_send()

            copy(n, d, h).start()

    def x5_send(n, o):
        @pl.when(n >= 1)
        def _():
            x5_copy(n, o, x).wait_send()

        x5_copy(n, o, x).start()

    def gather_arrive(copy, n, h, forward_x):
        for d in (0, 1):
            @pl.when(far(d) >= h + 1)
            def _():
                copy(n, d, h).wait_recv()
                if h < 2:
                    gather_hop(copy, n, d, h + 1)
                if forward_x:
                    x5_send(n, z - 1 - h if d == 0 else z + 1 + h)

    def gathered(n):
        for o in range(NZ):
            x5_copy(n, o, 1 - x).wait_recv()
        for e in (0, 1):
            @pl.when(n >= 1)
            def _():
                c_copy(n, e).wait_send()

            c_copy(n, e).start()

    def back_pooled(n):
        t, s = tower(n), part(n)
        lanes = pl.ds(al(s * rows), rows)

        @pl.loop(0, PIECES)
        def _(q):
            k = pl.ds(al(q * dm.third, 16), dm.third)
            acc[k, lanes] += lax.dot_general(
                wb[(n // dm.parts) % 4, k, :],
                gat[gpair(n), pl.ds(al(s * rows, 16), rows), :],
                NT,
                preferred_element_type=F32,
            )

        @pl.when(sub(n) == dm.subs - 1)
        def _():
            @pl.when((t > 0) | (s > 0))
            def _():
                pg_copy(t, s).wait()

            @pl.loop(0, dm.feats // 32)
            def _(k):
                at = pl.ds(al(k * 32, 32), 32)
                pgb[at] = acc[at, lanes].astype(BF16)
                acc[at, lanes] = jnp.zeros((32, rows), F32)

            pg_copy(t, s).start()

    def y_arrive(p, q):
        k = pl.ds(q * dm.third, dm.third)
        y_copy(p, q).wait_recv()
        for r, m in chunks(dm.third):
            at = pl.ds(q * dm.third + r, m)
            own[p % 2, at] += y_r[p % 2, at].astype(F32)
        for e in (0, 1):
            own_copy(p, q, e).start()

    def back_weight(p, q):
        if q == 0:
            for n in (2 * p, 2 * p + 1):
                for e in (0, 1):
                    c_copy(n, e).wait_recv()

            @pl.when(p % dm.subs == 0)
            def _():
                xb_load(p // dm.subs).wait()
                xpb_load(p // dm.subs).wait()

        @pl.when(p >= 1)
        def _():
            y_arrive(p - 1, q)
            y_copy(p, q).wait_send()

        @pl.when(p >= 2)
        def _():
            for e in (0, 1):
                own_copy(p, q, e).wait()

        k = pl.ds(q * dm.third, dm.third)

        def grads(yy):
            lanes = pl.ds(col(2 * yy + core, 0), NX * BLK)
            return jnp.dot(xb[k, :], gat[p % 2, :, lanes], preferred_element_type=F32) + jnp.dot(
                xpb[k, :], gatp[p % 2, :, pl.ds(al(yy * NX * BLK), NX * BLK)], preferred_element_type=F32
            )

        y_s[k, :] = grads(1 - y).astype(BF16)
        y_copy(p, q).start()
        own[p % 2, k, :] = grads(y)

    def sums_send():
        for u in range(dm.subs):
            for j in range(6):
                sum_s[u, j : j + 1] = jnp.sum(sacc[u, j], axis=0, keepdims=True)
            sum_s[u, 6:8] = jnp.zeros((2, BLK), F32)
        for k in (1, 2, 3):
            sum_copy(k).start()

    for w in range(NZ * NX):
        w_load(0, w).start()
    xt_load(0).start()
    for w in range(NZ * NX):
        w_load(1, w).start()
    xt_load(1).start()
    xb_load(0).start()

    barrier = pltpu.get_barrier_semaphore()
    peers = [x_dev] + [(wi, lax.rem(bi + k, 4)) for k in (1, 2, 3)]
    for dev in peers:
        pl.semaphore_signal(barrier, inc=1, device_id=dev, device_id_type=MESH)
    for d in (0, 1):
        @pl.when(far(d) <= 2)
        def _():
            pl.semaphore_signal(barrier, inc=1, device_id=z_dev(d), device_id_type=MESH)

    sacc[...] = jnp.zeros_like(sacc)

    @pl.loop(0, dm.feats // 8)
    def _(k):
        acc[pl.ds(al(k * 8, 8), 8)] = jnp.zeros((8, dm.images), F32)

    for d in (0, 1):
        @pl.when(far(d) == 0)
        def _():
            for s in (0, 1):
                for h in range(3):
                    xr_r[s, d, h] = jnp.zeros((rx, BLK), BF16)
                    zr_r[s, d, h] = jnp.zeros((rz, NX * BLK), BF16)

    pl.semaphore_wait(barrier, jnp.where((z == 0) | (z == NZ - 1), len(peers) + 1, len(peers) + 2))
    xp_copy.start()

    for w in range(NZ * NX):
        w_load(0, w).wait()
    xt_load(0).wait()
    for k in range(4):
        forward(0, k)

    def tick(i, carry):
        a, b, c = i, i - 1, i - 2
        on_a = i < n_units
        on_b = (i >= 1) & (i <= n_units)
        on_c = (i >= 2) & (i <= n_units + 1)
        on_f = i + 1 < n_units
        p = lax.div(i - 4, 2)
        on_p = (i >= 4) & (i % 2 == 0)

        @pl.when(on_a)
        def _():
            x1_send(a, 0)
            zr_hop(a, 0)

        @pl.when((i % 2 == 0) & (i // 2 + 2 < dm.towers * dm.subs))
        def _():
            for w in range(NZ * NX):
                w_load(i // 2 + 2, w).start()

        @pl.when(on_b)
        def _():
            z_final(b)
            x_final(b)

        @pl.when(on_c)
        def _():
            gather_arrive(gz_copy, c, 0, False)

        @pl.when(on_f)
        def _():
            @pl.when(i % 2 == 1)
            def _():
                for w in range(NZ * NX):
                    w_load((i + 1) // 2, w).wait()

            @pl.when(i + 1 == n_units // 2)
            def _():
                xt_load(1).wait()

            forward(i + 1, 0)

        @pl.when(on_p)
        def _():
            back_weight(p, 0)

        @pl.when(on_a)
        def _():
            x1_send(a, 1)
            zr_hop(a, 1)
            xr_hop(a, 0)

        @pl.when(on_c)
        def _():
            gather_arrive(gz_copy, c, 1, False)

        @pl.when(on_b)
        def _():
            gather_arrive(gx_copy, b, 0, True)

        @pl.when(on_f)
        def _():
            forward(i + 1, 1)

        @pl.when(on_p)
        def _():
            back_weight(p, 1)

        @pl.when(on_a)
        def _():
            x1_send(a, 2)
            zr_hop(a, 2)
            xr_hop(a, 1)

        @pl.when(on_b)
        def _():
            gather_arrive(gx_copy, b, 1, True)

        @pl.when(on_c)
        def _():
            gather_arrive(gz_copy, c, 2, False)
            gathered(c)

        @pl.when(on_f)
        def _():
            forward(i + 1, 2)

        @pl.when(on_p)
        def _():
            back_weight(p, 2)

        @pl.when(on_a)
        def _():
            x1_send(a, 3)
            z_sum(a)
            xr_hop(a, 2)

        @pl.when(on_b)
        def _():
            z4_copy(b).wait_recv()
            for d in (0, 1):
                gather_hop(gz_copy, b, d, 0)
            gather_arrive(gx_copy, b, 2, True)

        @pl.when(on_c)
        def _():
            back_pooled(c)

        @pl.when(on_f)
        def _():
            forward(i + 1, 3)

        @pl.when(i == 3)
        def _():
            xp_copy.wait_recv()
            xpb_load(0).start()

        @pl.when(i == 2 * dm.subs + 3)
        def _():
            xb_load(1).start()
            xpb_load(1).start()

        @pl.when(i == n_units)
        def _():
            sums_send()

        return carry

    lax.fori_loop(0, n_units + 3, tick, 0)

    last, pairs = n_units - 1, dm.towers * dm.subs
    for k in (1, 2, 3):
        sum_copy(k).wait_recv()
    total = sum_s[bi] + sum_r[0] + sum_r[1] + sum_r[2]
    out_small[0] = total
    out_small[1] = st8[:, pl.ds(al(bi * BLK), BLK)] - step_ref[0] * total
    for q in range(PIECES):
        y_arrive(pairs - 1, q)
    for q in range(PIECES):
        for e in (0, 1):
            own_copy(pairs - 2, q, e).wait()
            own_copy(pairs - 1, q, e).wait()
        y_copy(pairs - 1, q).wait_send()
    pg_copy(1, 1).wait()
    xp_copy.wait_send()
    for k in (1, 2, 3):
        sum_copy(k).wait_send()
    for e in (0, 1):
        c_copy(last, e).wait_send()
    for o in range(NZ):
        x1_copy(last, o).wait_send()
        x5_copy(last, o, x).wait_send()
    z2_copy(last).wait_send()
    z4_copy(last).wait_send()
    for d in (0, 1):
        for h in range(3):
            @pl.when(far(d) <= h)
            def _():
                xr_copy(last, d, h).wait_send()
                zr_copy(last, d, h).wait_send()

            @pl.when((far(d) >= h) & (far(d) <= 2))
            def _():
                gx_copy(last, d, h).wait_send()
                gz_copy(last, d, h).wait_send()


def fused(pooled, weight, fc_bias, stitch, cotangent, factor, step_rate):
    dm = Dims(pooled, weight, cotangent)
    masked = pooled * factor[None]
    masked_t = jnp.swapaxes(masked, 1, 2)
    cot_t = jnp.swapaxes(cotangent, 1, 2)
    towers, feats, images, own = dm.towers, dm.feats, dm.images, dm.own
    rows, rx, rz, cols = dm.rows, dm.rx, dm.rz, dm.cols
    dma = pltpu.SemaphoreType.DMA
    vm = pltpu.VMEM
    scratch = [
        vm((4, feats, cols), BF16),
        vm((towers, images, feats), BF16),
        vm((feats, images), BF16),
        vm((feats, images), BF16),
        vm((feats, images), F32),
        vm((2, rows, cols), F32),
        vm((2, images, cols), BF16),
        vm((2, images, cols // 2), BF16),
        vm((NZ, rx, BLK), BF16),
        vm((2, NZ, rx, BLK), BF16),
        vm((2, 3, rx, BLK), BF16),
        vm((2, 2, 3, rx, BLK), BF16),
        vm((2, 3, rz, NX * BLK), BF16),
        vm((2, 2, 3, rz, NX * BLK), BF16),
        vm((rz, BLK), F32),
        vm((rz, BLK), BF16),
        vm((2, rz, BLK), BF16),
        vm((2, feats, NX * BLK), F32),
        vm((feats, NX * BLK), BF16),
        vm((2, feats, NX * BLK), BF16),
        vm((images, own), F32),
        vm((max(rx, rz), BLK), F32),
        vm((feats, rows), BF16),
        vm((dm.subs, 6, 8, BLK), F32),
        vm((dm.subs, 8, BLK), F32),
        vm((3, 8, BLK), F32),
    ] + [
        dma(shape)
        for shape in (
            (4, NZ * NX), (4,), (NZ,), (2, NZ), (2, 3), (2, 2, 3), (2, 3), (2, 2, 3), (), (2,), (), (2,),
            (2, 3), (2, 2, 3), (2, 3), (2, 2, 3), (NZ,), (2, NZ), (2,), (4, 2), (PIECES,), (2, PIECES), (3,), (3,), (), (),
            (2, PIECES, 2), (),
        )
    ]
    anyspace = pl.BlockSpec(memory_space=pl.ANY)
    inside = pl.BlockSpec(memory_space=pltpu.VMEM)
    st8 = jnp.pad(stitch.reshape(4, own), ((2, 2), (0, 0)))
    stitched_t, pooled_raw, weight_grad, small, _ = pl.pallas_call(
        functools.partial(kernel, dm),
        name="stitch_fc6",
        out_shape=[
            jax.ShapeDtypeStruct((2, images, own), BF16),
            jax.ShapeDtypeStruct((towers, feats, images), BF16),
            jax.ShapeDtypeStruct((towers, feats, images), F32),
            jax.ShapeDtypeStruct((2, 8, BLK), F32),
            jax.ShapeDtypeStruct((towers, feats, images), BF16),
        ],
        in_specs=[pl.BlockSpec(memory_space=pltpu.SMEM), anyspace, anyspace, anyspace, inside, inside, inside, inside],
        out_specs=[inside, anyspace, anyspace, inside, anyspace],
        scratch_shapes=scratch,
        compiler_params=pltpu.CompilerParams(collective_id=1, has_side_effects=True, vmem_limit_bytes=60 * 2**20),
        cost_estimate=pl.CostEstimate(
            flops=6 * towers * feats * images * dm.chans, bytes_accessed=60 * 2**20, transcendentals=towers * images * own
        ),
    )(
        step_rate, weight, masked, masked_t, cot_t,
        fc_bias.reshape(towers, 1, own), stitch.reshape(4, 1, own), st8,
    )
    stitched = jnp.swapaxes(stitched_t, 1, 2)
    pooled_grad = pooled_raw * factor[None]
    sums, moved = small[0], small[1]
    return (
        stitched,
        pooled_grad,
        weight_grad,
        sums[:2],
        sums[2:6].reshape(2, 2, BLK),
        moved[2:6].reshape(2, 2, BLK),
    )


def gelu_local(values):
    return jax.nn.gelu(values, approximate=True)


def plain(pooled, weight, fc_bias, stitch, cotangent, factor, step_rate):
    highest = lax.Precision.HIGHEST
    masked = pooled * factor[None]
    owned = weight.shape[2] // lax.axis_size("wide")
    summed = lax.psum_scatter(
        jnp.einsum("tkc,tkb->ctb", weight, masked, preferred_element_type=F32), "wide", scatter_dimension=0, tiled=True
    )
    pre_act = summed + jnp.transpose(fc_bias)[:, :, None]
    hidden, gelu_back = jax.vjp(gelu_local, pre_act)
    stitched = jnp.einsum("ijc,cjb->icb", stitch, hidden, precision=highest)
    upstream = cotangent.astype(F32)
    stitch_part = jnp.einsum("icb,cjb->ijc", upstream, hidden, precision=highest)
    hidden_grad = jnp.einsum("ijc,icb->cjb", stitch, upstream, precision=highest)
    pre_grad = gelu_back(hidden_grad)[0]
    bias_part = jnp.transpose(jnp.sum(pre_grad, axis=2))
    pre_low = pre_grad.astype(BF16)
    bias_grad = lax.psum_scatter(bias_part, "batch", scatter_dimension=1, tiled=True)
    stitch_grad = lax.psum_scatter(stitch_part, "batch", scatter_dimension=2, tiled=True)
    portion = lax.all_gather(pre_low, "wide", axis=0, tiled=True)
    input_sum = jnp.einsum("tkc,ctb->tkb", weight, portion, preferred_element_type=F32)
    block_grad = jnp.einsum("tkb,ctb->tkc", masked, portion, preferred_element_type=F32)
    pooled_grad = (input_sum * factor.astype(F32)[None]).astype(BF16)
    weight_grad = lax.psum_scatter(block_grad, "batch", scatter_dimension=2, tiled=True)
    share = owned // lax.axis_size("batch")
    stitch_mine = lax.dynamic_slice_in_dim(stitch, lax.axis_index("batch") * share, share, 2)
    stitch_new = stitch_mine - step_rate[0] * stitch_grad
    return stitched.astype(BF16), pooled_grad, weight_grad, bias_grad, stitch_grad, stitch_new


def fits(mesh, pooled, weight, cotangent):
    return (
        (mesh.shape["wide"], mesh.shape["batch"]) == (NZ * NX, 4)
        and pooled.shape[0] == 2
        and cotangent.shape[1] == 4 * BLK
        and weight.shape[2] == NZ * NX * cotangent.shape[1]
        and pooled.shape[2] % 512 == 0
        and pooled.shape[1] % (16 * PIECES) == 0
    )


def solution(mesh):
    def body(pooled, weight, fc_bias, stitch, cotangent, valid_mask, image_group, step_rate):
        factor = 1.0 - image_group[None, :].astype(F32) * (1.0 - valid_mask[:, None].astype(F32))
        form = fused if fits(mesh, pooled, weight, cotangent) else plain
        return form(pooled, weight, fc_bias, stitch, cotangent, factor.astype(BF16), step_rate)

    return jax.shard_map(
        body,
        mesh=mesh,
        in_specs=(
            P(None, "wide", "batch"),
            P(None, "wide", None),
            P(None, "wide"),
            P(None, None, "wide"),
            P(None, "wide", "batch"),
            P("wide"),
            P("batch"),
            P(),
        ),
        out_specs=(
            P(None, "wide", "batch"),
            P(None, "wide", "batch"),
            P(None, "wide", "batch"),
            P(None, ("wide", "batch")),
            P(None, None, ("wide", "batch")),
            P(None, None, ("wide", "batch")),
        ),
        check_vma=False,
    )
```

```python
import functools
import math

import jax
import jax.numpy as jnp
from jax import lax
from jax.experimental import pallas as pl
from jax.experimental.pallas import tpu as pltpu
from jax.sharding import PartitionSpec as P

MESH = pl.DeviceIdType.MESH
BLK = 128
NZ, NX = 4, 2
F32, BF16 = jnp.float32, jnp.bfloat16
NT = (((1,), (1,)), ((), ()))
ROOT = math.sqrt(2.0 / math.pi)
CUBE = 0.044715
PIECES = 3
CUTS = 4


class Dims:
    def __init__(self, pooled, weight, cotangent):
        self.towers, self.feats, self.images = pooled.shape
        self.chans = weight.shape[2]
        self.own = cotangent.shape[1]
        self.subs = self.own // BLK
        self.parts = 2
        self.rows = self.images // self.parts
        self.rx = (self.rows * 19 // 32) // 16 * 16
        self.rz = self.rows - self.rx
        self.units = self.towers * self.subs * self.parts
        self.cols = NZ * NX * BLK
        self.third = self.feats // PIECES


def chunks(count, size=64):
    return [(r, min(size, count - r)) for r in range(0, count, size)]


def kernel(
    dm,
    step_ref, w_hbm, p_hbm, c_hbm, bias, st, valid, group,
    s_hbm, pg_hbm, wg_hbm, out_b, out_sg, out_sn,
    wb, xt, xb, xpb, hole, small_img, craw, cot, stmp, sbuf, acc, fwd, gat, gatp,
    x1_s, x1_r, xr_s, xr_r, zr_s, zr_r, zown, z2_s, z2_r,
    own, y_s, y_r, hid0, htmp, pgb, sacc, sum_s, sum_r,
    m_w, m_ld, m_x1s, m_x1r, m_xrs, m_xrr, m_zrs, m_zrr, m_z2s, m_z2r, m_z4s, m_z4r,
    m_gxs, m_gxr, m_gzs, m_gzr, m_x5s, m_x5r, m_cs, m_cr, m_ys, m_yr, m_ss, m_sr, m_xps, m_xpr, m_own, m_pg,
    m_cot, m_out,
):
    n_units, rows, rx, rz = dm.units, dm.rows, dm.rx, dm.rz
    wi, bi = lax.axis_index("wide"), lax.axis_index("batch")
    z, x = wi // NX, wi % NX
    y, core = bi // 2, bi % 2
    x_dev = (z * NX + 1 - x, bi)
    c_dev = (wi, y * 2 + 1 - core)
    y_dev = (wi, (1 - y) * 2 + core)

    def z_dev(d):
        return (wi + NX, bi) if d == 0 else (wi - NX, bi)

    def far(d):
        return z if d == 0 else NZ - 1 - z

    def rc(src, dst, ss, rs, dev):
        return pltpu.make_async_remote_copy(src, dst, ss, rs, device_id=dev, device_id_type=MESH)

    def al(v, k=BLK):
        return pl.multiple_of(v, k)

    def tower(n):
        return n // (dm.subs * dm.parts)

    def sub(n):
        return (n // dm.parts) % dm.subs

    def part(n):
        return n % dm.parts

    def gpair(n):
        return (n // dm.parts) % 2

    def col(o, xx):
        return al((o * NX + xx) * BLK)

    def w_load(p, w):
        t, u = p // dm.subs, p % dm.subs
        return pltpu.make_async_copy(
            w_hbm.at[t, :, pl.ds(al(w * dm.own + u * BLK), BLK)], wb.at[p % 4, :, pl.ds(w * BLK, BLK)], m_w.at[p % 4, w]
        )

    def x_load(t, s):
        lanes = pl.ds(s * rows, rows)
        return pltpu.make_async_copy(p_hbm.at[t, :, lanes], xb.at[t, :, lanes], m_ld.at[t, s])

    def cot_load(n, i):
        return pltpu.make_async_copy(
            c_hbm.at[i, pl.ds(al(sub(n) * BLK), BLK), pl.ds(al(part(n) * rows), rows)], craw.at[n % 2, i], m_cot.at[n % 2, i]
        )

    def s_copy(n, i):
        return pltpu.make_async_copy(
            sbuf.at[n % 2, i], s_hbm.at[i, pl.ds(al(sub(n) * BLK), BLK), pl.ds(al(part(n) * rows), rows)], m_out.at[n % 2, i]
        )

    def xp_copy(t):
        return rc(xb.at[t], xpb.at[t], m_xps.at[t], m_xpr.at[t], c_dev)

    def x1_copy(n, o):
        return rc(x1_s.at[o], x1_r.at[n % 2, o], m_x1s.at[o], m_x1r.at[n % 2, o], x_dev)

    def xr_copy(n, d, h):
        return rc(xr_s.at[d, h], xr_r.at[n % 2, d, h], m_xrs.at[d, h], m_xrr.at[n % 2, d, h], z_dev(d))

    def zr_copy(n, d, h):
        return rc(zr_s.at[d, h], zr_r.at[n % 2, d, h], m_zrs.at[d, h], m_zrr.at[n % 2, d, h], z_dev(d))

    def z2_copy(n):
        return rc(z2_s, z2_r.at[n % 2], m_z2s, m_z2r.at[n % 2], x_dev)

    def g_x(n, o, xx):
        return gat.at[gpair(n), pl.ds(al(part(n) * rows, 16), rx), pl.ds(col(o, xx), BLK)]

    def g_z(n, o, xx, width):
        return gat.at[gpair(n), pl.ds(al(part(n) * rows + rx, 16), rz), pl.ds(col(o, xx), width)]

    def z4_copy(n):
        return rc(g_z(n, z, x, BLK), g_z(n, z, x, BLK), m_z4s, m_z4r.at[n % 2], x_dev)

    def gx_copy(n, d, h):
        o = z - h if d == 0 else z + h
        return rc(g_x(n, o, x), g_x(n, o, x), m_gxs.at[d, h], m_gxr.at[n % 2, d, h], z_dev(d))

    def gz_copy(n, d, h):
        o = z - h if d == 0 else z + h
        blk = g_z(n, o, 0, NX * BLK)
        return rc(blk, blk, m_gzs.at[d, h], m_gzr.at[n % 2, d, h], z_dev(d))

    def x5_copy(n, o, xx):
        return rc(g_x(n, o, xx), g_x(n, o, xx), m_x5s.at[o], m_x5r.at[n % 2, o], x_dev)

    def c_copy(n, e):
        r = pl.ds(al(part(n) * rows, 16), rows)
        return rc(
            gat.at[gpair(n), r, pl.ds(col(2 * e + 1 - core, 0), NX * BLK)],
            gatp.at[gpair(n), r, pl.ds(e * NX * BLK, NX * BLK)],
            m_cs.at[e], m_cr.at[n % 4, e], c_dev,
        )

    def y_copy(p, q):
        k = pl.ds(q * dm.third, dm.third)
        return rc(y_s.at[k], y_r.at[p % 2, k], m_ys.at[q], m_yr.at[p % 2, q], y_dev)

    def own_copy(p, q, e):
        t, u = p // dm.subs, p % dm.subs
        k = pl.ds(q * dm.third, dm.third)
        return pltpu.make_async_copy(
            own.at[p % 2, k, pl.ds(e * BLK, BLK)],
            wg_hbm.at[t, k, pl.ds(al(e * dm.own + u * BLK), BLK)],
            m_own.at[p % 2, q, e],
        )

    def pg_copy(t, s):
        return pltpu.make_async_copy(pgb, pg_hbm.at[t, :, pl.ds(al(s * rows), rows)], m_pg)

    def sum_copy(k):
        to = lax.rem(bi + k, 4)
        return rc(sum_s.at[to], sum_r.at[k - 1], m_ss.at[k - 1], m_sr.at[k - 1], (wi, to))

    def factor(k, s):
        wide_hole = jnp.concatenate([hole[pl.ds(al(k * BLK), BLK)]] * (rows // BLK), axis=1)
        return 1.0 - small_img[:, pl.ds(al(s * rows), rows)] * wide_hole

    def prepare(t, s):
        @pl.loop(0, dm.feats // BLK)
        def _(k):
            at, lanes = pl.ds(al(k * BLK), BLK), pl.ds(s * rows, rows)
            masked = (xb[t, at, lanes].astype(F32) * factor(k, s)).astype(BF16)
            xb[t, at, lanes] = masked
            xt[t, pl.ds(s * rows, rows), at] = masked.T

    def prepare_cot(n):
        for i in (0, 1):
            cot_load(n, i).wait()
            cot[i, pl.ds(al(part(n) * rows), rows), pl.ds(al(sub(n) * BLK), BLK)] = craw[n % 2, i].T

    def forward(n, k):
        fwd[n % 2, :, pl.ds(k * 256, 256)] = jnp.dot(
            xt[tower(n), pl.ds(al(part(n) * rows, 16), rows), :],
            wb[(n // dm.parts) % 4, :, pl.ds(k * 256, 256)],
            preferred_element_type=F32,
        )

    def x1_send(n, q):
        o = (
            jnp.where(z < 2, 3, 0),
            jnp.where(z < 2, 2, 1),
            jnp.where(z < 2, 1 - z, 5 - z),
            z,
        )[q]

        @pl.when(n >= 1)
        def _():
            x1_copy(n, o).wait_send()

        for r, m in chunks(rx):
            x1_s[o, r : r + m] = fwd[n % 2, r : r + m, pl.ds(col(o, 1 - x), BLK)].astype(BF16)
        x1_copy(n, o).start()

    def xr_hop(n, h):
        for d in (0, 1):
            o = 3 - h + z if d == 0 else h - 3 + z

            @pl.when(far(d) <= h)
            def _():
                x1_copy(n, o).wait_recv()
                if h:
                    @pl.when(far(d) >= 1)
                    def _():
                        xr_copy(n, d, h - 1).wait_recv()

                @pl.when(n >= 1)
                def _():
                    xr_copy(n, d, h).wait_send()

                for r, m in chunks(rx):
                    v = fwd[n % 2, r : r + m, pl.ds(col(o, x), BLK)] + x1_r[n % 2, o, r : r + m].astype(F32)
                    if h:
                        v = v + xr_r[n % 2, d, h - 1, r : r + m].astype(F32)
                    xr_s[d, h, r : r + m] = v.astype(BF16)
                xr_copy(n, d, h).start()

    def zr_hop(n, h):
        for d in (0, 1):
            o = 3 - h + z if d == 0 else h - 3 + z

            @pl.when(far(d) <= h)
            def _():
                if h:
                    @pl.when(far(d) >= 1)
                    def _():
                        zr_copy(n, d, h - 1).wait_recv()

                @pl.when(n >= 1)
                def _():
                    zr_copy(n, d, h).wait_send()

                for r, m in chunks(rz):
                    v = fwd[n % 2, rx + r : rx + r + m, pl.ds(col(o, 0), NX * BLK)]
                    if h:
                        v = v + zr_r[n % 2, d, h - 1, r : r + m].astype(F32)
                    zr_s[d, h, r : r + m] = v.astype(BF16)
                zr_copy(n, d, h).start()

    def z_sum(n):
        for d in (0, 1):
            @pl.when(far(d) >= 1)
            def _():
                zr_copy(n, d, 2).wait_recv()

        @pl.when(n >= 1)
        def _():
            z2_copy(n).wait_send()

        for xx in (1 - x, x):
            for r, m in chunks(rz):
                lanes = pl.ds(al(xx * BLK), BLK)
                v = (
                    fwd[n % 2, rx + r : rx + r + m, pl.ds(col(z, xx), BLK)]
                    + zr_r[n % 2, 0, 2, r : r + m, lanes].astype(F32)
                    + zr_r[n % 2, 1, 2, r : r + m, lanes].astype(F32)
                )
                if xx is x:
                    zown[r : r + m] = v
                else:
                    z2_s[r : r + m] = v.astype(BF16)
            if xx is not x:
                z2_copy(n).start()

    def finish(n, row0, count, total):
        t, u = tower(n), sub(n)
        lanes = pl.ds(al(u * BLK), BLK)
        base = part(n) * rows + row0
        b_row = jnp.where(t == 0, bias[0:1, lanes], bias[1:2, lanes])
        from0 = jnp.where(t == 0, st[0, 0:1, lanes], st[0, 1:2, lanes])
        from1 = jnp.where(t == 0, st[1, 0:1, lanes], st[1, 1:2, lanes])
        for r, m in chunks(count):
            at = pl.ds(al(base + r, 16), m)
            v = total(r, m) + b_row
            sq = v * v
            th = jnp.tanh(ROOT * v * (1.0 + CUBE * sq))
            half = 0.5 * (1.0 + th)
            htmp[r : r + m] = v * half
            slope = half + 0.5 * v * (1.0 - th * th) * (ROOT * (1.0 + 3.0 * CUBE * sq))
            up0, up1 = cot[0, at, lanes].astype(F32), cot[1, at, lanes].astype(F32)
            grad = (from0 * up0 + from1 * up1) * slope
            sacc[u, t] += jnp.sum(grad.reshape(m // 8, 8, BLK), axis=0)
            gat[gpair(n), at, pl.ds(col(z, x), BLK)] = grad.astype(BF16)

    def mix(n, row0, count):
        t, u = tower(n), sub(n)
        lanes = pl.ds(al(u * BLK), BLK)
        base = part(n) * rows + row0

        @pl.when(t == 0)
        def _():
            for r, m in chunks(count):
                hid0[pl.ds(al(base + r, 16), m), lanes] = htmp[r : r + m]

        @pl.when(t == 1)
        def _():
            for r, m in chunks(count):
                at = pl.ds(al(base + r, 16), m)
                h = hid0[at, lanes], htmp[r : r + m]
                for i in (0, 1):
                    up = cot[i, at, lanes].astype(F32)
                    stmp[i, row0 + r : row0 + r + m] = (st[i, 0:1, lanes] * h[0] + st[i, 1:2, lanes] * h[1]).astype(BF16)
                    for j in (0, 1):
                        sacc[u, 2 + 2 * i + j] += jnp.sum((up * h[j]).reshape(m // 8, 8, BLK), axis=0)

    def emit(n):
        @pl.when(tower(n) == 1)
        def _():
            for i in (0, 1):
                @pl.when(n >= n_units // 2 + 2)
                def _():
                    s_copy(n, i).wait()

                sbuf[n % 2, i] = stmp[i].T
                s_copy(n, i).start()

    def z_final(n):
        z2_copy(n).wait_recv()
        finish(n, rx, rz, lambda r, m: zown[r : r + m] + z2_r[n % 2, r : r + m].astype(F32))

        @pl.when(n >= 1)
        def _():
            z4_copy(n).wait_send()

        z4_copy(n).start()
        mix(n, rx, rz)

    def x_final(n):
        x1_copy(n, z).wait_recv()
        for d in (0, 1):
            @pl.when(far(d) >= 1)
            def _():
                xr_copy(n, d, 2).wait_recv()

        def total(r, m):
            return (
                fwd[n % 2, r : r + m, pl.ds(col(z, x), BLK)]
                + x1_r[n % 2, z, r : r + m].astype(F32)
                + xr_r[n % 2, 0, 2, r : r + m].astype(F32)
                + xr_r[n % 2, 1, 2, r : r + m].astype(F32)
            )

        finish(n, 0, rx, total)
        for d in (0, 1):
            gather_hop(gx_copy, n, d, 0)
        x5_send(n, z)
        mix(n, 0, rx)

    def gather_hop(copy, n, d, h):
        @pl.when((far(d) >= h) & (far(d) <= 2))
        def _():
            @pl.when(n >= 1)
            def _():
                copy(n, d, h).wait_send()

            copy(n, d, h).start()

    def x5_send(n, o):
        @pl.when(n >= 1)
        def _():
            x5_copy(n, o, x).wait_send()

        x5_copy(n, o, x).start()

    def gather_arrive(copy, n, h, forward_x):
        for d in (0, 1):
            @pl.when(far(d) >= h + 1)
            def _():
                copy(n, d, h).wait_recv()
                if h < 2:
                    gather_hop(copy, n, d, h + 1)
                if forward_x:
                    x5_send(n, z - 1 - h if d == 0 else z + 1 + h)

    def gathered(n):
        for o in range(NZ):
            x5_copy(n, o, 1 - x).wait_recv()
        for e in (0, 1):
            @pl.when(n >= 1)
            def _():
                c_copy(n, e).wait_send()

            c_copy(n, e).start()

    def back_pooled(n):
        t, s = tower(n), part(n)
        lanes = pl.ds(al(s * rows), rows)

        @pl.loop(0, PIECES)
        def _(q):
            k = pl.ds(al(q * dm.third, 16), dm.third)
            acc[k, lanes] += lax.dot_general(
                wb[(n // dm.parts) % 4, k, :],
                gat[gpair(n), pl.ds(al(s * rows, 16), rows), :],
                NT,
                preferred_element_type=F32,
            )

        @pl.when(sub(n) == dm.subs - 1)
        def _():
            @pl.when((t > 0) | (s > 0))
            def _():
                pg_copy(t, s).wait()

            @pl.loop(0, dm.feats // BLK)
            def _(k):
                at = pl.ds(al(k * BLK), BLK)
                pgb[at] = (acc[at, lanes] * factor(k, s)).astype(BF16)
                acc[at, lanes] = jnp.zeros((BLK, rows), F32)

            pg_copy(t, s).start()

    def y_arrive(p, q):
        k = pl.ds(q * dm.third, dm.third)
        y_copy(p, q).wait_recv()
        for r, m in chunks(dm.third):
            at = pl.ds(q * dm.third + r, m)
            own[p % 2, at] += y_r[p % 2, at].astype(F32)
        for e in (0, 1):
            own_copy(p, q, e).start()

    def back_weight(p, q):
        if q == 0:
            for n in (2 * p, 2 * p + 1):
                for e in (0, 1):
                    c_copy(n, e).wait_recv()

            @pl.when(p % dm.subs == 0)
            def _():
                xp_copy(p // dm.subs).wait_recv()

        @pl.when(p >= 1)
        def _():
            y_arrive(p - 1, q)
            y_copy(p, q).wait_send()

        @pl.when(p >= 2)
        def _():
            for e in (0, 1):
                own_copy(p, q, e).wait()

        t, k = p // dm.subs, pl.ds(q * dm.third, dm.third)

        def grads(yy):
            lanes = pl.ds(col(2 * yy + core, 0), NX * BLK)
            return jnp.dot(xb[t, k, :], gat[p % 2, :, lanes], preferred_element_type=F32) + jnp.dot(
                xpb[t, k, :], gatp[p % 2, :, pl.ds(al(yy * NX * BLK), NX * BLK)], preferred_element_type=F32
            )

        y_s[k, :] = grads(1 - y).astype(BF16)
        y_copy(p, q).start()
        own[p % 2, k, :] = grads(y)

    def sums_send():
        for u in range(dm.subs):
            for j in range(6):
                sum_s[u, j : j + 1] = jnp.sum(sacc[u, j], axis=0, keepdims=True)
            sum_s[u, 6:8] = jnp.zeros((2, BLK), F32)
        for k in (1, 2, 3):
            sum_copy(k).start()

    x_load(0, 0).start()
    for w in range(NZ * NX):
        w_load(0, w).start()
    x_load(0, 1).start()
    for i in (0, 1):
        cot_load(0, i).start()
    for w in range(NZ * NX):
        w_load(1, w).start()
    for s in (0, 1):
        x_load(1, s).start()

    barrier = pltpu.get_barrier_semaphore()
    peers = [x_dev] + [(wi, lax.rem(bi + k, 4)) for k in (1, 2, 3)]
    for dev in peers:
        pl.semaphore_signal(barrier, inc=1, device_id=dev, device_id_type=MESH)
    for d in (0, 1):
        @pl.when(far(d) <= 2)
        def _():
            pl.semaphore_signal(barrier, inc=1, device_id=z_dev(d), device_id_type=MESH)

    small_img[...] = jnp.concatenate([group[j : j + 1] for j in range(dm.images // BLK)], axis=1).astype(F32)
    for j in range(dm.feats // BLK):
        gap = 1.0 - valid[j : j + 1].astype(F32)
        hole[j * BLK : (j + 1) * BLK] = jnp.broadcast_to(gap, (BLK, BLK)).T
    x_load(0, 0).wait()
    prepare(0, 0)

    @pl.loop(0, dm.feats // 8)
    def _(k):
        acc[pl.ds(al(k * 8, 8), 8)] = jnp.zeros((8, dm.images), F32)

    for d in (0, 1):
        @pl.when(far(d) == 0)
        def _():
            for s in (0, 1):
                for h in range(3):
                    xr_r[s, d, h] = jnp.zeros((rx, BLK), BF16)
                    zr_r[s, d, h] = jnp.zeros((rz, NX * BLK), BF16)

    pl.semaphore_wait(barrier, jnp.where((z == 0) | (z == NZ - 1), len(peers) + 1, len(peers) + 2))
    for w in range(NZ * NX):
        w_load(0, w).wait()
    for k in range(4):
        forward(0, k)
    sacc[...] = jnp.zeros_like(sacc)

    def tick(i, carry):
        a, b, c = i, i - 1, i - 2
        on_a = i < n_units
        on_b = (i >= 1) & (i <= n_units)
        on_c = (i >= 2) & (i <= n_units + 1)
        on_f = i + 1 < n_units
        p = lax.div(i - 4, 2)
        on_p = (i >= 4) & (i % 2 == 0)

        @pl.when(on_a)
        def _():
            x1_send(a, 0)
            zr_hop(a, 0)

        @pl.when((i % 2 == 0) & (i // 2 + 2 < dm.towers * dm.subs))
        def _():
            for w in range(NZ * NX):
                w_load(i // 2 + 2, w).start()

        @pl.when(on_b)
        def _():
            z_final(b)
            x_final(b)

        @pl.when(on_c)
        def _():
            gather_arrive(gz_copy, c, 0, False)

        @pl.when(on_f)
        def _():
            @pl.when(i % 2 == 1)
            def _():
                for w in range(NZ * NX):
                    w_load((i + 1) // 2, w).wait()

            @pl.when(i == 0)
            def _():
                x_load(0, 1).wait()
                prepare(0, 1)
                xp_copy(0).start()

            forward(i + 1, 0)

        @pl.when(on_p)
        def _():
            back_weight(p, 0)

        @pl.when(on_a)
        def _():
            x1_send(a, 1)
            zr_hop(a, 1)
            xr_hop(a, 0)

        @pl.when(on_c)
        def _():
            gather_arrive(gz_copy, c, 1, False)

        @pl.when(on_b)
        def _():
            gather_arrive(gx_copy, b, 0, True)
            emit(b)

        @pl.when(on_f)
        def _():
            forward(i + 1, 1)

        @pl.when(on_p)
        def _():
            back_weight(p, 1)

        @pl.when(on_a)
        def _():
            x1_send(a, 2)
            zr_hop(a, 2)
            xr_hop(a, 1)

        @pl.when(on_b)
        def _():
            gather_arrive(gx_copy, b, 1, True)

        @pl.when(on_c)
        def _():
            gather_arrive(gz_copy, c, 2, False)
            gathered(c)

        @pl.when(i < n_units // 2)
        def _():
            prepare_cot(i)

            @pl.when(i + 1 < n_units // 2)
            def _():
                for j in (0, 1):
                    cot_load(i + 1, j).start()

        @pl.when(on_f)
        def _():
            forward(i + 1, 2)

        @pl.when(on_p)
        def _():
            back_weight(p, 2)

        @pl.when(on_a)
        def _():
            x1_send(a, 3)
            z_sum(a)
            xr_hop(a, 2)

        @pl.when(on_b)
        def _():
            z4_copy(b).wait_recv()
            for d in (0, 1):
                gather_hop(gz_copy, b, d, 0)
            gather_arrive(gx_copy, b, 2, True)

        @pl.when(on_c)
        def _():
            back_pooled(c)

        @pl.when(on_f)
        def _():
            forward(i + 1, 3)

        for s in (0, 1):
            @pl.when(i == 4 + s)
            def _():
                x_load(1, s).wait()
                prepare(1, s)
                if s:
                    xp_copy(1).start()

        @pl.when(i == n_units)
        def _():
            sums_send()

        return carry

    lax.fori_loop(0, n_units + 3, tick, 0)

    last, pairs = n_units - 1, dm.towers * dm.subs
    for k in (1, 2, 3):
        sum_copy(k).wait_recv()
    total = sum_s[bi] + sum_r[0] + sum_r[1] + sum_r[2]
    out_b[...] = total[0:2]
    for i in (0, 1):
        out_sg[i] = total[2 + 2 * i : 4 + 2 * i]
        out_sn[i] = st[i, :, pl.ds(al(bi * BLK), BLK)] - step_ref[0] * total[2 + 2 * i : 4 + 2 * i]
    for q in range(PIECES):
        y_arrive(pairs - 1, q)
    for q in range(PIECES):
        for e in (0, 1):
            own_copy(pairs - 2, q, e).wait()
            own_copy(pairs - 1, q, e).wait()
        y_copy(pairs - 1, q).wait_send()
    pg_copy(1, 1).wait()
    for i in (0, 1):
        s_copy(last - 1, i).wait()
        s_copy(last, i).wait()
    for t in range(dm.towers):
        xp_copy(t).wait_send()
    for k in (1, 2, 3):
        sum_copy(k).wait_send()
    for e in (0, 1):
        c_copy(last, e).wait_send()
    for o in range(NZ):
        x1_copy(last, o).wait_send()
        x5_copy(last, o, x).wait_send()
    z2_copy(last).wait_send()
    z4_copy(last).wait_send()
    for d in (0, 1):
        for h in range(3):
            @pl.when(far(d) <= h)
            def _():
                xr_copy(last, d, h).wait_send()
                zr_copy(last, d, h).wait_send()

            @pl.when((far(d) >= h) & (far(d) <= 2))
            def _():
                gx_copy(last, d, h).wait_send()
                gz_copy(last, d, h).wait_send()


def carry_out(*refs):
    count = len(refs) // 2
    for src, dst in zip(refs[:count], refs[count:]):
        dst[...] = src[...]


def fused(pooled, weight, fc_bias, stitch, cotangent, valid_mask, image_group, step_rate):
    dm = Dims(pooled, weight, cotangent)
    towers, feats, images, own = dm.towers, dm.feats, dm.images, dm.own
    rows, rx, rz, cols = dm.rows, dm.rx, dm.rz, dm.cols
    dma = pltpu.SemaphoreType.DMA
    vm = pltpu.VMEM
    scratch = [
        vm((4, feats, cols), BF16),
        vm((towers, images, feats), BF16),
        vm((towers, feats, images), BF16),
        vm((towers, feats, images), BF16),
        vm((feats, BLK), F32),
        vm((1, images), F32),
        vm((2, 2, BLK, rows), BF16),
        vm((2, images, own), BF16),
        vm((2, rows, BLK), BF16),
        vm((2, 2, BLK, rows), BF16),
        vm((feats, images), F32),
        vm((2, rows, cols), F32),
        vm((2, images, cols), BF16),
        vm((2, images, cols // 2), BF16),
        vm((NZ, rx, BLK), BF16),
        vm((2, NZ, rx, BLK), BF16),
        vm((2, 3, rx, BLK), BF16),
        vm((2, 2, 3, rx, BLK), BF16),
        vm((2, 3, rz, NX * BLK), BF16),
        vm((2, 2, 3, rz, NX * BLK), BF16),
        vm((rz, BLK), F32),
        vm((rz, BLK), BF16),
        vm((2, rz, BLK), BF16),
        vm((2, feats, NX * BLK), F32),
        vm((feats, NX * BLK), BF16),
        vm((2, feats, NX * BLK), BF16),
        vm((images, own), F32),
        vm((max(rx, rz), BLK), F32),
        vm((feats, rows), BF16),
        vm((dm.subs, 6, 8, BLK), F32),
        vm((dm.subs, 8, BLK), F32),
        vm((3, 8, BLK), F32),
    ] + [
        dma(shape)
        for shape in (
            (4, NZ * NX), (2, 2), (NZ,), (2, NZ), (2, 3), (2, 2, 3), (2, 3), (2, 2, 3), (), (2,), (), (2,),
            (2, 3), (2, 2, 3), (2, 3), (2, 2, 3), (NZ,), (2, NZ), (2,), (4, 2), (PIECES,), (2, PIECES), (3,), (3,), (2,), (2,),
            (2, PIECES, 2), (), (2, 2), (2, 2),
        )
    ]
    anyspace = pl.BlockSpec(memory_space=pl.ANY)
    inside = pl.BlockSpec(memory_space=pltpu.VMEM)
    out_shape = [
        jax.ShapeDtypeStruct((2, own, images), BF16),
        jax.ShapeDtypeStruct((towers, feats, images), BF16),
        jax.ShapeDtypeStruct((towers, feats, images), F32),
        jax.ShapeDtypeStruct((2, BLK), F32),
        jax.ShapeDtypeStruct((2, 2, BLK), F32),
        jax.ShapeDtypeStruct((2, 2, BLK), F32),
    ]
    out_specs = [anyspace] * 3 + [inside] * 3
    results = pl.pallas_call(
        functools.partial(kernel, dm),
        name="stitch_fc6",
        out_shape=out_shape,
        in_specs=[pl.BlockSpec(memory_space=pltpu.SMEM)] + [anyspace] * 3 + [inside] * 4,
        out_specs=out_specs,
        scratch_shapes=scratch,
        compiler_params=pltpu.CompilerParams(collective_id=1, has_side_effects=True, vmem_limit_bytes=61 * 2**20),
        cost_estimate=pl.CostEstimate(
            flops=6 * towers * feats * images * dm.chans, bytes_accessed=60 * 2**20, transcendentals=towers * images * own
        ),
    )(
        step_rate, weight, pooled, cotangent, fc_bias, stitch,
        valid_mask.reshape(feats // BLK, BLK), image_group.reshape(images // BLK, BLK),
    )
    def block(shape):
        if len(shape.shape) == 3 and shape.shape[1] % (CUTS * 16) == 0:
            return pl.BlockSpec((shape.shape[0], shape.shape[1] // CUTS, shape.shape[2]), lambda c: (0, c, 0))
        return pl.BlockSpec(shape.shape, lambda c: (0,) * len(shape.shape))

    blocks = [block(shape) for shape in out_shape]
    return pl.pallas_call(
        carry_out,
        name="carry_out",
        grid=(CUTS,),
        out_shape=out_shape,
        in_specs=blocks,
        out_specs=blocks,
        compiler_params=pltpu.CompilerParams(vmem_limit_bytes=60 * 2**20),
    )(*results)


def gelu_local(values):
    return jax.nn.gelu(values, approximate=True)


def plain(pooled, weight, fc_bias, stitch, cotangent, valid_mask, image_group, step_rate):
    highest = lax.Precision.HIGHEST
    factor = 1.0 - image_group[None, :].astype(F32) * (1.0 - valid_mask[:, None].astype(F32))
    masked = pooled * factor.astype(BF16)[None]
    owned = weight.shape[2] // lax.axis_size("wide")
    summed = lax.psum_scatter(
        jnp.einsum("tkc,tkb->ctb", weight, masked, preferred_element_type=F32), "wide", scatter_dimension=0, tiled=True
    )
    pre_act = summed + jnp.transpose(fc_bias)[:, :, None]
    hidden, gelu_back = jax.vjp(gelu_local, pre_act)
    stitched = jnp.einsum("ijc,cjb->icb", stitch, hidden, precision=highest)
    upstream = cotangent.astype(F32)
    stitch_part = jnp.einsum("icb,cjb->ijc", upstream, hidden, precision=highest)
    hidden_grad = jnp.einsum("ijc,icb->cjb", stitch, upstream, precision=highest)
    pre_grad = gelu_back(hidden_grad)[0]
    bias_part = jnp.transpose(jnp.sum(pre_grad, axis=2))
    pre_low = pre_grad.astype(BF16)
    bias_grad = lax.psum_scatter(bias_part, "batch", scatter_dimension=1, tiled=True)
    stitch_grad = lax.psum_scatter(stitch_part, "batch", scatter_dimension=2, tiled=True)
    portion = lax.all_gather(pre_low, "wide", axis=0, tiled=True)
    input_sum = jnp.einsum("tkc,ctb->tkb", weight, portion, preferred_element_type=F32)
    block_grad = jnp.einsum("tkb,ctb->tkc", masked, portion, preferred_element_type=F32)
    pooled_grad = (input_sum * factor[None]).astype(BF16)
    weight_grad = lax.psum_scatter(block_grad, "batch", scatter_dimension=2, tiled=True)
    share = owned // lax.axis_size("batch")
    stitch_mine = lax.dynamic_slice_in_dim(stitch, lax.axis_index("batch") * share, share, 2)
    stitch_new = stitch_mine - step_rate[0] * stitch_grad
    return stitched.astype(BF16), pooled_grad, weight_grad, bias_grad, stitch_grad, stitch_new


def fits(mesh, pooled, weight, cotangent):
    return (
        (mesh.shape["wide"], mesh.shape["batch"]) == (NZ * NX, 4)
        and pooled.shape[0] == 2
        and cotangent.shape[1] == 4 * BLK
        and weight.shape[2] == NZ * NX * cotangent.shape[1]
        and pooled.shape[2] % 512 == 0
        and pooled.shape[1] % (16 * PIECES) == 0
        and pooled.shape[1] % BLK == 0
    )


def solution(mesh):
    def body(pooled, weight, fc_bias, stitch, cotangent, *rest):
        form = fused if fits(mesh, pooled, weight, cotangent) else plain
        return form(pooled, weight, fc_bias, stitch, cotangent, *rest)

    return jax.shard_map(
        body,
        mesh=mesh,
        in_specs=(
            P(None, "wide", "batch"),
            P(None, "wide", None),
            P(None, "wide"),
            P(None, None, "wide"),
            P(None, "wide", "batch"),
            P("wide"),
            P("batch"),
            P(),
        ),
        out_specs=(
            P(None, "wide", "batch"),
            P(None, "wide", "batch"),
            P(None, "wide", "batch"),
            P(None, ("wide", "batch")),
            P(None, None, ("wide", "batch")),
            P(None, None, ("wide", "batch")),
        ),
        check_vma=False,
    )
```

```python
import functools
import math

import jax
import jax.numpy as jnp
from jax import lax
from jax.experimental import pallas as pl
from jax.experimental.pallas import tpu as pltpu
from jax.sharding import PartitionSpec as P

MESH = pl.DeviceIdType.MESH
BLK = 128
NZ, NX = 4, 2
F32, BF16 = jnp.float32, jnp.bfloat16
NT = (((1,), (1,)), ((), ()))
ROOT = math.sqrt(2.0 / math.pi)
CUBE = 0.044715
PIECES = 3
CUTS = 4


class Dims:
    def __init__(self, pooled, weight, cotangent):
        self.towers, self.feats, self.images = pooled.shape
        self.chans = weight.shape[2]
        self.own = cotangent.shape[1]
        self.subs = self.own // BLK
        self.parts = 2
        self.rows = self.images // self.parts
        self.rx = (self.rows * 21 // 32) // 16 * 16
        self.rz = self.rows - self.rx
        self.units = self.towers * self.subs * self.parts
        self.cols = NZ * NX * BLK
        self.third = self.feats // PIECES


def chunks(count, size=64):
    return [(r, min(size, count - r)) for r in range(0, count, size)]


def kernel(
    dm,
    step_ref, w_hbm, p_hbm, c_hbm, bias, st, valid, group,
    s_hbm, pg_hbm, wg_hbm, out_b, out_sg, out_sn,
    wb, xt, xb, xpb, hole, small_img, craw, cot, stmp, sbuf, acc, fwd, gat, gatp,
    x1_s, x1_r, xr_s, xr_r, zr_s, zr_r, zown, z2_s, z2_r,
    own, y_s, y_r, hid0, htmp, pgb, sacc, sum_s, sum_r,
    m_w, m_ld, m_x1s, m_x1r, m_xrs, m_xrr, m_zrs, m_zrr, m_z2s, m_z2r, m_z4s, m_z4r,
    m_gxs, m_gxr, m_gzs, m_gzr, m_x5s, m_x5r, m_cs, m_cr, m_ys, m_yr, m_ss, m_sr, m_xps, m_xpr, m_own, m_pg,
    m_cot, m_out,
):
    n_units, rows, rx, rz = dm.units, dm.rows, dm.rx, dm.rz
    wi, bi = lax.axis_index("wide"), lax.axis_index("batch")
    z, x = wi // NX, wi % NX
    y, core = bi // 2, bi % 2
    x_dev = (z * NX + 1 - x, bi)
    c_dev = (wi, y * 2 + 1 - core)
    y_dev = (wi, (1 - y) * 2 + core)

    def z_dev(d):
        return (wi + NX, bi) if d == 0 else (wi - NX, bi)

    def far(d):
        return z if d == 0 else NZ - 1 - z

    def rc(src, dst, ss, rs, dev):
        return pltpu.make_async_remote_copy(src, dst, ss, rs, device_id=dev, device_id_type=MESH)

    def al(v, k=BLK):
        return pl.multiple_of(v, k)

    def tower(n):
        return n // (dm.subs * dm.parts)

    def sub(n):
        return (n // dm.parts) % dm.subs

    def part(n):
        return n % dm.parts

    def gpair(n):
        return (n // dm.parts) % 2

    def col(o, xx):
        return al((o * NX + xx) * BLK)

    def w_load(p, w):
        t, u = p // dm.subs, p % dm.subs
        return pltpu.make_async_copy(
            w_hbm.at[t, :, pl.ds(al(w * dm.own + u * BLK), BLK)], wb.at[p % 4, :, pl.ds(w * BLK, BLK)], m_w.at[p % 4, w]
        )

    def x_load(t, s):
        lanes = pl.ds(s * rows, rows)
        return pltpu.make_async_copy(p_hbm.at[t, :, lanes], xb.at[t, :, lanes], m_ld.at[t, s])

    def cot_load(n, i):
        return pltpu.make_async_copy(
            c_hbm.at[i, pl.ds(al(sub(n) * BLK), BLK), pl.ds(al(part(n) * rows), rows)], craw.at[n % 2, i], m_cot.at[n % 2, i]
        )

    def s_copy(n, i):
        return pltpu.make_async_copy(
            sbuf.at[n % 2, i], s_hbm.at[i, pl.ds(al(sub(n) * BLK), BLK), pl.ds(al(part(n) * rows), rows)], m_out.at[n % 2, i]
        )

    def xp_copy(t):
        return rc(xb.at[t], xpb.at[t], m_xps.at[t], m_xpr.at[t], c_dev)

    def x1_copy(n, o):
        return rc(x1_s.at[o], x1_r.at[n % 2, o], m_x1s.at[o], m_x1r.at[n % 2, o], x_dev)

    def xr_copy(n, d, h):
        return rc(xr_s.at[d, h], xr_r.at[n % 2, d, h], m_xrs.at[d, h], m_xrr.at[n % 2, d, h], z_dev(d))

    def zr_copy(n, d, h):
        return rc(zr_s.at[d, h], zr_r.at[n % 2, d, h], m_zrs.at[d, h], m_zrr.at[n % 2, d, h], z_dev(d))

    def z2_copy(n):
        return rc(z2_s, z2_r.at[n % 2], m_z2s, m_z2r.at[n % 2], x_dev)

    def g_x(n, o, xx):
        return gat.at[gpair(n), pl.ds(al(part(n) * rows, 16), rx), pl.ds(col(o, xx), BLK)]

    def g_z(n, o, xx, width):
        return gat.at[gpair(n), pl.ds(al(part(n) * rows + rx, 16), rz), pl.ds(col(o, xx), width)]

    def z4_copy(n):
        return rc(g_z(n, z, x, BLK), g_z(n, z, x, BLK), m_z4s, m_z4r.at[n % 2], x_dev)

    def gx_copy(n, d, h):
        o = z - h if d == 0 else z + h
        return rc(g_x(n, o, x), g_x(n, o, x), m_gxs.at[d, h], m_gxr.at[n % 2, d, h], z_dev(d))

    def gz_copy(n, d, h):
        o = z - h if d == 0 else z + h
        blk = g_z(n, o, 0, NX * BLK)
        return rc(blk, blk, m_gzs.at[d, h], m_gzr.at[n % 2, d, h], z_dev(d))

    def x5_copy(n, o, xx):
        return rc(g_x(n, o, xx), g_x(n, o, xx), m_x5s.at[o], m_x5r.at[n % 2, o], x_dev)

    def c_copy(n, e):
        r = pl.ds(al(part(n) * rows, 16), rows)
        return rc(
            gat.at[gpair(n), r, pl.ds(col(2 * e + 1 - core, 0), NX * BLK)],
            gatp.at[gpair(n), r, pl.ds(e * NX * BLK, NX * BLK)],
            m_cs.at[e], m_cr.at[n % 4, e], c_dev,
        )

    def y_copy(p, q):
        k = pl.ds(q * dm.third, dm.third)
        return rc(y_s.at[k], y_r.at[p % 2, k], m_ys.at[q], m_yr.at[p % 2, q], y_dev)

    def own_copy(p, q, e):
        t, u = p // dm.subs, p % dm.subs
        k = pl.ds(q * dm.third, dm.third)
        return pltpu.make_async_copy(
            own.at[p % 2, k, pl.ds(e * BLK, BLK)],
            wg_hbm.at[t, k, pl.ds(al(e * dm.own + u * BLK), BLK)],
            m_own.at[p % 2, q, e],
        )

    def pg_copy(t, s):
        return pltpu.make_async_copy(pgb, pg_hbm.at[t, :, pl.ds(al(s * rows), rows)], m_pg)

    def sum_copy(k):
        to = lax.rem(bi + k, 4)
        return rc(sum_s.at[to], sum_r.at[k - 1], m_ss.at[k - 1], m_sr.at[k - 1], (wi, to))

    def factor(k, s):
        wide_hole = jnp.concatenate([hole[pl.ds(al(k * BLK), BLK)]] * (rows // BLK), axis=1)
        return 1.0 - small_img[:, pl.ds(al(s * rows), rows)] * wide_hole

    def prepare(t, s):
        @pl.loop(0, dm.feats // BLK)
        def _(k):
            at, lanes = pl.ds(al(k * BLK), BLK), pl.ds(s * rows, rows)
            masked = (xb[t, at, lanes].astype(F32) * factor(k, s)).astype(BF16)
            xb[t, at, lanes] = masked
            xt[t, pl.ds(s * rows, rows), at] = masked.T

    def prepare_cot(n):
        for i in (0, 1):
            cot_load(n, i).wait()
            cot[i, pl.ds(al(part(n) * rows), rows), pl.ds(al(sub(n) * BLK), BLK)] = craw[n % 2, i].T

    def forward(n, k):
        fwd[n % 2, :, pl.ds(k * 256, 256)] = jnp.dot(
            xt[tower(n), pl.ds(al(part(n) * rows, 16), rows), :],
            wb[(n // dm.parts) % 4, :, pl.ds(k * 256, 256)],
            preferred_element_type=F32,
        )

    def x1_send(n, q):
        o = (
            jnp.where(z < 2, 3, 0),
            jnp.where(z < 2, 2, 1),
            jnp.where(z < 2, 1 - z, 5 - z),
            z,
        )[q]

        @pl.when(n >= 1)
        def _():
            x1_copy(n, o).wait_send()

        for r, m in chunks(rx):
            x1_s[o, r : r + m] = fwd[n % 2, r : r + m, pl.ds(col(o, 1 - x), BLK)].astype(BF16)
        x1_copy(n, o).start()

    def xr_hop(n, h):
        for d in (0, 1):
            o = 3 - h + z if d == 0 else h - 3 + z

            @pl.when(far(d) <= h)
            def _():
                x1_copy(n, o).wait_recv()
                if h:
                    @pl.when(far(d) >= 1)
                    def _():
                        xr_copy(n, d, h - 1).wait_recv()

                @pl.when(n >= 1)
                def _():
                    xr_copy(n, d, h).wait_send()

                for r, m in chunks(rx):
                    v = fwd[n % 2, r : r + m, pl.ds(col(o, x), BLK)] + x1_r[n % 2, o, r : r + m].astype(F32)
                    if h:
                        v = v + xr_r[n % 2, d, h - 1, r : r + m].astype(F32)
                    xr_s[d, h, r : r + m] = v.astype(BF16)
                xr_copy(n, d, h).start()

    def zr_hop(n, h):
        for d in (0, 1):
            o = 3 - h + z if d == 0 else h - 3 + z

            @pl.when(far(d) <= h)
            def _():
                if h:
                    @pl.when(far(d) >= 1)
                    def _():
                        zr_copy(n, d, h - 1).wait_recv()

                @pl.when(n >= 1)
                def _():
                    zr_copy(n, d, h).wait_send()

                for r, m in chunks(rz):
                    v = fwd[n % 2, rx + r : rx + r + m, pl.ds(col(o, 0), NX * BLK)]
                    if h:
                        v = v + zr_r[n % 2, d, h - 1, r : r + m].astype(F32)
                    zr_s[d, h, r : r + m] = v.astype(BF16)
                zr_copy(n, d, h).start()

    def z_sum(n):
        for d in (0, 1):
            @pl.when(far(d) >= 1)
            def _():
                zr_copy(n, d, 2).wait_recv()

        @pl.when(n >= 1)
        def _():
            z2_copy(n).wait_send()

        for xx in (1 - x, x):
            for r, m in chunks(rz):
                lanes = pl.ds(al(xx * BLK), BLK)
                v = (
                    fwd[n % 2, rx + r : rx + r + m, pl.ds(col(z, xx), BLK)]
                    + zr_r[n % 2, 0, 2, r : r + m, lanes].astype(F32)
                    + zr_r[n % 2, 1, 2, r : r + m, lanes].astype(F32)
                )
                if xx is x:
                    zown[r : r + m] = v
                else:
                    z2_s[r : r + m] = v.astype(BF16)
            if xx is not x:
                z2_copy(n).start()

    def finish(n, row0, count, total):
        t, u = tower(n), sub(n)
        lanes = pl.ds(al(u * BLK), BLK)
        base = part(n) * rows + row0
        b_row = jnp.where(t == 0, bias[0:1, lanes], bias[1:2, lanes])
        from0 = jnp.where(t == 0, st[0, 0:1, lanes], st[0, 1:2, lanes])
        from1 = jnp.where(t == 0, st[1, 0:1, lanes], st[1, 1:2, lanes])
        for r, m in chunks(count):
            at = pl.ds(al(base + r, 16), m)
            v = total(r, m) + b_row
            sq = v * v
            th = jnp.tanh(ROOT * v * (1.0 + CUBE * sq))
            half = 0.5 * (1.0 + th)
            htmp[r : r + m] = v * half
            slope = half + 0.5 * v * (1.0 - th * th) * (ROOT * (1.0 + 3.0 * CUBE * sq))
            up0, up1 = cot[0, at, lanes].astype(F32), cot[1, at, lanes].astype(F32)
            grad = (from0 * up0 + from1 * up1) * slope
            sacc[u, t] += jnp.sum(grad.reshape(m // 8, 8, BLK), axis=0)
            gat[gpair(n), at, pl.ds(col(z, x), BLK)] = grad.astype(BF16)

    def mix(n, row0, count):
        t, u = tower(n), sub(n)
        lanes = pl.ds(al(u * BLK), BLK)
        base = part(n) * rows + row0

        @pl.when(t == 0)
        def _():
            for r, m in chunks(count):
                hid0[pl.ds(al(base + r, 16), m), lanes] = htmp[r : r + m]

        @pl.when(t == 1)
        def _():
            for r, m in chunks(count):
                at = pl.ds(al(base + r, 16), m)
                h = hid0[at, lanes], htmp[r : r + m]
                for i in (0, 1):
                    up = cot[i, at, lanes].astype(F32)
                    stmp[i, row0 + r : row0 + r + m] = (st[i, 0:1, lanes] * h[0] + st[i, 1:2, lanes] * h[1]).astype(BF16)
                    for j in (0, 1):
                        sacc[u, 2 + 2 * i + j] += jnp.sum((up * h[j]).reshape(m // 8, 8, BLK), axis=0)

    def emit(n):
        @pl.when(tower(n) == 1)
        def _():
            for i in (0, 1):
                @pl.when(n >= n_units // 2 + 2)
                def _():
                    s_copy(n, i).wait()

                sbuf[n % 2, i] = stmp[i].T
                s_copy(n, i).start()

    def z_final(n):
        z2_copy(n).wait_recv()
        finish(n, rx, rz, lambda r, m: zown[r : r + m] + z2_r[n % 2, r : r + m].astype(F32))

        @pl.when(n >= 1)
        def _():
            z4_copy(n).wait_send()

        z4_copy(n).start()
        mix(n, rx, rz)

    def x_final(n):
        x1_copy(n, z).wait_recv()
        for d in (0, 1):
            @pl.when(far(d) >= 1)
            def _():
                xr_copy(n, d, 2).wait_recv()

        def total(r, m):
            return (
                fwd[n % 2, r : r + m, pl.ds(col(z, x), BLK)]
                + x1_r[n % 2, z, r : r + m].astype(F32)
                + xr_r[n % 2, 0, 2, r : r + m].astype(F32)
                + xr_r[n % 2, 1, 2, r : r + m].astype(F32)
            )

        finish(n, 0, rx, total)
        for d in (0, 1):
            gather_hop(gx_copy, n, d, 0)
        x5_send(n, z)
        mix(n, 0, rx)

    def gather_hop(copy, n, d, h):
        @pl.when((far(d) >= h) & (far(d) <= 2))
        def _():
            @pl.when(n >= 1)
            def _():
                copy(n, d, h).wait_send()

            copy(n, d, h).start()

    def x5_send(n, o):
        @pl.when(n >= 1)
        def _():
            x5_copy(n, o, x).wait_send()

        x5_copy(n, o, x).start()

    def gather_arrive(copy, n, h, forward_x):
        for d in (0, 1):
            @pl.when(far(d) >= h + 1)
            def _():
                copy(n, d, h).wait_recv()
                if h < 2:
                    gather_hop(copy, n, d, h + 1)
                if forward_x:
                    x5_send(n, z - 1 - h if d == 0 else z + 1 + h)

    def gathered(n):
        for o in range(NZ):
            x5_copy(n, o, 1 - x).wait_recv()
        for e in (0, 1):
            @pl.when(n >= 1)
            def _():
                c_copy(n, e).wait_send()

            c_copy(n, e).start()

    def back_pooled(n):
        t, s = tower(n), part(n)
        lanes = pl.ds(al(s * rows), rows)

        @pl.loop(0, PIECES)
        def _(q):
            k = pl.ds(al(q * dm.third, 16), dm.third)
            acc[k, lanes] += lax.dot_general(
                wb[(n // dm.parts) % 4, k, :],
                gat[gpair(n), pl.ds(al(s * rows, 16), rows), :],
                NT,
                preferred_element_type=F32,
            )

        @pl.when(sub(n) == dm.subs - 1)
        def _():
            @pl.when((t > 0) | (s > 0))
            def _():
                pg_copy(t, s).wait()

            @pl.loop(0, dm.feats // BLK)
            def _(k):
                at = pl.ds(al(k * BLK), BLK)
                pgb[at] = (acc[at, lanes] * factor(k, s)).astype(BF16)
                acc[at, lanes] = jnp.zeros((BLK, rows), F32)

            pg_copy(t, s).start()

    def y_arrive(p, q):
        k = pl.ds(q * dm.third, dm.third)
        y_copy(p, q).wait_recv()
        for r, m in chunks(dm.third):
            at = pl.ds(q * dm.third + r, m)
            own[p % 2, at] += y_r[p % 2, at].astype(F32)
        for e in (0, 1):
            own_copy(p, q, e).start()

    def back_weight(p, q):
        if q == 0:
            for n in (2 * p, 2 * p + 1):
                for e in (0, 1):
                    c_copy(n, e).wait_recv()

            @pl.when(p % dm.subs == 0)
            def _():
                xp_copy(p // dm.subs).wait_recv()

        @pl.when(p >= 1)
        def _():
            y_arrive(p - 1, q)
            y_copy(p, q).wait_send()

        @pl.when(p >= 2)
        def _():
            for e in (0, 1):
                own_copy(p, q, e).wait()

        t, k = p // dm.subs, pl.ds(q * dm.third, dm.third)

        def grads(yy):
            lanes = pl.ds(col(2 * yy + core, 0), NX * BLK)
            return jnp.dot(xb[t, k, :], gat[p % 2, :, lanes], preferred_element_type=F32) + jnp.dot(
                xpb[t, k, :], gatp[p % 2, :, pl.ds(al(yy * NX * BLK), NX * BLK)], preferred_element_type=F32
            )

        y_s[k, :] = grads(1 - y).astype(BF16)
        y_copy(p, q).start()
        own[p % 2, k, :] = grads(y)

    def sums_send():
        for u in range(dm.subs):
            for j in range(6):
                sum_s[u, j : j + 1] = jnp.sum(sacc[u, j], axis=0, keepdims=True)
            sum_s[u, 6:8] = jnp.zeros((2, BLK), F32)
        for k in (1, 2, 3):
            sum_copy(k).start()

    x_load(0, 0).start()
    for w in range(NZ * NX):
        w_load(0, w).start()
    x_load(0, 1).start()
    for i in (0, 1):
        cot_load(0, i).start()
    for w in range(NZ * NX):
        w_load(1, w).start()
    for s in (0, 1):
        x_load(1, s).start()

    barrier = pltpu.get_barrier_semaphore()
    peers = [x_dev] + [(wi, lax.rem(bi + k, 4)) for k in (1, 2, 3)]
    for dev in peers:
        pl.semaphore_signal(barrier, inc=1, device_id=dev, device_id_type=MESH)
    for d in (0, 1):
        @pl.when(far(d) <= 2)
        def _():
            pl.semaphore_signal(barrier, inc=1, device_id=z_dev(d), device_id_type=MESH)

    small_img[...] = jnp.concatenate([group[j : j + 1] for j in range(dm.images // BLK)], axis=1).astype(F32)
    for j in range(dm.feats // BLK):
        gap = 1.0 - valid[j : j + 1].astype(F32)
        hole[j * BLK : (j + 1) * BLK] = jnp.broadcast_to(gap, (BLK, BLK)).T
    x_load(0, 0).wait()
    prepare(0, 0)

    @pl.loop(0, dm.feats // 8)
    def _(k):
        acc[pl.ds(al(k * 8, 8), 8)] = jnp.zeros((8, dm.images), F32)

    for d in (0, 1):
        @pl.when(far(d) == 0)
        def _():
            for s in (0, 1):
                for h in range(3):
                    xr_r[s, d, h] = jnp.zeros((rx, BLK), BF16)
                    zr_r[s, d, h] = jnp.zeros((rz, NX * BLK), BF16)

    pl.semaphore_wait(barrier, jnp.where((z == 0) | (z == NZ - 1), len(peers) + 1, len(peers) + 2))
    for w in range(NZ * NX):
        w_load(0, w).wait()
    for k in range(4):
        forward(0, k)
    sacc[...] = jnp.zeros_like(sacc)

    def tick(i, carry):
        a, b, c = i, i - 1, i - 2
        on_a = i < n_units
        on_b = (i >= 1) & (i <= n_units)
        on_c = (i >= 2) & (i <= n_units + 1)
        on_f = i + 1 < n_units
        p = lax.div(i - 4, 2)
        on_p = (i >= 4) & (i % 2 == 0)

        @pl.when(on_a)
        def _():
            zr_hop(a, 0)

        @pl.when((i % 2 == 0) & (i // 2 + 2 < dm.towers * dm.subs))
        def _():
            for w in range(NZ * NX):
                w_load(i // 2 + 2, w).start()

        @pl.when(on_b)
        def _():
            z_final(b)

        @pl.when(on_c)
        def _():
            gather_arrive(gz_copy, c, 0, False)

        @pl.when(on_p)
        def _():
            back_weight(p, 0)

        @pl.when(on_a)
        def _():
            x1_send(a, 0)

        @pl.when(on_b)
        def _():
            x_final(b)

        @pl.when(on_f)
        def _():
            @pl.when(i % 2 == 1)
            def _():
                for w in range(NZ * NX):
                    w_load((i + 1) // 2, w).wait()

            @pl.when(i == 0)
            def _():
                x_load(0, 1).wait()
                prepare(0, 1)
                xp_copy(0).start()

            forward(i + 1, 0)

        @pl.when(on_a)
        def _():
            zr_hop(a, 1)

        @pl.when(on_c)
        def _():
            gather_arrive(gz_copy, c, 1, False)

        @pl.when(on_f)
        def _():
            forward(i + 1, 1)

        @pl.when(on_b)
        def _():
            emit(b)

        @pl.when(on_a)
        def _():
            x1_send(a, 1)
            xr_hop(a, 0)

        @pl.when(on_b)
        def _():
            gather_arrive(gx_copy, b, 0, True)

        @pl.when(on_p)
        def _():
            back_weight(p, 1)

        @pl.when(on_a)
        def _():
            zr_hop(a, 2)

        @pl.when(on_c)
        def _():
            gather_arrive(gz_copy, c, 2, False)

        @pl.when(on_f)
        def _():
            forward(i + 1, 2)

        @pl.when(on_a)
        def _():
            x1_send(a, 2)
            xr_hop(a, 1)

        @pl.when(on_b)
        def _():
            gather_arrive(gx_copy, b, 1, True)

        @pl.when(on_c)
        def _():
            gathered(c)

        @pl.when(i < n_units // 2)
        def _():
            prepare_cot(i)

            @pl.when(i + 1 < n_units // 2)
            def _():
                for j in (0, 1):
                    cot_load(i + 1, j).start()

        @pl.when(on_p)
        def _():
            back_weight(p, 2)

        @pl.when(on_a)
        def _():
            z_sum(a)

        @pl.when(on_b)
        def _():
            z4_copy(b).wait_recv()
            for d in (0, 1):
                gather_hop(gz_copy, b, d, 0)

        @pl.when(on_f)
        def _():
            forward(i + 1, 3)

        @pl.when(on_a)
        def _():
            x1_send(a, 3)
            xr_hop(a, 2)

        @pl.when(on_b)
        def _():
            gather_arrive(gx_copy, b, 2, True)

        @pl.when(on_c)
        def _():
            back_pooled(c)

        for s in (0, 1):
            @pl.when(i == 4 + s)
            def _():
                x_load(1, s).wait()
                prepare(1, s)
                if s:
                    xp_copy(1).start()

        @pl.when(i == n_units)
        def _():
            sums_send()

        return carry

    lax.fori_loop(0, n_units + 3, tick, 0)

    last, pairs = n_units - 1, dm.towers * dm.subs
    for k in (1, 2, 3):
        sum_copy(k).wait_recv()
    total = sum_s[bi] + sum_r[0] + sum_r[1] + sum_r[2]
    out_b[...] = total[0:2]
    for i in (0, 1):
        out_sg[i] = total[2 + 2 * i : 4 + 2 * i]
        out_sn[i] = st[i, :, pl.ds(al(bi * BLK), BLK)] - step_ref[0] * total[2 + 2 * i : 4 + 2 * i]
    for q in range(PIECES):
        y_arrive(pairs - 1, q)
    for q in range(PIECES):
        for e in (0, 1):
            own_copy(pairs - 2, q, e).wait()
            own_copy(pairs - 1, q, e).wait()
        y_copy(pairs - 1, q).wait_send()
    pg_copy(1, 1).wait()
    for i in (0, 1):
        s_copy(last - 1, i).wait()
        s_copy(last, i).wait()
    for t in range(dm.towers):
        xp_copy(t).wait_send()
    for k in (1, 2, 3):
        sum_copy(k).wait_send()
    for e in (0, 1):
        c_copy(last, e).wait_send()
    for o in range(NZ):
        x1_copy(last, o).wait_send()
        x5_copy(last, o, x).wait_send()
    z2_copy(last).wait_send()
    z4_copy(last).wait_send()
    for d in (0, 1):
        for h in range(3):
            @pl.when(far(d) <= h)
            def _():
                xr_copy(last, d, h).wait_send()
                zr_copy(last, d, h).wait_send()

            @pl.when((far(d) >= h) & (far(d) <= 2))
            def _():
                gx_copy(last, d, h).wait_send()
                gz_copy(last, d, h).wait_send()


def carry_out(*refs):
    count = len(refs) // 2
    for src, dst in zip(refs[:count], refs[count:]):
        dst[...] = src[...]


def fused(pooled, weight, fc_bias, stitch, cotangent, valid_mask, image_group, step_rate):
    dm = Dims(pooled, weight, cotangent)
    towers, feats, images, own = dm.towers, dm.feats, dm.images, dm.own
    rows, rx, rz, cols = dm.rows, dm.rx, dm.rz, dm.cols
    dma = pltpu.SemaphoreType.DMA
    vm = pltpu.VMEM
    scratch = [
        vm((4, feats, cols), BF16),
        vm((towers, images, feats), BF16),
        vm((towers, feats, images), BF16),
        vm((towers, feats, images), BF16),
        vm((feats, BLK), F32),
        vm((1, images), F32),
        vm((2, 2, BLK, rows), BF16),
        vm((2, images, own), BF16),
        vm((2, rows, BLK), BF16),
        vm((2, 2, BLK, rows), BF16),
        vm((feats, images), F32),
        vm((2, rows, cols), F32),
        vm((2, images, cols), BF16),
        vm((2, images, cols // 2), BF16),
        vm((NZ, rx, BLK), BF16),
        vm((2, NZ, rx, BLK), BF16),
        vm((2, 3, rx, BLK), BF16),
        vm((2, 2, 3, rx, BLK), BF16),
        vm((2, 3, rz, NX * BLK), BF16),
        vm((2, 2, 3, rz, NX * BLK), BF16),
        vm((rz, BLK), F32),
        vm((rz, BLK), BF16),
        vm((2, rz, BLK), BF16),
        vm((2, feats, NX * BLK), F32),
        vm((feats, NX * BLK), BF16),
        vm((2, feats, NX * BLK), BF16),
        vm((images, own), F32),
        vm((max(rx, rz), BLK), F32),
        vm((feats, rows), BF16),
        vm((dm.subs, 6, 8, BLK), F32),
        vm((dm.subs, 8, BLK), F32),
        vm((3, 8, BLK), F32),
    ] + [
        dma(shape)
        for shape in (
            (4, NZ * NX), (2, 2), (NZ,), (2, NZ), (2, 3), (2, 2, 3), (2, 3), (2, 2, 3), (), (2,), (), (2,),
            (2, 3), (2, 2, 3), (2, 3), (2, 2, 3), (NZ,), (2, NZ), (2,), (4, 2), (PIECES,), (2, PIECES), (3,), (3,), (2,), (2,),
            (2, PIECES, 2), (), (2, 2), (2, 2),
        )
    ]
    anyspace = pl.BlockSpec(memory_space=pl.ANY)
    inside = pl.BlockSpec(memory_space=pltpu.VMEM)
    out_shape = [
        jax.ShapeDtypeStruct((2, own, images), BF16),
        jax.ShapeDtypeStruct((towers, feats, images), BF16),
        jax.ShapeDtypeStruct((towers, feats, images), F32),
        jax.ShapeDtypeStruct((2, BLK), F32),
        jax.ShapeDtypeStruct((2, 2, BLK), F32),
        jax.ShapeDtypeStruct((2, 2, BLK), F32),
    ]
    out_specs = [anyspace] * 3 + [inside] * 3
    results = pl.pallas_call(
        functools.partial(kernel, dm),
        name="stitch_fc6",
        out_shape=out_shape,
        in_specs=[pl.BlockSpec(memory_space=pltpu.SMEM)] + [anyspace] * 3 + [inside] * 4,
        out_specs=out_specs,
        scratch_shapes=scratch,
        compiler_params=pltpu.CompilerParams(collective_id=1, has_side_effects=True, vmem_limit_bytes=61 * 2**20),
        cost_estimate=pl.CostEstimate(
            flops=6 * towers * feats * images * dm.chans, bytes_accessed=60 * 2**20, transcendentals=towers * images * own
        ),
    )(
        step_rate, weight, pooled, cotangent, fc_bias, stitch,
        valid_mask.reshape(feats // BLK, BLK), image_group.reshape(images // BLK, BLK),
    )
    def block(shape):
        if len(shape.shape) == 3 and shape.shape[1] % (CUTS * 16) == 0:
            return pl.BlockSpec((shape.shape[0], shape.shape[1] // CUTS, shape.shape[2]), lambda c: (0, c, 0))
        return pl.BlockSpec(shape.shape, lambda c: (0,) * len(shape.shape))

    blocks = [block(shape) for shape in out_shape]
    return pl.pallas_call(
        carry_out,
        name="carry_out",
        grid=(CUTS,),
        out_shape=out_shape,
        in_specs=blocks,
        out_specs=blocks,
        compiler_params=pltpu.CompilerParams(vmem_limit_bytes=60 * 2**20),
    )(*results)


def gelu_local(values):
    return jax.nn.gelu(values, approximate=True)


def plain(pooled, weight, fc_bias, stitch, cotangent, valid_mask, image_group, step_rate):
    highest = lax.Precision.HIGHEST
    factor = 1.0 - image_group[None, :].astype(F32) * (1.0 - valid_mask[:, None].astype(F32))
    masked = pooled * factor.astype(BF16)[None]
    owned = weight.shape[2] // lax.axis_size("wide")
    summed = lax.psum_scatter(
        jnp.einsum("tkc,tkb->ctb", weight, masked, preferred_element_type=F32), "wide", scatter_dimension=0, tiled=True
    )
    pre_act = summed + jnp.transpose(fc_bias)[:, :, None]
    hidden, gelu_back = jax.vjp(gelu_local, pre_act)
    stitched = jnp.einsum("ijc,cjb->icb", stitch, hidden, precision=highest)
    upstream = cotangent.astype(F32)
    stitch_part = jnp.einsum("icb,cjb->ijc", upstream, hidden, precision=highest)
    hidden_grad = jnp.einsum("ijc,icb->cjb", stitch, upstream, precision=highest)
    pre_grad = gelu_back(hidden_grad)[0]
    bias_part = jnp.transpose(jnp.sum(pre_grad, axis=2))
    pre_low = pre_grad.astype(BF16)
    bias_grad = lax.psum_scatter(bias_part, "batch", scatter_dimension=1, tiled=True)
    stitch_grad = lax.psum_scatter(stitch_part, "batch", scatter_dimension=2, tiled=True)
    portion = lax.all_gather(pre_low, "wide", axis=0, tiled=True)
    input_sum = jnp.einsum("tkc,ctb->tkb", weight, portion, preferred_element_type=F32)
    block_grad = jnp.einsum("tkb,ctb->tkc", masked, portion, preferred_element_type=F32)
    pooled_grad = (input_sum * factor[None]).astype(BF16)
    weight_grad = lax.psum_scatter(block_grad, "batch", scatter_dimension=2, tiled=True)
    share = owned // lax.axis_size("batch")
    stitch_mine = lax.dynamic_slice_in_dim(stitch, lax.axis_index("batch") * share, share, 2)
    stitch_new = stitch_mine - step_rate[0] * stitch_grad
    return stitched.astype(BF16), pooled_grad, weight_grad, bias_grad, stitch_grad, stitch_new


def fits(mesh, pooled, weight, cotangent):
    return (
        (mesh.shape["wide"], mesh.shape["batch"]) == (NZ * NX, 4)
        and pooled.shape[0] == 2
        and cotangent.shape[1] == 4 * BLK
        and weight.shape[2] == NZ * NX * cotangent.shape[1]
        and pooled.shape[2] % 512 == 0
        and pooled.shape[1] % (16 * PIECES) == 0
        and pooled.shape[1] % BLK == 0
    )


def solution(mesh):
    def body(pooled, weight, fc_bias, stitch, cotangent, *rest):
        form = fused if fits(mesh, pooled, weight, cotangent) else plain
        return form(pooled, weight, fc_bias, stitch, cotangent, *rest)

    return jax.shard_map(
        body,
        mesh=mesh,
        in_specs=(
            P(None, "wide", "batch"),
            P(None, "wide", None),
            P(None, "wide"),
            P(None, None, "wide"),
            P(None, "wide", "batch"),
            P("wide"),
            P("batch"),
            P(),
        ),
        out_specs=(
            P(None, "wide", "batch"),
            P(None, "wide", "batch"),
            P(None, "wide", "batch"),
            P(None, ("wide", "batch")),
            P(None, None, ("wide", "batch")),
            P(None, None, ("wide", "batch")),
        ),
        check_vma=False,
    )
```

```python
import functools
import math

import jax
import jax.numpy as jnp
from jax import lax
from jax.experimental import pallas as pl
from jax.experimental.pallas import tpu as pltpu
from jax.sharding import PartitionSpec as P

MESH = pl.DeviceIdType.MESH
BLK = 128
NZ, NX = 4, 2
F32, BF16 = jnp.float32, jnp.bfloat16
NT = (((1,), (1,)), ((), ()))
ROOT = math.sqrt(2.0 / math.pi)
CUBE = 0.044715
PIECES = 3
CUTS = 4
DRAIN = (
    "zf0", "xf0", "zf1", "xf1", "hz00", "hz01", "bv0", "gs0", "gx00", "gs1", "gx01", "hz10", "hz11", "bv1", "em",
    "gz00", "gx10", "gz01", "gx11", "hz20", "hz21", "hd", "bv2", "gz10", "gx20", "gz11", "gx21", "hp0", "hp1", "hp2",
    "ss", "bw0", "bw1", "bw2", "gz20", "gz21", "gd", "bp0", "bp1", "bp2", "bx0", "bx1", "bx2",
)
ORDER = (
    "zr00", "ws", "zf0", "gz00", "bw0", "x10", "xf0", "ww", "p0", "zr01", "zf1", "gz01", "xf1", "f0",
    "zr10", "gz10", "f1", "x11", "xr00", "gx00", "zr11", "gz11", "bw1", "xr01", "gx01", "em",
    "zr20", "gz20", "f2", "x12", "xr10", "gx10", "ct", "zr21", "gz21", "bw2", "xr11", "gx11", "gd",
    "zs0", "gs0", "f3", "x13", "xr20", "gx20", "bp0", "zs1", "gs1", "bp1", "xr21", "gx21", "bp2",
)


class Dims:
    def __init__(self, pooled, weight, cotangent):
        self.towers, self.feats, self.images = pooled.shape
        self.chans = weight.shape[2]
        self.own = cotangent.shape[1]
        self.subs = self.own // BLK
        self.parts = 2
        self.rows = self.images // self.parts
        self.rx = (self.rows * 19 // 32) // 16 * 16
        self.rz = self.rows - self.rx
        self.units = self.towers * self.subs * self.parts
        self.cols = NZ * NX * BLK
        self.third = self.feats // PIECES


def chunks(count, size=64):
    return [(r, min(size, count - r)) for r in range(0, count, size)]


def kernel(
    dm,
    step_ref, w_hbm, p_hbm, c_hbm, bias, st, valid, group,
    s_hbm, pg_hbm, wg_hbm, out_b, out_sg, out_sn,
    wb, xt, xb, xpb, hole, small_img, craw, cot, stmp, sbuf, acc, fwd, gat, gatp,
    x1_s, x1_r, xr_s, xr_r, zr_s, zr_r, zown, z2_s, z2_r,
    own, tacc, y_s, y_r, hid0, htmp, pgb, sacc, sum_s, sum_r,
    m_w, m_ld, m_x1s, m_x1r, m_xrs, m_xrr, m_zrs, m_zrr, m_z2s, m_z2r, m_z4s, m_z4r,
    m_gxs, m_gxr, m_gzs, m_gzr, m_x5s, m_x5r, m_cs, m_cr, m_ys, m_yr, m_ss, m_sr, m_xps, m_xpr, m_own, m_pg,
    m_cot, m_out,
):
    n_units, rows, rx, rz = dm.units, dm.rows, dm.rx, dm.rz
    mid_x, mid_z = rx // 32 * 16, rz // 32 * 16
    cuts_x = (0, mid_x), (mid_x, rx - mid_x)
    cuts_z = (0, mid_z), (mid_z, rz - mid_z)
    wi, bi = lax.axis_index("wide"), lax.axis_index("batch")
    z, x = wi // NX, wi % NX
    y, core = bi // 2, bi % 2
    x_dev = (z * NX + 1 - x, bi)
    c_dev = (wi, y * 2 + 1 - core)
    y_dev = (wi, (1 - y) * 2 + core)

    def z_dev(d):
        return (wi + NX, bi) if d == 0 else (wi - NX, bi)

    def far(d):
        return z if d == 0 else NZ - 1 - z

    def rc(src, dst, ss, rs, dev):
        return pltpu.make_async_remote_copy(src, dst, ss, rs, device_id=dev, device_id_type=MESH)

    def al(v, k=BLK):
        return v if isinstance(v, int) else pl.multiple_of(v, k)

    def tower(n):
        return n // (dm.subs * dm.parts)

    def sub(n):
        return (n // dm.parts) % dm.subs

    def part(n):
        return n % dm.parts

    def gpair(n):
        return (n // dm.parts) % 2

    def col(o, xx):
        return al((o * NX + xx) * BLK)

    def w_load(p, w):
        t, u = p // dm.subs, p % dm.subs
        return pltpu.make_async_copy(
            w_hbm.at[t, :, pl.ds(al(w * dm.own + u * BLK), BLK)], wb.at[p % 4, :, pl.ds(w * BLK, BLK)], m_w.at[p % 4, w]
        )

    def x_load(t, s):
        lanes = pl.ds(s * rows, rows)
        return pltpu.make_async_copy(p_hbm.at[t, :, lanes], xb.at[t, :, lanes], m_ld.at[t, s])

    def cot_load(n, i):
        return pltpu.make_async_copy(
            c_hbm.at[i, pl.ds(al(sub(n) * BLK), BLK), pl.ds(al(part(n) * rows), rows)], craw.at[n % 2, i], m_cot.at[n % 2, i]
        )

    def s_copy(n, i):
        return pltpu.make_async_copy(
            sbuf.at[n % 2, i], s_hbm.at[i, pl.ds(al(sub(n) * BLK), BLK), pl.ds(al(part(n) * rows), rows)], m_out.at[n % 2, i]
        )

    def xp_copy(t):
        return rc(xb.at[t], xpb.at[t], m_xps.at[t], m_xpr.at[t], c_dev)

    def x1_copy(n, o):
        return rc(x1_s.at[o], x1_r.at[n % 2, o], m_x1s.at[o], m_x1r.at[n % 2, o], x_dev)

    def xr_copy(n, d, h, f):
        cut = pl.ds(*cuts_x[f])
        return rc(xr_s.at[d, h, cut], xr_r.at[n % 2, d, h, cut], m_xrs.at[d, h, f], m_xrr.at[n % 2, d, h, f], z_dev(d))

    def zr_copy(n, d, h, f):
        cut = pl.ds(*cuts_z[f])
        return rc(zr_s.at[d, h, cut], zr_r.at[n % 2, d, h, cut], m_zrs.at[d, h, f], m_zrr.at[n % 2, d, h, f], z_dev(d))

    def z2_copy(n, f):
        cut = pl.ds(*cuts_z[f])
        return rc(z2_s.at[cut], z2_r.at[n % 2, cut], m_z2s.at[f], m_z2r.at[n % 2, f], x_dev)

    def g_x(n, o, xx, f):
        start, size = cuts_x[f]
        return gat.at[gpair(n), pl.ds(al(part(n) * rows + start, 16), size), pl.ds(col(o, xx), BLK)]

    def g_z(n, o, xx, width, f):
        start, size = cuts_z[f]
        return gat.at[gpair(n), pl.ds(al(part(n) * rows + rx + start, 16), size), pl.ds(col(o, xx), width)]

    def z4_copy(n, f):
        blk = g_z(n, z, x, BLK, f)
        return rc(blk, blk, m_z4s.at[f], m_z4r.at[n % 2, f], x_dev)

    def gx_copy(n, d, h, f):
        blk = g_x(n, z - h if d == 0 else z + h, x, f)
        return rc(blk, blk, m_gxs.at[d, h, f], m_gxr.at[n % 2, d, h, f], z_dev(d))

    def gz_copy(n, d, h, f):
        blk = g_z(n, z - h if d == 0 else z + h, 0, NX * BLK, f)
        return rc(blk, blk, m_gzs.at[d, h, f], m_gzr.at[n % 2, d, h, f], z_dev(d))

    def x5_copy(n, o, xx, f):
        blk = g_x(n, o, xx, f)
        return rc(blk, blk, m_x5s.at[o, f], m_x5r.at[n % 2, o, f], x_dev)

    def c_copy(n, e):
        r = pl.ds(al(part(n) * rows, 16), rows)
        return rc(
            gat.at[gpair(n), r, pl.ds(col(2 * e + 1 - core, 0), NX * BLK)],
            gatp.at[gpair(n), r, pl.ds(e * NX * BLK, NX * BLK)],
            m_cs.at[e], m_cr.at[n % 4, e], c_dev,
        )

    def y_copy(p, q):
        k = pl.ds(q * dm.third, dm.third)
        return rc(y_s.at[k], y_r.at[p % 2, k], m_ys.at[q], m_yr.at[p % 2, q], y_dev)

    def own_copy(p, q, e):
        t, u = p // dm.subs, p % dm.subs
        k = pl.ds(q * dm.third, dm.third)
        return pltpu.make_async_copy(
            own.at[p % 2, k, pl.ds(e * BLK, BLK)],
            wg_hbm.at[t, k, pl.ds(al(e * dm.own + u * BLK), BLK)],
            m_own.at[p % 2, q, e],
        )

    def pg_copy(t, s):
        return pltpu.make_async_copy(pgb, pg_hbm.at[t, :, pl.ds(al(s * rows), rows)], m_pg)

    def sum_copy(k):
        to = lax.rem(bi + k, 4)
        return rc(sum_s.at[to], sum_r.at[k - 1], m_ss.at[k - 1], m_sr.at[k - 1], (wi, to))

    def factor(k, s):
        wide_hole = jnp.concatenate([hole[pl.ds(al(k * BLK), BLK)]] * (rows // BLK), axis=1)
        return 1.0 - small_img[:, pl.ds(al(s * rows), rows)] * wide_hole

    def prepare(t, s):
        @pl.loop(0, dm.feats // BLK)
        def _(k):
            at, lanes = pl.ds(al(k * BLK), BLK), pl.ds(s * rows, rows)
            masked = (xb[t, at, lanes].astype(F32) * factor(k, s)).astype(BF16)
            xb[t, at, lanes] = masked
            xt[t, pl.ds(s * rows, rows), at] = masked.T

    def prepare_cot(n):
        for i in (0, 1):
            cot_load(n, i).wait()
            cot[i, pl.ds(al(part(n) * rows), rows), pl.ds(al(sub(n) * BLK), BLK)] = craw[n % 2, i].T

    def forward(n, k):
        fwd[n % 2, :, pl.ds(k * 256, 256)] = jnp.dot(
            xt[tower(n), pl.ds(al(part(n) * rows, 16), rows), :],
            wb[(n // dm.parts) % 4, :, pl.ds(k * 256, 256)],
            preferred_element_type=F32,
        )

    def x1_send(n, q):
        o = (
            jnp.where(z < 2, 3, 0),
            jnp.where(z < 2, 2, 1),
            jnp.where(z < 2, 1 - z, 5 - z),
            z,
        )[q]

        @pl.when(n >= 1)
        def _():
            x1_copy(n, o).wait_send()

        for r, m in chunks(rx):
            x1_s[o, r : r + m] = fwd[n % 2, r : r + m, pl.ds(col(o, 1 - x), BLK)].astype(BF16)
        x1_copy(n, o).start()

    def xr_hop(n, h, f):
        start, size = cuts_x[f]
        for d in (0, 1):
            o = 3 - h + z if d == 0 else h - 3 + z

            @pl.when(far(d) <= h)
            def _():
                if f == 0:
                    x1_copy(n, o).wait_recv()
                if h:
                    @pl.when(far(d) >= 1)
                    def _():
                        xr_copy(n, d, h - 1, f).wait_recv()

                @pl.when(n >= 1)
                def _():
                    xr_copy(n, d, h, f).wait_send()

                for r, m in chunks(size):
                    r += start
                    v = fwd[n % 2, r : r + m, pl.ds(col(o, x), BLK)] + x1_r[n % 2, o, r : r + m].astype(F32)
                    if h:
                        v = v + xr_r[n % 2, d, h - 1, r : r + m].astype(F32)
                    xr_s[d, h, r : r + m] = v.astype(BF16)
                xr_copy(n, d, h, f).start()

    def zr_hop(n, h, f):
        start, size = cuts_z[f]
        for d in (0, 1):
            o = 3 - h + z if d == 0 else h - 3 + z

            @pl.when(far(d) <= h)
            def _():
                if h:
                    @pl.when(far(d) >= 1)
                    def _():
                        zr_copy(n, d, h - 1, f).wait_recv()

                @pl.when(n >= 1)
                def _():
                    zr_copy(n, d, h, f).wait_send()

                for r, m in chunks(size):
                    r += start
                    v = fwd[n % 2, rx + r : rx + r + m, pl.ds(col(o, 0), NX * BLK)]
                    if h:
                        v = v + zr_r[n % 2, d, h - 1, r : r + m].astype(F32)
                    zr_s[d, h, r : r + m] = v.astype(BF16)
                zr_copy(n, d, h, f).start()

    def z_sum(n, f):
        for d in (0, 1):
            @pl.when(far(d) >= 1)
            def _():
                zr_copy(n, d, 2, f).wait_recv()

        @pl.when(n >= 1)
        def _():
            z2_copy(n, f).wait_send()

        start, size = cuts_z[f]
        for xx in (1 - x, x):
            for r, m in chunks(size):
                r += start
                lanes = pl.ds(al(xx * BLK), BLK)
                v = (
                    fwd[n % 2, rx + r : rx + r + m, pl.ds(col(z, xx), BLK)]
                    + zr_r[n % 2, 0, 2, r : r + m, lanes].astype(F32)
                    + zr_r[n % 2, 1, 2, r : r + m, lanes].astype(F32)
                )
                if xx is x:
                    zown[r : r + m] = v
                else:
                    z2_s[r : r + m] = v.astype(BF16)
            if xx is not x:
                z2_copy(n, f).start()

    def finish(n, row0, count, total):
        t, u = tower(n), sub(n)
        lanes = pl.ds(al(u * BLK), BLK)
        base = part(n) * rows + row0
        b_row = jnp.where(t == 0, bias[0:1, lanes], bias[1:2, lanes])
        from0 = jnp.where(t == 0, st[0, 0:1, lanes], st[0, 1:2, lanes])
        from1 = jnp.where(t == 0, st[1, 0:1, lanes], st[1, 1:2, lanes])
        for r, m in chunks(count):
            at = pl.ds(al(base + r, 16), m)
            v = total(r, m) + b_row
            sq = v * v
            th = jnp.tanh(ROOT * v * (1.0 + CUBE * sq))
            half = 0.5 * (1.0 + th)
            htmp[r : r + m] = v * half
            slope = half + 0.5 * v * (1.0 - th * th) * (ROOT * (1.0 + 3.0 * CUBE * sq))
            up0, up1 = cot[0, at, lanes].astype(F32), cot[1, at, lanes].astype(F32)
            grad = (from0 * up0 + from1 * up1) * slope
            sacc[u, t] += jnp.sum(grad.reshape(m // 8, 8, BLK), axis=0)
            gat[gpair(n), at, pl.ds(col(z, x), BLK)] = grad.astype(BF16)

    def mix(n, row0, count):
        t, u = tower(n), sub(n)
        lanes = pl.ds(al(u * BLK), BLK)
        base = part(n) * rows + row0

        @pl.when(t == 0)
        def _():
            for r, m in chunks(count):
                hid0[pl.ds(al(base + r, 16), m), lanes] = htmp[r : r + m]

        @pl.when(t == 1)
        def _():
            for r, m in chunks(count):
                at = pl.ds(al(base + r, 16), m)
                h = hid0[at, lanes], htmp[r : r + m]
                for i in (0, 1):
                    up = cot[i, at, lanes].astype(F32)
                    stmp[i, row0 + r : row0 + r + m] = (st[i, 0:1, lanes] * h[0] + st[i, 1:2, lanes] * h[1]).astype(BF16)
                    for j in (0, 1):
                        sacc[u, 2 + 2 * i + j] += jnp.sum((up * h[j]).reshape(m // 8, 8, BLK), axis=0)

    def emit(n):
        @pl.when(tower(n) == 1)
        def _():
            for i in (0, 1):
                @pl.when(n >= n_units // 2 + 2)
                def _():
                    s_copy(n, i).wait()

                sbuf[n % 2, i] = stmp[i].T
                s_copy(n, i).start()

    def z_final(n, f):
        z2_copy(n, f).wait_recv()
        start, size = cuts_z[f]

        def total(r, m):
            r += start
            return zown[r : r + m] + z2_r[n % 2, r : r + m].astype(F32)

        finish(n, rx + start, size, total)

        @pl.when(n >= 1)
        def _():
            z4_copy(n, f).wait_send()

        z4_copy(n, f).start()
        mix(n, rx + start, size)

    def x_final(n, f):
        if f == 0:
            x1_copy(n, z).wait_recv()
        for d in (0, 1):
            @pl.when(far(d) >= 1)
            def _():
                xr_copy(n, d, 2, f).wait_recv()

        start, size = cuts_x[f]

        def total(r, m):
            r += start
            return (
                fwd[n % 2, r : r + m, pl.ds(col(z, x), BLK)]
                + x1_r[n % 2, z, r : r + m].astype(F32)
                + xr_r[n % 2, 0, 2, r : r + m].astype(F32)
                + xr_r[n % 2, 1, 2, r : r + m].astype(F32)
            )

        finish(n, start, size, total)
        for d in (0, 1):
            gather_hop(gx_copy, n, d, 0, f)
        x5_send(n, z, f)
        mix(n, start, size)

    def gather_hop(copy, n, d, h, f):
        @pl.when((far(d) >= h) & (far(d) <= 2))
        def _():
            @pl.when(n >= 1)
            def _():
                copy(n, d, h, f).wait_send()

            copy(n, d, h, f).start()

    def x5_send(n, o, f):
        @pl.when(n >= 1)
        def _():
            x5_copy(n, o, x, f).wait_send()

        x5_copy(n, o, x, f).start()

    def gz_first(n, f):
        z4_copy(n, f).wait_recv()
        for d in (0, 1):
            gather_hop(gz_copy, n, d, 0, f)

    def gather_arrive(copy, n, h, forward_x, f):
        for d in (0, 1):
            @pl.when(far(d) >= h + 1)
            def _():
                copy(n, d, h, f).wait_recv()
                if h < 2:
                    gather_hop(copy, n, d, h + 1, f)
                if forward_x:
                    x5_send(n, z - 1 - h if d == 0 else z + 1 + h, f)

    def gathered(n):
        for o in range(NZ):
            for f in (0, 1):
                x5_copy(n, o, 1 - x, f).wait_recv()
        for e in (0, 1):
            @pl.when(n >= 1)
            def _():
                c_copy(n, e).wait_send()

            c_copy(n, e).start()

    def back_pooled(n, q):
        t, s = tower(n), part(n)
        lanes = pl.ds(al(s * rows), rows)
        k = pl.ds(q * dm.third, dm.third)
        acc[k, lanes] += lax.dot_general(
            wb[(n // dm.parts) % 4, k, :],
            gat[gpair(n), pl.ds(al(s * rows, 16), rows), :],
            NT,
            preferred_element_type=F32,
        )
        if q < PIECES - 1:
            return

        @pl.when(sub(n) == dm.subs - 1)
        def _():
            @pl.when((t > 0) | (s > 0))
            def _():
                pg_copy(t, s).wait()

            @pl.loop(0, dm.feats // BLK)
            def _(k):
                at = pl.ds(al(k * BLK), BLK)
                pgb[at] = (acc[at, lanes] * factor(k, s)).astype(BF16)
                acc[at, lanes] = jnp.zeros((BLK, rows), F32)

            pg_copy(t, s).start()

    def y_arrive(p, q):
        k = pl.ds(q * dm.third, dm.third)
        y_copy(p, q).wait_recv()
        for r, m in chunks(dm.third):
            at = pl.ds(q * dm.third + r, m)
            own[p % 2, at] += y_r[p % 2, at].astype(F32)
        for e in (0, 1):
            own_copy(p, q, e).start()

    def back_weight(n, q):
        t, s, p = tower(n), part(n), n // dm.parts
        k, imgs = pl.ds(q * dm.third, dm.third), pl.ds(al(part(n) * rows), rows)
        if q == 0:
            for e in (0, 1):
                c_copy(n, e).wait_recv()

            @pl.when((s == 0) & (p % dm.subs == 0))
            def _():
                xp_copy(t).wait_recv()

        def grads(yy):
            lanes = pl.ds(col(2 * yy + core, 0), NX * BLK)
            return jnp.dot(xb[t, k, imgs], gat[p % 2, imgs, lanes], preferred_element_type=F32) + jnp.dot(
                xpb[t, k, imgs], gatp[p % 2, imgs, pl.ds(al(yy * NX * BLK), NX * BLK)], preferred_element_type=F32
            )

        @pl.when(s == 0)
        def _():
            @pl.when(p >= 1)
            def _():
                y_arrive(p - 1, q)

            @pl.when(p >= 2)
            def _():
                for e in (0, 1):
                    own_copy(p, q, e).wait()

            tacc[k, :] = grads(1 - y)
            own[p % 2, k, :] = grads(y)

        @pl.when(s == 1)
        def _():
            @pl.when(p >= 1)
            def _():
                y_copy(p - 1, q).wait_send()

            y_s[k, :] = (tacc[k, :] + grads(1 - y)).astype(BF16)
            y_copy(p, q).start()
            own[p % 2, k, :] += grads(y)

    def sums_send():
        for u in range(dm.subs):
            for j in range(6):
                sum_s[u, j : j + 1] = jnp.sum(sacc[u, j], axis=0, keepdims=True)
            sum_s[u, 6:8] = jnp.zeros((2, BLK), F32)
        for k in (1, 2, 3):
            sum_copy(k).start()

    x_load(0, 0).start()
    for w in range(NZ * NX):
        w_load(0, w).start()
    x_load(0, 1).start()
    for i in (0, 1):
        cot_load(0, i).start()
    for w in range(NZ * NX):
        w_load(1, w).start()
    for s in (0, 1):
        x_load(1, s).start()

    barrier = pltpu.get_barrier_semaphore()
    peers = [x_dev] + [(wi, lax.rem(bi + k, 4)) for k in (1, 2, 3)]
    for dev in peers:
        pl.semaphore_signal(barrier, inc=1, device_id=dev, device_id_type=MESH)
    for d in (0, 1):
        @pl.when(far(d) <= 2)
        def _():
            pl.semaphore_signal(barrier, inc=1, device_id=z_dev(d), device_id_type=MESH)

    small_img[...] = jnp.concatenate([group[j : j + 1] for j in range(dm.images // BLK)], axis=1).astype(F32)
    for j in range(dm.feats // BLK):
        gap = 1.0 - valid[j : j + 1].astype(F32)
        hole[j * BLK : (j + 1) * BLK] = jnp.broadcast_to(gap, (BLK, BLK)).T
    x_load(0, 0).wait()
    prepare(0, 0)

    @pl.loop(0, dm.feats // 8)
    def _(k):
        acc[pl.ds(al(k * 8, 8), 8)] = jnp.zeros((8, dm.images), F32)

    for d in (0, 1):
        @pl.when(far(d) == 0)
        def _():
            for s in (0, 1):
                for h in range(3):
                    xr_r[s, d, h] = jnp.zeros((rx, BLK), BF16)
                    zr_r[s, d, h] = jnp.zeros((rz, NX * BLK), BF16)

    pl.semaphore_wait(barrier, jnp.where((z == 0) | (z == NZ - 1), len(peers) + 1, len(peers) + 2))
    for w in range(NZ * NX):
        w_load(0, w).wait()
    for k in range(4):
        forward(0, k)
    sacc[...] = jnp.zeros_like(sacc)

    def tick(i, carry):
        a, b, c = i, i - 1, i - 2
        on_a, on_b, on_c = i >= 0, i >= 1, i >= 2
        on_f = i + 1 < n_units
        on_p = i >= 3

        def w_start():
            for w in range(NZ * NX):
                w_load(i // 2 + 2, w).start()

        def w_wait():
            for w in range(NZ * NX):
                w_load((i + 1) // 2, w).wait()

        def first_images():
            x_load(0, 1).wait()
            prepare(0, 1)
            xp_copy(0).start()

        def cot_next():
            prepare_cot(i)

            @pl.when(i + 1 < n_units // 2)
            def _():
                for j in (0, 1):
                    cot_load(i + 1, j).start()

        steps = {
            "ws": ((i % 2 == 0) & (i // 2 + 2 < dm.towers * dm.subs), w_start),
            "ww": (on_f & (i % 2 == 1), w_wait),
            "p0": (i == 0, first_images),
            "ct": (i < n_units // 2, cot_next),
            "em": (on_b, lambda: emit(b)),
            "gd": (on_c, lambda: gathered(c)),
        }
        for q in range(4):
            steps[f"x1{q}"] = on_a, functools.partial(x1_send, a, q)
            steps[f"f{q}"] = on_f, functools.partial(forward, i + 1, q)
        for h in range(PIECES):
            steps[f"bw{h}"] = on_p, functools.partial(back_weight, i - 3, h)
            steps[f"bp{h}"] = on_c, functools.partial(back_pooled, c, h)
        for f in (0, 1):
            steps[f"zf{f}"] = on_b, functools.partial(z_final, b, f)
            steps[f"xf{f}"] = on_b, functools.partial(x_final, b, f)
            steps[f"zs{f}"] = on_a, functools.partial(z_sum, a, f)
            steps[f"gs{f}"] = on_b, functools.partial(gz_first, b, f)
            for h in range(3):
                steps[f"zr{h}{f}"] = on_a, functools.partial(zr_hop, a, h, f)
                steps[f"xr{h}{f}"] = on_a, functools.partial(xr_hop, a, h, f)
                steps[f"gx{h}{f}"] = on_b, functools.partial(gather_arrive, gx_copy, b, h, True, f)
                steps[f"gz{h}{f}"] = on_c, functools.partial(gather_arrive, gz_copy, c, h, False, f)
        for name in ORDER:
            pl.when(steps[name][0])(steps[name][1])

        for s in (0, 1):
            @pl.when(i == 4 + s)
            def _():
                x_load(1, s).wait()
                prepare(1, s)
                if s:
                    xp_copy(1).start()

        return carry

    lax.fori_loop(0, n_units, tick, 0)

    last, pairs = n_units - 1, dm.towers * dm.subs
    ends = {
        "em": lambda: emit(last),
        "hd": lambda: gathered(last - 1),
        "gd": lambda: gathered(last),
        "ss": sums_send,
    }
    for q in range(PIECES):
        ends[f"bv{q}"] = functools.partial(back_weight, last - 2, q)
        ends[f"bw{q}"] = functools.partial(back_weight, last - 1, q)
        ends[f"bx{q}"] = functools.partial(back_weight, last, q)
        ends[f"hp{q}"] = functools.partial(back_pooled, last - 1, q)
        ends[f"bp{q}"] = functools.partial(back_pooled, last, q)
    for f in (0, 1):
        ends[f"zf{f}"] = functools.partial(z_final, last, f)
        ends[f"xf{f}"] = functools.partial(x_final, last, f)
        ends[f"gs{f}"] = functools.partial(gz_first, last, f)
        for h in range(3):
            ends[f"gx{h}{f}"] = functools.partial(gather_arrive, gx_copy, last, h, True, f)
            ends[f"gz{h}{f}"] = functools.partial(gather_arrive, gz_copy, last, h, False, f)
            ends[f"hz{h}{f}"] = functools.partial(gather_arrive, gz_copy, last - 1, h, False, f)
    for name in DRAIN:
        ends[name]()

    for k in (1, 2, 3):
        sum_copy(k).wait_recv()
    total = sum_s[bi] + sum_r[0] + sum_r[1] + sum_r[2]
    out_b[...] = total[0:2]
    for i in (0, 1):
        out_sg[i] = total[2 + 2 * i : 4 + 2 * i]
        out_sn[i] = st[i, :, pl.ds(al(bi * BLK), BLK)] - step_ref[0] * total[2 + 2 * i : 4 + 2 * i]
    for q in range(PIECES):
        y_arrive(pairs - 1, q)
    for q in range(PIECES):
        for e in (0, 1):
            own_copy(pairs - 2, q, e).wait()
            own_copy(pairs - 1, q, e).wait()
        y_copy(pairs - 1, q).wait_send()
    pg_copy(1, 1).wait()
    for i in (0, 1):
        s_copy(last - 1, i).wait()
        s_copy(last, i).wait()
    for t in range(dm.towers):
        xp_copy(t).wait_send()
    for k in (1, 2, 3):
        sum_copy(k).wait_send()
    for e in (0, 1):
        c_copy(last, e).wait_send()
    for o in range(NZ):
        x1_copy(last, o).wait_send()
    for f in (0, 1):
        for o in range(NZ):
            x5_copy(last, o, x, f).wait_send()
        z2_copy(last, f).wait_send()
        z4_copy(last, f).wait_send()
        for d in (0, 1):
            for h in range(3):
                @pl.when(far(d) <= h)
                def _():
                    xr_copy(last, d, h, f).wait_send()
                    zr_copy(last, d, h, f).wait_send()

                @pl.when((far(d) >= h) & (far(d) <= 2))
                def _():
                    gx_copy(last, d, h, f).wait_send()
                    gz_copy(last, d, h, f).wait_send()


def carry_out(*refs):
    count = len(refs) // 2
    for src, dst in zip(refs[:count], refs[count:]):
        dst[...] = src[...]


def fused(pooled, weight, fc_bias, stitch, cotangent, valid_mask, image_group, step_rate):
    dm = Dims(pooled, weight, cotangent)
    towers, feats, images, own = dm.towers, dm.feats, dm.images, dm.own
    rows, rx, rz, cols = dm.rows, dm.rx, dm.rz, dm.cols
    dma = pltpu.SemaphoreType.DMA
    vm = pltpu.VMEM
    scratch = [
        vm((4, feats, cols), BF16),
        vm((towers, images, feats), BF16),
        vm((towers, feats, images), BF16),
        vm((towers, feats, images), BF16),
        vm((feats, BLK), F32),
        vm((1, images), F32),
        vm((2, 2, BLK, rows), BF16),
        vm((2, images, own), BF16),
        vm((2, rows, BLK), BF16),
        vm((2, 2, BLK, rows), BF16),
        vm((feats, images), F32),
        vm((2, rows, cols), F32),
        vm((2, images, cols), BF16),
        vm((2, images, cols // 2), BF16),
        vm((NZ, rx, BLK), BF16),
        vm((2, NZ, rx, BLK), BF16),
        vm((2, 3, rx, BLK), BF16),
        vm((2, 2, 3, rx, BLK), BF16),
        vm((2, 3, rz, NX * BLK), BF16),
        vm((2, 2, 3, rz, NX * BLK), BF16),
        vm((rz, BLK), F32),
        vm((rz, BLK), BF16),
        vm((2, rz, BLK), BF16),
        vm((2, feats, NX * BLK), F32),
        vm((feats, NX * BLK), F32),
        vm((feats, NX * BLK), BF16),
        vm((2, feats, NX * BLK), BF16),
        vm((images, own), F32),
        vm((max(rx, rz), BLK), F32),
        vm((feats, rows), BF16),
        vm((dm.subs, 6, 8, BLK), F32),
        vm((dm.subs, 8, BLK), F32),
        vm((3, 8, BLK), F32),
    ] + [
        dma(shape)
        for shape in (
            (4, NZ * NX), (2, 2), (NZ,), (2, NZ), (2, 3, 2), (2, 2, 3, 2), (2, 3, 2), (2, 2, 3, 2), (2,), (2, 2), (2,), (2, 2),
            (2, 3, 2), (2, 2, 3, 2), (2, 3, 2), (2, 2, 3, 2), (NZ, 2), (2, NZ, 2), (2,), (4, 2), (PIECES,), (2, PIECES), (3,), (3,),
            (2,), (2,), (2, PIECES, 2), (), (2, 2), (2, 2),
        )
    ]
    anyspace = pl.BlockSpec(memory_space=pl.ANY)
    inside = pl.BlockSpec(memory_space=pltpu.VMEM)
    out_shape = [
        jax.ShapeDtypeStruct((2, own, images), BF16),
        jax.ShapeDtypeStruct((towers, feats, images), BF16),
        jax.ShapeDtypeStruct((towers, feats, images), F32),
        jax.ShapeDtypeStruct((2, BLK), F32),
        jax.ShapeDtypeStruct((2, 2, BLK), F32),
        jax.ShapeDtypeStruct((2, 2, BLK), F32),
    ]
    out_specs = [anyspace] * 3 + [inside] * 3
    results = pl.pallas_call(
        functools.partial(kernel, dm),
        name="stitch_fc6",
        out_shape=out_shape,
        in_specs=[pl.BlockSpec(memory_space=pltpu.SMEM)] + [anyspace] * 3 + [inside] * 4,
        out_specs=out_specs,
        scratch_shapes=scratch,
        compiler_params=pltpu.CompilerParams(collective_id=1, has_side_effects=True, vmem_limit_bytes=61 * 2**20),
        cost_estimate=pl.CostEstimate(
            flops=6 * towers * feats * images * dm.chans, bytes_accessed=60 * 2**20, transcendentals=towers * images * own
        ),
    )(
        step_rate, weight, pooled, cotangent, fc_bias, stitch,
        valid_mask.reshape(feats // BLK, BLK), image_group.reshape(images // BLK, BLK),
    )
    def block(shape):
        if len(shape.shape) == 3 and shape.shape[1] % (CUTS * 16) == 0:
            return pl.BlockSpec((shape.shape[0], shape.shape[1] // CUTS, shape.shape[2]), lambda c: (0, c, 0))
        return pl.BlockSpec(shape.shape, lambda c: (0,) * len(shape.shape))

    blocks = [block(shape) for shape in out_shape]
    return pl.pallas_call(
        carry_out,
        name="carry_out",
        grid=(CUTS,),
        out_shape=out_shape,
        in_specs=blocks,
        out_specs=blocks,
        compiler_params=pltpu.CompilerParams(vmem_limit_bytes=60 * 2**20),
    )(*results)


def gelu_local(values):
    return jax.nn.gelu(values, approximate=True)


def plain(pooled, weight, fc_bias, stitch, cotangent, valid_mask, image_group, step_rate):
    highest = lax.Precision.HIGHEST
    factor = 1.0 - image_group[None, :].astype(F32) * (1.0 - valid_mask[:, None].astype(F32))
    masked = pooled * factor.astype(BF16)[None]
    owned = weight.shape[2] // lax.axis_size("wide")
    summed = lax.psum_scatter(
        jnp.einsum("tkc,tkb->ctb", weight, masked, preferred_element_type=F32), "wide", scatter_dimension=0, tiled=True
    )
    pre_act = summed + jnp.transpose(fc_bias)[:, :, None]
    hidden, gelu_back = jax.vjp(gelu_local, pre_act)
    stitched = jnp.einsum("ijc,cjb->icb", stitch, hidden, precision=highest)
    upstream = cotangent.astype(F32)
    stitch_part = jnp.einsum("icb,cjb->ijc", upstream, hidden, precision=highest)
    hidden_grad = jnp.einsum("ijc,icb->cjb", stitch, upstream, precision=highest)
    pre_grad = gelu_back(hidden_grad)[0]
    bias_part = jnp.transpose(jnp.sum(pre_grad, axis=2))
    pre_low = pre_grad.astype(BF16)
    bias_grad = lax.psum_scatter(bias_part, "batch", scatter_dimension=1, tiled=True)
    stitch_grad = lax.psum_scatter(stitch_part, "batch", scatter_dimension=2, tiled=True)
    portion = lax.all_gather(pre_low, "wide", axis=0, tiled=True)
    input_sum = jnp.einsum("tkc,ctb->tkb", weight, portion, preferred_element_type=F32)
    block_grad = jnp.einsum("tkb,ctb->tkc", masked, portion, preferred_element_type=F32)
    pooled_grad = (input_sum * factor[None]).astype(BF16)
    weight_grad = lax.psum_scatter(block_grad, "batch", scatter_dimension=2, tiled=True)
    share = owned // lax.axis_size("batch")
    stitch_mine = lax.dynamic_slice_in_dim(stitch, lax.axis_index("batch") * share, share, 2)
    stitch_new = stitch_mine - step_rate[0] * stitch_grad
    return stitched.astype(BF16), pooled_grad, weight_grad, bias_grad, stitch_grad, stitch_new


def fits(mesh, pooled, weight, cotangent):
    return (
        (mesh.shape["wide"], mesh.shape["batch"]) == (NZ * NX, 4)
        and pooled.shape[0] == 2
        and cotangent.shape[1] == 4 * BLK
        and weight.shape[2] == NZ * NX * cotangent.shape[1]
        and pooled.shape[2] % 512 == 0
        and pooled.shape[1] % (16 * PIECES) == 0
        and pooled.shape[1] % BLK == 0
    )


def solution(mesh):
    def body(pooled, weight, fc_bias, stitch, cotangent, *rest):
        form = fused if fits(mesh, pooled, weight, cotangent) else plain
        return form(pooled, weight, fc_bias, stitch, cotangent, *rest)

    return jax.shard_map(
        body,
        mesh=mesh,
        in_specs=(
            P(None, "wide", "batch"),
            P(None, "wide", None),
            P(None, "wide"),
            P(None, None, "wide"),
            P(None, "wide", "batch"),
            P("wide"),
            P("batch"),
            P(),
        ),
        out_specs=(
            P(None, "wide", "batch"),
            P(None, "wide", "batch"),
            P(None, "wide", "batch"),
            P(None, ("wide", "batch")),
            P(None, None, ("wide", "batch")),
            P(None, None, ("wide", "batch")),
        ),
        check_vma=False,
    )
```

```python
import functools
import math

import jax
import jax.numpy as jnp
from jax import lax
from jax.experimental import pallas as pl
from jax.experimental.pallas import tpu as pltpu
from jax.sharding import PartitionSpec as P

MESH = pl.DeviceIdType.MESH
BLK = 128
NZ, NX = 4, 2
F32, BF16 = jnp.float32, jnp.bfloat16
NT = (((1,), (1,)), ((), ()))
ROOT = math.sqrt(2.0 / math.pi)
CUBE = 0.044715
PIECES = 3
CUTS = 4
DRAIN = (
    "zf0", "xf0", "zf1", "xf1", "hz00", "hz01", "bv0", "gs0", "gx00", "gs1", "gx01", "hz10", "hz11", "bv1", "em",
    "gz00", "gx10", "gz01", "gx11", "hz20", "hz21", "hd", "bv2", "gz10", "gx20", "gz11", "gx21", "hp0", "hp1", "hp2",
    "ss", "bw0", "bw1", "bw2", "gz20", "gz21", "gd", "bp0", "bp1", "bp2", "bx0", "bx1", "bx2",
)
ORDER = (
    "zr00", "ws", "zf0", "gz00", "bw0", "x10", "xf0", "ww", "p0", "zr01", "zf1", "gz01", "bw1", "xf1", "f0",
    "zr10", "gz10", "f1", "x11", "xr00", "gx00", "em", "zr11", "gz11", "bw2", "xr01", "gx01", "f2",
    "zr20", "gz20", "ct", "az", "x12", "xr10", "gx10", "f3", "zr21", "gz21", "gd", "bp0", "xr11", "gx11",
    "zs0", "gs0", "x13", "xr20", "gx20", "bp1", "zs1", "gs1", "bp2", "xr21", "gx21",
)


class Dims:
    def __init__(self, pooled, weight, cotangent):
        self.towers, self.feats, self.images = pooled.shape
        self.chans = weight.shape[2]
        self.own = cotangent.shape[1]
        self.subs = self.own // BLK
        self.parts = 2
        self.rows = self.images // self.parts
        self.rx = (self.rows * 19 // 32) // 16 * 16
        self.rz = self.rows - self.rx
        self.units = self.towers * self.subs * self.parts
        self.cols = NZ * NX * BLK
        self.third = self.feats // PIECES


def chunks(count, size=64):
    return [(r, min(size, count - r)) for r in range(0, count, size)]


def kernel(
    dm,
    step_ref, w_hbm, p_hbm, c_hbm, bias, st, valid, group,
    s_hbm, pg_hbm, wg_hbm, out_b, out_sg, out_sn, mine_hbm, theirs_hbm,
    wb, xt, xb, xpb, hole, small_img, craw, cot, stmp, sbuf, acc, fwd, gat, gatp,
    x1_s, x1_r, xr_s, xr_r, zr_s, zr_r, zown, z2_s, z2_r,
    own, tacc, y_s, y_r, hid0, htmp, pgb, sacc, sum_s, sum_r,
    m_w, m_ld, m_x1s, m_x1r, m_xrs, m_xrr, m_zrs, m_zrr, m_z2s, m_z2r, m_z4s, m_z4r,
    m_gxs, m_gxr, m_gzs, m_gzr, m_x5s, m_x5r, m_cs, m_cr, m_ys, m_yr, m_ss, m_sr, m_xps, m_xpr, m_own, m_pg,
    m_cot, m_out, m_last,
):
    n_units, rows, rx, rz = dm.units, dm.rows, dm.rx, dm.rz
    mid_x, mid_z = rx // 32 * 16, rz // 32 * 16
    cuts_x = (0, mid_x), (mid_x, rx - mid_x)
    cuts_z = (0, mid_z), (mid_z, rz - mid_z)
    wi, bi = lax.axis_index("wide"), lax.axis_index("batch")
    z, x = wi // NX, wi % NX
    y, core = bi // 2, bi % 2
    x_dev = (z * NX + 1 - x, bi)
    c_dev = (wi, y * 2 + 1 - core)
    y_dev = (wi, (1 - y) * 2 + core)

    def z_dev(d):
        return (wi + NX, bi) if d == 0 else (wi - NX, bi)

    def far(d):
        return z if d == 0 else NZ - 1 - z

    def rc(src, dst, ss, rs, dev):
        return pltpu.make_async_remote_copy(src, dst, ss, rs, device_id=dev, device_id_type=MESH)

    def al(v, k=BLK):
        return v if isinstance(v, int) else pl.multiple_of(v, k)

    def tower(n):
        return n // (dm.subs * dm.parts)

    def sub(n):
        return (n // dm.parts) % dm.subs

    def part(n):
        return n % dm.parts

    def gpair(n):
        return (n // dm.parts) % 2

    def col(o, xx):
        return al((o * NX + xx) * BLK)

    def w_load(p, w):
        t, u = p // dm.subs, p % dm.subs
        return pltpu.make_async_copy(
            w_hbm.at[t, :, pl.ds(al(w * dm.own + u * BLK), BLK)], wb.at[p % 4, :, pl.ds(w * BLK, BLK)], m_w.at[p % 4, w]
        )

    def x_load(t, s):
        lanes = pl.ds(s * rows, rows)
        return pltpu.make_async_copy(p_hbm.at[t, :, lanes], xb.at[t, :, lanes], m_ld.at[t, s])

    def cot_load(n, i):
        return pltpu.make_async_copy(
            c_hbm.at[i, pl.ds(al(sub(n) * BLK), BLK), pl.ds(al(part(n) * rows), rows)], craw.at[n % 2, i], m_cot.at[n % 2, i]
        )

    def s_copy(n, i):
        return pltpu.make_async_copy(
            sbuf.at[n % 2, i], s_hbm.at[i, pl.ds(al(sub(n) * BLK), BLK), pl.ds(al(part(n) * rows), rows)], m_out.at[n % 2, i]
        )

    def xp_copy(t):
        return rc(xb.at[t], xpb.at[t], m_xps.at[t], m_xpr.at[t], c_dev)

    def x1_copy(n, o):
        return rc(x1_s.at[o], x1_r.at[n % 2, o], m_x1s.at[o], m_x1r.at[n % 2, o], x_dev)

    def xr_copy(n, d, h, f):
        cut = pl.ds(*cuts_x[f])
        return rc(xr_s.at[d, h, cut], xr_r.at[n % 2, d, h, cut], m_xrs.at[d, h, f], m_xrr.at[n % 2, d, h, f], z_dev(d))

    def zr_copy(n, d, h, f):
        cut = pl.ds(*cuts_z[f])
        return rc(zr_s.at[d, h, cut], zr_r.at[n % 2, d, h, cut], m_zrs.at[d, h, f], m_zrr.at[n % 2, d, h, f], z_dev(d))

    def z2_copy(n, f):
        cut = pl.ds(*cuts_z[f])
        return rc(z2_s.at[cut], z2_r.at[n % 2, cut], m_z2s.at[f], m_z2r.at[n % 2, f], x_dev)

    def g_x(n, o, xx, f):
        start, size = cuts_x[f]
        return gat.at[gpair(n), pl.ds(al(part(n) * rows + start, 16), size), pl.ds(col(o, xx), BLK)]

    def g_z(n, o, xx, width, f):
        start, size = cuts_z[f]
        return gat.at[gpair(n), pl.ds(al(part(n) * rows + rx + start, 16), size), pl.ds(col(o, xx), width)]

    def z4_copy(n, f):
        blk = g_z(n, z, x, BLK, f)
        return rc(blk, blk, m_z4s.at[f], m_z4r.at[n % 2, f], x_dev)

    def gx_copy(n, d, h, f):
        blk = g_x(n, z - h if d == 0 else z + h, x, f)
        return rc(blk, blk, m_gxs.at[d, h, f], m_gxr.at[n % 2, d, h, f], z_dev(d))

    def gz_copy(n, d, h, f):
        blk = g_z(n, z - h if d == 0 else z + h, 0, NX * BLK, f)
        return rc(blk, blk, m_gzs.at[d, h, f], m_gzr.at[n % 2, d, h, f], z_dev(d))

    def x5_copy(n, o, xx, f):
        blk = g_x(n, o, xx, f)
        return rc(blk, blk, m_x5s.at[o, f], m_x5r.at[n % 2, o, f], x_dev)

    def c_copy(n, e):
        r = pl.ds(al(part(n) * rows, 16), rows)
        return rc(
            gat.at[gpair(n), r, pl.ds(col(2 * e + 1 - core, 0), NX * BLK)],
            gatp.at[gpair(n), r, pl.ds(e * NX * BLK, NX * BLK)],
            m_cs.at[e], m_cr.at[n % 4, e], c_dev,
        )

    def y_copy(p, q):
        k = pl.ds(q * dm.third, dm.third)
        return rc(y_s.at[k], y_r.at[p % 2, k], m_ys.at[q], m_yr.at[p % 2, q], y_dev)

    def own_copy(p, q, e):
        t, u = p // dm.subs, p % dm.subs
        k = pl.ds(q * dm.third, dm.third)
        return pltpu.make_async_copy(
            own.at[p % 2, k, pl.ds(e * BLK, BLK)],
            wg_hbm.at[t, k, pl.ds(al(e * dm.own + u * BLK), BLK)],
            m_own.at[p % 2, q, e],
        )

    def last_copies(q):
        k = pl.ds(q * dm.third, dm.third)
        return (
            pltpu.make_async_copy(y_s.at[k], theirs_hbm.at[k], m_last.at[q, 0]),
            pltpu.make_async_copy(own.at[(dm.towers * dm.subs - 1) % 2, k], mine_hbm.at[k], m_last.at[q, 1]),
        )

    def pg_copy(t, s):
        return pltpu.make_async_copy(pgb, pg_hbm.at[t, :, pl.ds(al(s * rows), rows)], m_pg)

    def sum_copy(k):
        to = lax.rem(bi + k, 4)
        return rc(sum_s.at[to], sum_r.at[k - 1], m_ss.at[k - 1], m_sr.at[k - 1], (wi, to))

    def factor(k, s):
        wide_hole = jnp.concatenate([hole[pl.ds(al(k * BLK), BLK)]] * (rows // BLK), axis=1)
        return 1.0 - small_img[:, pl.ds(al(s * rows), rows)] * wide_hole

    def prepare(t, s):
        @pl.loop(0, dm.feats // BLK)
        def _(k):
            at, lanes = pl.ds(al(k * BLK), BLK), pl.ds(s * rows, rows)
            masked = (xb[t, at, lanes].astype(F32) * factor(k, s)).astype(BF16)
            xb[t, at, lanes] = masked
            xt[t, pl.ds(s * rows, rows), at] = masked.T

    def prepare_cot(n):
        for i in (0, 1):
            cot_load(n, i).wait()
            cot[i, pl.ds(al(part(n) * rows), rows), pl.ds(al(sub(n) * BLK), BLK)] = craw[n % 2, i].T

    def forward(n, k):
        fwd[n % 2, :, pl.ds(k * 256, 256)] = jnp.dot(
            xt[tower(n), pl.ds(al(part(n) * rows, 16), rows), :],
            wb[(n // dm.parts) % 4, :, pl.ds(k * 256, 256)],
            preferred_element_type=F32,
        )

    def x1_send(n, q):
        o = (
            jnp.where(z < 2, 3, 0),
            jnp.where(z < 2, 2, 1),
            jnp.where(z < 2, 1 - z, 5 - z),
            z,
        )[q]

        @pl.when(n >= 1)
        def _():
            x1_copy(n, o).wait_send()

        for r, m in chunks(rx):
            x1_s[o, r : r + m] = fwd[n % 2, r : r + m, pl.ds(col(o, 1 - x), BLK)].astype(BF16)
        x1_copy(n, o).start()

    def xr_hop(n, h, f):
        start, size = cuts_x[f]
        for d in (0, 1):
            o = 3 - h + z if d == 0 else h - 3 + z

            @pl.when(far(d) <= h)
            def _():
                if f == 0:
                    x1_copy(n, o).wait_recv()
                if h:
                    @pl.when(far(d) >= 1)
                    def _():
                        xr_copy(n, d, h - 1, f).wait_recv()

                @pl.when(n >= 1)
                def _():
                    xr_copy(n, d, h, f).wait_send()

                for r, m in chunks(size):
                    r += start
                    v = fwd[n % 2, r : r + m, pl.ds(col(o, x), BLK)] + x1_r[n % 2, o, r : r + m].astype(F32)
                    if h:
                        v = v + xr_r[n % 2, d, h - 1, r : r + m].astype(F32)
                    xr_s[d, h, r : r + m] = v.astype(BF16)
                xr_copy(n, d, h, f).start()

    def zr_hop(n, h, f):
        start, size = cuts_z[f]
        for d in (0, 1):
            o = 3 - h + z if d == 0 else h - 3 + z

            @pl.when(far(d) <= h)
            def _():
                if h:
                    @pl.when(far(d) >= 1)
                    def _():
                        zr_copy(n, d, h - 1, f).wait_recv()

                @pl.when(n >= 1)
                def _():
                    zr_copy(n, d, h, f).wait_send()

                for r, m in chunks(size):
                    r += start
                    v = fwd[n % 2, rx + r : rx + r + m, pl.ds(col(o, 0), NX * BLK)]
                    if h:
                        v = v + zr_r[n % 2, d, h - 1, r : r + m].astype(F32)
                    zr_s[d, h, r : r + m] = v.astype(BF16)
                zr_copy(n, d, h, f).start()

    def z_sum(n, f):
        for d in (0, 1):
            @pl.when(far(d) >= 1)
            def _():
                zr_copy(n, d, 2, f).wait_recv()

        @pl.when(n >= 1)
        def _():
            z2_copy(n, f).wait_send()

        start, size = cuts_z[f]
        for xx in (1 - x, x):
            for r, m in chunks(size):
                r += start
                lanes = pl.ds(al(xx * BLK), BLK)
                v = (
                    fwd[n % 2, rx + r : rx + r + m, pl.ds(col(z, xx), BLK)]
                    + zr_r[n % 2, 0, 2, r : r + m, lanes].astype(F32)
                    + zr_r[n % 2, 1, 2, r : r + m, lanes].astype(F32)
                )
                if xx is x:
                    zown[r : r + m] = v
                else:
                    z2_s[r : r + m] = v.astype(BF16)
            if xx is not x:
                z2_copy(n, f).start()

    def finish(n, row0, count, total):
        t, u = tower(n), sub(n)
        lanes = pl.ds(al(u * BLK), BLK)
        base = part(n) * rows + row0
        b_row = jnp.where(t == 0, bias[0:1, lanes], bias[1:2, lanes])
        from0 = jnp.where(t == 0, st[0, 0:1, lanes], st[0, 1:2, lanes])
        from1 = jnp.where(t == 0, st[1, 0:1, lanes], st[1, 1:2, lanes])
        for r, m in chunks(count):
            at = pl.ds(al(base + r, 16), m)
            v = total(r, m) + b_row
            sq = v * v
            th = jnp.tanh(ROOT * v * (1.0 + CUBE * sq))
            half = 0.5 * (1.0 + th)
            htmp[r : r + m] = v * half
            slope = half + 0.5 * v * (1.0 - th * th) * (ROOT * (1.0 + 3.0 * CUBE * sq))
            up0, up1 = cot[0, at, lanes].astype(F32), cot[1, at, lanes].astype(F32)
            grad = (from0 * up0 + from1 * up1) * slope
            sacc[u, t] += jnp.sum(grad.reshape(m // 8, 8, BLK), axis=0)
            gat[gpair(n), at, pl.ds(col(z, x), BLK)] = grad.astype(BF16)

    def mix(n, row0, count):
        t, u = tower(n), sub(n)
        lanes = pl.ds(al(u * BLK), BLK)
        base = part(n) * rows + row0

        @pl.when(t == 0)
        def _():
            for r, m in chunks(count):
                hid0[pl.ds(al(base + r, 16), m), lanes] = htmp[r : r + m]

        @pl.when(t == 1)
        def _():
            for r, m in chunks(count):
                at = pl.ds(al(base + r, 16), m)
                h = hid0[at, lanes], htmp[r : r + m]
                for i in (0, 1):
                    up = cot[i, at, lanes].astype(F32)
                    stmp[i, row0 + r : row0 + r + m] = (st[i, 0:1, lanes] * h[0] + st[i, 1:2, lanes] * h[1]).astype(BF16)
                    for j in (0, 1):
                        sacc[u, 2 + 2 * i + j] += jnp.sum((up * h[j]).reshape(m // 8, 8, BLK), axis=0)

    def emit(n):
        @pl.when(tower(n) == 1)
        def _():
            for i in (0, 1):
                @pl.when(n >= n_units // 2 + 2)
                def _():
                    s_copy(n, i).wait()

                sbuf[n % 2, i] = stmp[i].T
                s_copy(n, i).start()

    def z_final(n, f):
        z2_copy(n, f).wait_recv()
        start, size = cuts_z[f]

        def total(r, m):
            r += start
            return zown[r : r + m] + z2_r[n % 2, r : r + m].astype(F32)

        finish(n, rx + start, size, total)

        @pl.when(n >= 1)
        def _():
            z4_copy(n, f).wait_send()

        z4_copy(n, f).start()
        mix(n, rx + start, size)

    def x_final(n, f):
        if f == 0:
            x1_copy(n, z).wait_recv()
        for d in (0, 1):
            @pl.when(far(d) >= 1)
            def _():
                xr_copy(n, d, 2, f).wait_recv()

        start, size = cuts_x[f]

        def total(r, m):
            r += start
            return (
                fwd[n % 2, r : r + m, pl.ds(col(z, x), BLK)]
                + x1_r[n % 2, z, r : r + m].astype(F32)
                + xr_r[n % 2, 0, 2, r : r + m].astype(F32)
                + xr_r[n % 2, 1, 2, r : r + m].astype(F32)
            )

        finish(n, start, size, total)
        for d in (0, 1):
            gather_hop(gx_copy, n, d, 0, f)
        x5_send(n, z, f)
        mix(n, start, size)

    def gather_hop(copy, n, d, h, f):
        @pl.when((far(d) >= h) & (far(d) <= 2))
        def _():
            @pl.when(n >= 1)
            def _():
                copy(n, d, h, f).wait_send()

            copy(n, d, h, f).start()

    def x5_send(n, o, f):
        @pl.when(n >= 1)
        def _():
            x5_copy(n, o, x, f).wait_send()

        x5_copy(n, o, x, f).start()

    def gz_first(n, f):
        z4_copy(n, f).wait_recv()
        for d in (0, 1):
            gather_hop(gz_copy, n, d, 0, f)

    def gather_arrive(copy, n, h, forward_x, f):
        for d in (0, 1):
            @pl.when(far(d) >= h + 1)
            def _():
                copy(n, d, h, f).wait_recv()
                if h < 2:
                    gather_hop(copy, n, d, h + 1, f)
                if forward_x:
                    x5_send(n, z - 1 - h if d == 0 else z + 1 + h, f)

    def gathered(n):
        for o in range(NZ):
            for f in (0, 1):
                x5_copy(n, o, 1 - x, f).wait_recv()
        for e in (0, 1):
            @pl.when(n >= 1)
            def _():
                c_copy(n, e).wait_send()

            c_copy(n, e).start()

    def back_pooled(n, q):
        t, s = tower(n), part(n)
        lanes = pl.ds(al(s * rows), rows)
        k = pl.ds(q * dm.third, dm.third)
        acc[k, lanes] += lax.dot_general(
            wb[(n // dm.parts) % 4, k, :],
            gat[gpair(n), pl.ds(al(s * rows, 16), rows), :],
            NT,
            preferred_element_type=F32,
        )
        if q < PIECES - 1:
            return

        @pl.when(sub(n) == dm.subs - 1)
        def _():
            @pl.when((t > 0) | (s > 0))
            def _():
                pg_copy(t, s).wait()

            @pl.loop(0, dm.feats // BLK)
            def _(k):
                at = pl.ds(al(k * BLK), BLK)
                pgb[at] = (acc[at, lanes] * factor(k, s)).astype(BF16)
                acc[at, lanes] = jnp.zeros((BLK, rows), F32)

            pg_copy(t, s).start()

    def y_arrive(p, q):
        k = pl.ds(q * dm.third, dm.third)
        y_copy(p, q).wait_recv()
        for r, m in chunks(dm.third):
            at = pl.ds(q * dm.third + r, m)
            own[p % 2, at] += y_r[p % 2, at].astype(F32)
        for e in (0, 1):
            own_copy(p, q, e).start()

    def back_weight(n, q):
        t, s, p = tower(n), part(n), n // dm.parts
        is_last = isinstance(n, int) and n == n_units - 1
        k, imgs = pl.ds(q * dm.third, dm.third), pl.ds(al(part(n) * rows), rows)
        if q == 0:
            for e in (0, 1):
                c_copy(n, e).wait_recv()

            @pl.when((s == 0) & (p % dm.subs == 0))
            def _():
                xp_copy(t).wait_recv()

        def grads(yy):
            lanes = pl.ds(col(2 * yy + core, 0), NX * BLK)
            return jnp.dot(xb[t, k, imgs], gat[p % 2, imgs, lanes], preferred_element_type=F32) + jnp.dot(
                xpb[t, k, imgs], gatp[p % 2, imgs, pl.ds(al(yy * NX * BLK), NX * BLK)], preferred_element_type=F32
            )

        @pl.when(s == 0)
        def _():
            @pl.when(p >= 1)
            def _():
                y_arrive(p - 1, q)

            @pl.when(p >= 2)
            def _():
                for e in (0, 1):
                    own_copy(p, q, e).wait()

            tacc[k, :] = grads(1 - y)
            own[p % 2, k, :] = grads(y)

        @pl.when(s == 1)
        def _():
            @pl.when(p >= 1)
            def _():
                y_copy(p - 1, q).wait_send()

            y_s[k, :] = (tacc[k, :] + grads(1 - y)).astype(BF16)
            if not is_last:
                y_copy(p, q).start()
            own[p % 2, k, :] += grads(y)
            if is_last:
                for copy in last_copies(q):
                    copy.start()

    def sums_send():
        for u in range(dm.subs):
            for j in range(6):
                sum_s[u, j : j + 1] = jnp.sum(sacc[u, j], axis=0, keepdims=True)
            sum_s[u, 6:8] = jnp.zeros((2, BLK), F32)
        for k in (1, 2, 3):
            sum_copy(k).start()

    x_load(0, 0).start()
    for w in range(NZ * NX):
        w_load(0, w).start()
    x_load(0, 1).start()
    for i in (0, 1):
        cot_load(0, i).start()
    for w in range(NZ * NX):
        w_load(1, w).start()
    for s in (0, 1):
        x_load(1, s).start()

    barrier = pltpu.get_barrier_semaphore()
    peers = [x_dev] + [(wi, lax.rem(bi + k, 4)) for k in (1, 2, 3)]
    for dev in peers:
        pl.semaphore_signal(barrier, inc=1, device_id=dev, device_id_type=MESH)
    for d in (0, 1):
        @pl.when(far(d) <= 2)
        def _():
            pl.semaphore_signal(barrier, inc=1, device_id=z_dev(d), device_id_type=MESH)

    small_img[...] = jnp.concatenate([group[j : j + 1] for j in range(dm.images // BLK)], axis=1).astype(F32)
    for j in range(dm.feats // BLK):
        gap = 1.0 - valid[j : j + 1].astype(F32)
        hole[j * BLK : (j + 1) * BLK] = jnp.broadcast_to(gap, (BLK, BLK)).T
    x_load(0, 0).wait()
    prepare(0, 0)

    for d in (0, 1):
        @pl.when(far(d) == 0)
        def _():
            for s in (0, 1):
                for h in range(3):
                    xr_r[s, d, h] = jnp.zeros((rx, BLK), BF16)
                    zr_r[s, d, h] = jnp.zeros((rz, NX * BLK), BF16)

    pl.semaphore_wait(barrier, jnp.where((z == 0) | (z == NZ - 1), len(peers) + 1, len(peers) + 2))
    for w in range(NZ * NX):
        w_load(0, w).wait()
    for k in range(4):
        forward(0, k)
    sacc[...] = jnp.zeros_like(sacc)

    def tick(i, carry):
        a, b, c = i, i - 1, i - 2
        on_a, on_b, on_c = i >= 0, i >= 1, i >= 2
        on_f = i + 1 < n_units
        on_p = i >= 3

        def clear():
            @pl.loop(0, dm.feats // 32)
            def _(k):
                acc[pl.ds(al(k * 32, 32), 32)] = jnp.zeros((32, dm.images), F32)

        def w_start():
            for w in range(NZ * NX):
                w_load(i // 2 + 2, w).start()

        def w_wait():
            for w in range(NZ * NX):
                w_load((i + 1) // 2, w).wait()

        def first_images():
            x_load(0, 1).wait()
            prepare(0, 1)
            xp_copy(0).start()

        def cot_next():
            prepare_cot(i)

            @pl.when(i + 1 < n_units // 2)
            def _():
                for j in (0, 1):
                    cot_load(i + 1, j).start()

        steps = {
            "ws": ((i % 2 == 0) & (i // 2 + 2 < dm.towers * dm.subs), w_start),
            "ww": (on_f & (i % 2 == 1), w_wait),
            "az": (i == 0, clear),
            "p0": (i == 0, first_images),
            "ct": (i < n_units // 2, cot_next),
            "em": (on_b, lambda: emit(b)),
            "gd": (on_c, lambda: gathered(c)),
        }
        for q in range(4):
            steps[f"x1{q}"] = on_a, functools.partial(x1_send, a, q)
            steps[f"f{q}"] = on_f, functools.partial(forward, i + 1, q)
        for h in range(PIECES):
            steps[f"bw{h}"] = on_p, functools.partial(back_weight, i - 3, h)
            steps[f"bp{h}"] = on_c, functools.partial(back_pooled, c, h)
        for f in (0, 1):
            steps[f"zf{f}"] = on_b, functools.partial(z_final, b, f)
            steps[f"xf{f}"] = on_b, functools.partial(x_final, b, f)
            steps[f"zs{f}"] = on_a, functools.partial(z_sum, a, f)
            steps[f"gs{f}"] = on_b, functools.partial(gz_first, b, f)
            for h in range(3):
                steps[f"zr{h}{f}"] = on_a, functools.partial(zr_hop, a, h, f)
                steps[f"xr{h}{f}"] = on_a, functools.partial(xr_hop, a, h, f)
                steps[f"gx{h}{f}"] = on_b, functools.partial(gather_arrive, gx_copy, b, h, True, f)
                steps[f"gz{h}{f}"] = on_c, functools.partial(gather_arrive, gz_copy, c, h, False, f)
        for name in ORDER:
            pl.when(steps[name][0])(steps[name][1])

        for s in (0, 1):
            @pl.when(i == 4 + s)
            def _():
                x_load(1, s).wait()
                prepare(1, s)
                if s:
                    xp_copy(1).start()

        return carry

    lax.fori_loop(0, n_units, tick, 0)

    last, pairs = n_units - 1, dm.towers * dm.subs
    ends = {
        "em": lambda: emit(last),
        "hd": lambda: gathered(last - 1),
        "gd": lambda: gathered(last),
        "ss": sums_send,
    }
    for q in range(PIECES):
        ends[f"bv{q}"] = functools.partial(back_weight, last - 2, q)
        ends[f"bw{q}"] = functools.partial(back_weight, last - 1, q)
        ends[f"bx{q}"] = functools.partial(back_weight, last, q)
        ends[f"hp{q}"] = functools.partial(back_pooled, last - 1, q)
        ends[f"bp{q}"] = functools.partial(back_pooled, last, q)
    for f in (0, 1):
        ends[f"zf{f}"] = functools.partial(z_final, last, f)
        ends[f"xf{f}"] = functools.partial(x_final, last, f)
        ends[f"gs{f}"] = functools.partial(gz_first, last, f)
        for h in range(3):
            ends[f"gx{h}{f}"] = functools.partial(gather_arrive, gx_copy, last, h, True, f)
            ends[f"gz{h}{f}"] = functools.partial(gather_arrive, gz_copy, last, h, False, f)
            ends[f"hz{h}{f}"] = functools.partial(gather_arrive, gz_copy, last - 1, h, False, f)
    for name in DRAIN:
        ends[name]()

    for k in (1, 2, 3):
        sum_copy(k).wait_recv()
    total = sum_s[bi] + sum_r[0] + sum_r[1] + sum_r[2]
    out_b[...] = total[0:2]
    for i in (0, 1):
        out_sg[i] = total[2 + 2 * i : 4 + 2 * i]
        out_sn[i] = st[i, :, pl.ds(al(bi * BLK), BLK)] - step_ref[0] * total[2 + 2 * i : 4 + 2 * i]
    for q in range(PIECES):
        for e in (0, 1):
            own_copy(pairs - 2, q, e).wait()
        for copy in last_copies(q):
            copy.wait()
    pg_copy(1, 1).wait()
    for i in (0, 1):
        s_copy(last - 1, i).wait()
        s_copy(last, i).wait()
    for t in range(dm.towers):
        xp_copy(t).wait_send()
    for k in (1, 2, 3):
        sum_copy(k).wait_send()
    for e in (0, 1):
        c_copy(last, e).wait_send()
    for o in range(NZ):
        x1_copy(last, o).wait_send()
    for f in (0, 1):
        for o in range(NZ):
            x5_copy(last, o, x, f).wait_send()
        z2_copy(last, f).wait_send()
        z4_copy(last, f).wait_send()
        for d in (0, 1):
            for h in range(3):
                @pl.when(far(d) <= h)
                def _():
                    xr_copy(last, d, h, f).wait_send()
                    zr_copy(last, d, h, f).wait_send()

                @pl.when((far(d) >= h) & (far(d) <= 2))
                def _():
                    gx_copy(last, d, h, f).wait_send()
                    gz_copy(last, d, h, f).wait_send()


def carry_out(*refs):
    count = len(refs) // 2
    for src, dst in zip(refs[:count], refs[count:]):
        dst[...] = src[...]


def settle(dm, _, mine, arrived, out, total, heard, sems):
    u, step = dm.subs - 1, dm.third
    inward, outward = [], []
    for q in range(PIECES):
        k = pl.ds(q * step, step)
        inward.append(
            (
                pltpu.make_async_copy(mine.at[k], total.at[k], sems.at[q, 0]),
                pltpu.make_async_copy(arrived.at[k], heard.at[k], sems.at[q, 1]),
            )
        )
        outward.append(
            [
                pltpu.make_async_copy(
                    total.at[k, pl.ds(e * BLK, BLK)],
                    out.at[dm.towers - 1, k, pl.ds(e * dm.own + u * BLK, BLK)],
                    sems.at[q, 2 + e],
                )
                for e in (0, 1)
            ]
        )
    for copies in inward:
        for copy in copies:
            copy.start()
    for q in range(PIECES):
        for copy in inward[q]:
            copy.wait()
        k = pl.ds(q * step, step)
        total[k] += heard[k].astype(F32)
        for copy in outward[q]:
            copy.start()
    for copies in outward:
        for copy in copies:
            copy.wait()


def fused(pooled, weight, fc_bias, stitch, cotangent, valid_mask, image_group, step_rate):
    dm = Dims(pooled, weight, cotangent)
    towers, feats, images, own = dm.towers, dm.feats, dm.images, dm.own
    rows, rx, rz, cols = dm.rows, dm.rx, dm.rz, dm.cols
    dma = pltpu.SemaphoreType.DMA
    vm = pltpu.VMEM
    scratch = [
        vm((4, feats, cols), BF16),
        vm((towers, images, feats), BF16),
        vm((towers, feats, images), BF16),
        vm((towers, feats, images), BF16),
        vm((feats, BLK), F32),
        vm((1, images), F32),
        vm((2, 2, BLK, rows), BF16),
        vm((2, images, own), BF16),
        vm((2, rows, BLK), BF16),
        vm((2, 2, BLK, rows), BF16),
        vm((feats, images), F32),
        vm((2, rows, cols), F32),
        vm((2, images, cols), BF16),
        vm((2, images, cols // 2), BF16),
        vm((NZ, rx, BLK), BF16),
        vm((2, NZ, rx, BLK), BF16),
        vm((2, 3, rx, BLK), BF16),
        vm((2, 2, 3, rx, BLK), BF16),
        vm((2, 3, rz, NX * BLK), BF16),
        vm((2, 2, 3, rz, NX * BLK), BF16),
        vm((rz, BLK), F32),
        vm((rz, BLK), BF16),
        vm((2, rz, BLK), BF16),
        vm((2, feats, NX * BLK), F32),
        vm((feats, NX * BLK), F32),
        vm((feats, NX * BLK), BF16),
        vm((2, feats, NX * BLK), BF16),
        vm((images, own), F32),
        vm((max(rx, rz), BLK), F32),
        vm((feats, rows), BF16),
        vm((dm.subs, 6, 8, BLK), F32),
        vm((dm.subs, 8, BLK), F32),
        vm((3, 8, BLK), F32),
    ] + [
        dma(shape)
        for shape in (
            (4, NZ * NX), (2, 2), (NZ,), (2, NZ), (2, 3, 2), (2, 2, 3, 2), (2, 3, 2), (2, 2, 3, 2), (2,), (2, 2), (2,), (2, 2),
            (2, 3, 2), (2, 2, 3, 2), (2, 3, 2), (2, 2, 3, 2), (NZ, 2), (2, NZ, 2), (2,), (4, 2), (PIECES,), (2, PIECES), (3,), (3,),
            (2,), (2,), (2, PIECES, 2), (), (2, 2), (2, 2), (PIECES, 2),
        )
    ]
    anyspace = pl.BlockSpec(memory_space=pl.ANY)
    inside = pl.BlockSpec(memory_space=pltpu.VMEM)
    out_shape = [
        jax.ShapeDtypeStruct((2, own, images), BF16),
        jax.ShapeDtypeStruct((towers, feats, images), BF16),
        jax.ShapeDtypeStruct((towers, feats, images), F32),
        jax.ShapeDtypeStruct((2, BLK), F32),
        jax.ShapeDtypeStruct((2, 2, BLK), F32),
        jax.ShapeDtypeStruct((2, 2, BLK), F32),
    ]
    out_specs = [anyspace] * 3 + [inside] * 3
    block = (feats, NX * BLK)
    *results, mine, theirs = pl.pallas_call(
        functools.partial(kernel, dm),
        name="stitch_fc6",
        out_shape=out_shape + [jax.ShapeDtypeStruct(block, F32), jax.ShapeDtypeStruct(block, BF16)],
        in_specs=[pl.BlockSpec(memory_space=pltpu.SMEM)] + [anyspace] * 3 + [inside] * 4,
        out_specs=out_specs + [anyspace] * 2,
        scratch_shapes=scratch,
        compiler_params=pltpu.CompilerParams(collective_id=1, has_side_effects=True, vmem_limit_bytes=61 * 2**20),
        cost_estimate=pl.CostEstimate(
            flops=6 * towers * feats * images * dm.chans, bytes_accessed=60 * 2**20, transcendentals=towers * images * own
        ),
    )(
        step_rate, weight, pooled, cotangent, fc_bias, stitch,
        valid_mask.reshape(feats // BLK, BLK), image_group.reshape(images // BLK, BLK),
    )
    arrived = lax.ppermute(theirs, "batch", [(0, 2), (1, 3), (2, 0), (3, 1)])

    def cut(shape):
        if len(shape.shape) == 3 and shape.shape[1] % (CUTS * 16) == 0:
            return pl.BlockSpec((shape.shape[0], shape.shape[1] // CUTS, shape.shape[2]), lambda c: (0, c, 0))
        return pl.BlockSpec(shape.shape, lambda c: (0,) * len(shape.shape))

    blocks = [cut(shape) for shape in out_shape]
    results = pl.pallas_call(
        carry_out,
        name="carry_out",
        grid=(CUTS,),
        out_shape=out_shape,
        in_specs=blocks,
        out_specs=blocks,
        compiler_params=pltpu.CompilerParams(vmem_limit_bytes=60 * 2**20),
        cost_estimate=pl.CostEstimate(flops=0, bytes_accessed=32 * 2**20, transcendentals=0),
    )(*results)
    weight_grad = pl.pallas_call(
        functools.partial(settle, dm),
        name="settle",
        out_shape=out_shape[2],
        in_specs=[anyspace] * 3,
        out_specs=anyspace,
        scratch_shapes=[vm(block, F32), vm(block, BF16), dma((PIECES, 4))],
        input_output_aliases={0: 0},
        compiler_params=pltpu.CompilerParams(vmem_limit_bytes=6 * 2**20),
    )(results[2], mine, arrived)
    return *results[:2], weight_grad, *results[3:]


def gelu_local(values):
    return jax.nn.gelu(values, approximate=True)


def plain(pooled, weight, fc_bias, stitch, cotangent, valid_mask, image_group, step_rate):
    highest = lax.Precision.HIGHEST
    factor = 1.0 - image_group[None, :].astype(F32) * (1.0 - valid_mask[:, None].astype(F32))
    masked = pooled * factor.astype(BF16)[None]
    owned = weight.shape[2] // lax.axis_size("wide")
    summed = lax.psum_scatter(
        jnp.einsum("tkc,tkb->ctb", weight, masked, preferred_element_type=F32), "wide", scatter_dimension=0, tiled=True
    )
    pre_act = summed + jnp.transpose(fc_bias)[:, :, None]
    hidden, gelu_back = jax.vjp(gelu_local, pre_act)
    stitched = jnp.einsum("ijc,cjb->icb", stitch, hidden, precision=highest)
    upstream = cotangent.astype(F32)
    stitch_part = jnp.einsum("icb,cjb->ijc", upstream, hidden, precision=highest)
    hidden_grad = jnp.einsum("ijc,icb->cjb", stitch, upstream, precision=highest)
    pre_grad = gelu_back(hidden_grad)[0]
    bias_part = jnp.transpose(jnp.sum(pre_grad, axis=2))
    pre_low = pre_grad.astype(BF16)
    bias_grad = lax.psum_scatter(bias_part, "batch", scatter_dimension=1, tiled=True)
    stitch_grad = lax.psum_scatter(stitch_part, "batch", scatter_dimension=2, tiled=True)
    portion = lax.all_gather(pre_low, "wide", axis=0, tiled=True)
    input_sum = jnp.einsum("tkc,ctb->tkb", weight, portion, preferred_element_type=F32)
    block_grad = jnp.einsum("tkb,ctb->tkc", masked, portion, preferred_element_type=F32)
    pooled_grad = (input_sum * factor[None]).astype(BF16)
    weight_grad = lax.psum_scatter(block_grad, "batch", scatter_dimension=2, tiled=True)
    share = owned // lax.axis_size("batch")
    stitch_mine = lax.dynamic_slice_in_dim(stitch, lax.axis_index("batch") * share, share, 2)
    stitch_new = stitch_mine - step_rate[0] * stitch_grad
    return stitched.astype(BF16), pooled_grad, weight_grad, bias_grad, stitch_grad, stitch_new


def fits(mesh, pooled, weight, cotangent):
    return (
        (mesh.shape["wide"], mesh.shape["batch"]) == (NZ * NX, 4)
        and pooled.shape[0] == 2
        and cotangent.shape[1] == 4 * BLK
        and weight.shape[2] == NZ * NX * cotangent.shape[1]
        and pooled.shape[2] % 512 == 0
        and pooled.shape[1] % (16 * PIECES) == 0
        and pooled.shape[1] % BLK == 0
    )


def solution(mesh):
    def body(pooled, weight, fc_bias, stitch, cotangent, *rest):
        form = fused if fits(mesh, pooled, weight, cotangent) else plain
        return form(pooled, weight, fc_bias, stitch, cotangent, *rest)

    return jax.shard_map(
        body,
        mesh=mesh,
        in_specs=(
            P(None, "wide", "batch"),
            P(None, "wide", None),
            P(None, "wide"),
            P(None, None, "wide"),
            P(None, "wide", "batch"),
            P("wide"),
            P("batch"),
            P(),
        ),
        out_specs=(
            P(None, "wide", "batch"),
            P(None, "wide", "batch"),
            P(None, "wide", "batch"),
            P(None, ("wide", "batch")),
            P(None, None, ("wide", "batch")),
            P(None, None, ("wide", "batch")),
        ),
        check_vma=False,
    )
```

```python
import functools
import math

import jax
import jax.numpy as jnp
from jax import lax
from jax.experimental import pallas as pl
from jax.experimental.pallas import tpu as pltpu
from jax.sharding import PartitionSpec as P

MESH = pl.DeviceIdType.MESH
BLK = 128
NZ, NX = 4, 2
F32, BF16 = jnp.float32, jnp.bfloat16
NT = (((1,), (1,)), ((), ()))
ROOT = math.sqrt(2.0 / math.pi)
CUBE = 0.044715
PIECES = 3
CUTS = 4
TAILX = 30
DRAIN = (
    "zf0", "zf1", "sz0", "sz1", "xf0", "xf1", "sx0", "sx1", "bv0", "hz00", "hz01", "bv1", "gs0", "gx00", "gs1", "gx01",
    "hz10", "hz11", "bv2", "em", "gz00", "gx10", "gz01", "gx11", "hz20", "hz21", "hd", "gz10", "gx20", "gz11", "gx21",
    "hp0", "hp1", "hp2", "ss", "bw0", "bw1", "bw2", "gz20", "gz21", "gd", "bp0", "bp1", "bp2", "ya0", "bx0", "ya1",
    "bx1", "bx2", "ya2",
)
ORDER = (
    "zr00", "ws", "zf0", "gz00", "bw0", "x10", "xf0", "ww", "p0", "zr01", "zf1", "gz01", "bw1", "xf1", "f0",
    "zr10", "gz10", "f1", "x11", "xr00", "gx00", "em", "zr11", "gz11", "bw2", "xr01", "gx01", "f2",
    "zr20", "gz20", "ct", "az", "x12", "xr10", "gx10", "f3", "zr21", "gz21", "gd", "bp0", "xr11", "gx11",
    "zs0", "gs0", "x13", "xr20", "gx20", "bp1", "zs1", "gs1", "bp2", "xr21", "gx21",
)


class Dims:
    def __init__(self, pooled, weight, cotangent):
        self.towers, self.feats, self.images = pooled.shape
        self.chans = weight.shape[2]
        self.own = cotangent.shape[1]
        self.subs = self.own // BLK
        self.parts = 2
        self.rows = self.images // self.parts
        self.rx = (self.rows * 19 // 32) // 16 * 16
        self.rz = self.rows - self.rx
        self.units = self.towers * self.subs * self.parts
        self.cols = NZ * NX * BLK
        self.third = self.feats // PIECES


def chunks(count, size=64):
    return [(r, min(size, count - r)) for r in range(0, count, size)]


def kernel(
    dm,
    step_ref, w_hbm, p_hbm, c_hbm, bias, st, valid, group,
    s_hbm, pg_hbm, wg_hbm, out_b, out_sg, out_sn, mine_hbm, theirs_hbm,
    wb, xt, xb, xpb, hole, small_img, craw, cot, stmp, sbuf, acc, fwd, gat, gatp,
    x1_s, x1_r, xr_s, xr_r, zr_s, zr_r, zown, z2_s, z2_r,
    own, tacc, y_s, y_r, hid0, htmp, pgb, sacc, sum_s, sum_r,
    m_w, m_ld, m_x1s, m_x1r, m_xrs, m_xrr, m_zrs, m_zrr, m_z2s, m_z2r, m_z4s, m_z4r,
    m_gxs, m_gxr, m_gzs, m_gzr, m_x5s, m_x5r, m_cs, m_cr, m_ys, m_yr, m_ss, m_sr, m_xps, m_xpr, m_own, m_pg,
    m_cot, m_out, m_last,
):
    n_units, rows, rx, rz = dm.units, dm.rows, dm.rx, dm.rz
    mid_x, mid_z = rx // 32 * 16, rz // 32 * 16
    cuts_x = (0, mid_x), (mid_x, rx - mid_x)
    cuts_z = (0, mid_z), (mid_z, rz - mid_z)
    late = rows * TAILX // 32 // 32 * 32
    rest = (rows - late) // 32 * 16
    tail_x = (0, late // 2), (late // 2, late // 2)
    tail_z = (late - rx, rest), (late - rx + rest, rows - late - rest)
    wi, bi = lax.axis_index("wide"), lax.axis_index("batch")
    z, x = wi // NX, wi % NX
    y, core = bi // 2, bi % 2
    x_dev = (z * NX + 1 - x, bi)
    c_dev = (wi, y * 2 + 1 - core)
    y_dev = (wi, (1 - y) * 2 + core)

    def z_dev(d):
        return (wi + NX, bi) if d == 0 else (wi - NX, bi)

    def far(d):
        return z if d == 0 else NZ - 1 - z

    def rc(src, dst, ss, rs, dev):
        return pltpu.make_async_remote_copy(src, dst, ss, rs, device_id=dev, device_id_type=MESH)

    def al(v, k=BLK):
        return v if isinstance(v, int) else pl.multiple_of(v, k)

    def tower(n):
        return n // (dm.subs * dm.parts)

    def sub(n):
        return (n // dm.parts) % dm.subs

    def part(n):
        return n % dm.parts

    def gpair(n):
        return (n // dm.parts) % 2

    def col(o, xx):
        return al((o * NX + xx) * BLK)

    def w_load(p, w):
        t, u = p // dm.subs, p % dm.subs
        return pltpu.make_async_copy(
            w_hbm.at[t, :, pl.ds(al(w * dm.own + u * BLK), BLK)], wb.at[p % 4, :, pl.ds(w * BLK, BLK)], m_w.at[p % 4, w]
        )

    def x_load(t, s):
        lanes = pl.ds(s * rows, rows)
        return pltpu.make_async_copy(p_hbm.at[t, :, lanes], xb.at[t, :, lanes], m_ld.at[t, s])

    def cot_load(n, i):
        return pltpu.make_async_copy(
            c_hbm.at[i, pl.ds(al(sub(n) * BLK), BLK), pl.ds(al(part(n) * rows), rows)], craw.at[n % 2, i], m_cot.at[n % 2, i]
        )

    def s_copy(n, i):
        return pltpu.make_async_copy(
            sbuf.at[n % 2, i], s_hbm.at[i, pl.ds(al(sub(n) * BLK), BLK), pl.ds(al(part(n) * rows), rows)], m_out.at[n % 2, i]
        )

    def xp_copy(t):
        return rc(xb.at[t], xpb.at[t], m_xps.at[t], m_xpr.at[t], c_dev)

    def x1_copy(n, o):
        return rc(x1_s.at[o], x1_r.at[n % 2, o], m_x1s.at[o], m_x1r.at[n % 2, o], x_dev)

    def xr_copy(n, d, h, f):
        cut = pl.ds(*cuts_x[f])
        return rc(xr_s.at[d, h, cut], xr_r.at[n % 2, d, h, cut], m_xrs.at[d, h, f], m_xrr.at[n % 2, d, h, f], z_dev(d))

    def zr_copy(n, d, h, f):
        cut = pl.ds(*cuts_z[f])
        return rc(zr_s.at[d, h, cut], zr_r.at[n % 2, d, h, cut], m_zrs.at[d, h, f], m_zrr.at[n % 2, d, h, f], z_dev(d))

    def z2_copy(n, f):
        cut = pl.ds(*cuts_z[f])
        return rc(z2_s.at[cut], z2_r.at[n % 2, cut], m_z2s.at[f], m_z2r.at[n % 2, f], x_dev)

    def final(n):
        return isinstance(n, int) and n == n_units - 1

    def g_x(n, o, xx, f):
        start, size = tail_x[f] if final(n) else cuts_x[f]
        return gat.at[gpair(n), pl.ds(al(part(n) * rows + start, 16), size), pl.ds(col(o, xx), BLK)]

    def g_z(n, o, xx, width, f):
        start, size = tail_z[f] if final(n) else cuts_z[f]
        return gat.at[gpair(n), pl.ds(al(part(n) * rows + rx + start, 16), size), pl.ds(col(o, xx), width)]

    def z4_copy(n, f):
        blk = g_z(n, z, x, BLK, f)
        return rc(blk, blk, m_z4s.at[f], m_z4r.at[n % 2, f], x_dev)

    def gx_copy(n, d, h, f):
        blk = g_x(n, z - h if d == 0 else z + h, x, f)
        return rc(blk, blk, m_gxs.at[d, h, f], m_gxr.at[n % 2, d, h, f], z_dev(d))

    def gz_copy(n, d, h, f):
        blk = g_z(n, z - h if d == 0 else z + h, 0, NX * BLK, f)
        return rc(blk, blk, m_gzs.at[d, h, f], m_gzr.at[n % 2, d, h, f], z_dev(d))

    def x5_copy(n, o, xx, f):
        blk = g_x(n, o, xx, f)
        return rc(blk, blk, m_x5s.at[o, f], m_x5r.at[n % 2, o, f], x_dev)

    def c_copy(n, e):
        r = pl.ds(al(part(n) * rows, 16), rows)
        return rc(
            gat.at[gpair(n), r, pl.ds(col(2 * e + 1 - core, 0), NX * BLK)],
            gatp.at[gpair(n), r, pl.ds(e * NX * BLK, NX * BLK)],
            m_cs.at[e], m_cr.at[n % 4, e], c_dev,
        )

    def y_copy(p, q):
        k = pl.ds(q * dm.third, dm.third)
        return rc(y_s.at[p % 2, k], y_r.at[p % 2, k], m_ys.at[p % 2, q], m_yr.at[p % 2, q], y_dev)

    def own_copy(p, q, e):
        t, u = p // dm.subs, p % dm.subs
        k = pl.ds(q * dm.third, dm.third)
        return pltpu.make_async_copy(
            own.at[p % 2, k, pl.ds(e * BLK, BLK)],
            wg_hbm.at[t, k, pl.ds(al(e * dm.own + u * BLK), BLK)],
            m_own.at[p % 2, q, e],
        )

    def last_copies(q):
        slot = (dm.towers * dm.subs - 1) % 2
        k = pl.ds(q * dm.third, dm.third)
        return (
            pltpu.make_async_copy(y_s.at[slot, k], theirs_hbm.at[k], m_last.at[q, 0]),
            pltpu.make_async_copy(own.at[slot, k], mine_hbm.at[k], m_last.at[q, 1]),
        )

    def pg_copy(t, s):
        return pltpu.make_async_copy(pgb, pg_hbm.at[t, :, pl.ds(al(s * rows), rows)], m_pg)

    def sum_copy(k):
        to = lax.rem(bi + k, 4)
        return rc(sum_s.at[to], sum_r.at[k - 1], m_ss.at[k - 1], m_sr.at[k - 1], (wi, to))

    def factor(k, s):
        wide_hole = jnp.concatenate([hole[pl.ds(al(k * BLK), BLK)]] * (rows // BLK), axis=1)
        return 1.0 - small_img[:, pl.ds(al(s * rows), rows)] * wide_hole

    def prepare(t, s):
        @pl.loop(0, dm.feats // BLK)
        def _(k):
            at, lanes = pl.ds(al(k * BLK), BLK), pl.ds(s * rows, rows)
            masked = (xb[t, at, lanes].astype(F32) * factor(k, s)).astype(BF16)
            xb[t, at, lanes] = masked
            xt[t, pl.ds(s * rows, rows), at] = masked.T

    def prepare_cot(n):
        for i in (0, 1):
            cot_load(n, i).wait()
            cot[i, pl.ds(al(part(n) * rows), rows), pl.ds(al(sub(n) * BLK), BLK)] = craw[n % 2, i].T

    def forward(n, k):
        fwd[n % 2, :, pl.ds(k * 256, 256)] = jnp.dot(
            xt[tower(n), pl.ds(al(part(n) * rows, 16), rows), :],
            wb[(n // dm.parts) % 4, :, pl.ds(k * 256, 256)],
            preferred_element_type=F32,
        )

    def x1_send(n, q):
        o = (
            jnp.where(z < 2, 3, 0),
            jnp.where(z < 2, 2, 1),
            jnp.where(z < 2, 1 - z, 5 - z),
            z,
        )[q]

        @pl.when(n >= 1)
        def _():
            x1_copy(n, o).wait_send()

        for r, m in chunks(rx):
            x1_s[o, r : r + m] = fwd[n % 2, r : r + m, pl.ds(col(o, 1 - x), BLK)].astype(BF16)
        x1_copy(n, o).start()

    def xr_hop(n, h, f):
        start, size = cuts_x[f]
        for d in (0, 1):
            o = 3 - h + z if d == 0 else h - 3 + z

            @pl.when(far(d) <= h)
            def _():
                if f == 0:
                    x1_copy(n, o).wait_recv()
                if h:
                    @pl.when(far(d) >= 1)
                    def _():
                        xr_copy(n, d, h - 1, f).wait_recv()

                @pl.when(n >= 1)
                def _():
                    xr_copy(n, d, h, f).wait_send()

                for r, m in chunks(size):
                    r += start
                    v = fwd[n % 2, r : r + m, pl.ds(col(o, x), BLK)] + x1_r[n % 2, o, r : r + m].astype(F32)
                    if h:
                        v = v + xr_r[n % 2, d, h - 1, r : r + m].astype(F32)
                    xr_s[d, h, r : r + m] = v.astype(BF16)
                xr_copy(n, d, h, f).start()

    def zr_hop(n, h, f):
        start, size = cuts_z[f]
        for d in (0, 1):
            o = 3 - h + z if d == 0 else h - 3 + z

            @pl.when(far(d) <= h)
            def _():
                if h:
                    @pl.when(far(d) >= 1)
                    def _():
                        zr_copy(n, d, h - 1, f).wait_recv()

                @pl.when(n >= 1)
                def _():
                    zr_copy(n, d, h, f).wait_send()

                for r, m in chunks(size):
                    r += start
                    v = fwd[n % 2, rx + r : rx + r + m, pl.ds(col(o, 0), NX * BLK)]
                    if h:
                        v = v + zr_r[n % 2, d, h - 1, r : r + m].astype(F32)
                    zr_s[d, h, r : r + m] = v.astype(BF16)
                zr_copy(n, d, h, f).start()

    def z_sum(n, f):
        for d in (0, 1):
            @pl.when(far(d) >= 1)
            def _():
                zr_copy(n, d, 2, f).wait_recv()

        @pl.when(n >= 1)
        def _():
            z2_copy(n, f).wait_send()

        start, size = cuts_z[f]
        for xx in (1 - x, x):
            for r, m in chunks(size):
                r += start
                lanes = pl.ds(al(xx * BLK), BLK)
                v = (
                    fwd[n % 2, rx + r : rx + r + m, pl.ds(col(z, xx), BLK)]
                    + zr_r[n % 2, 0, 2, r : r + m, lanes].astype(F32)
                    + zr_r[n % 2, 1, 2, r : r + m, lanes].astype(F32)
                )
                if xx is x:
                    zown[r : r + m] = v
                else:
                    z2_s[r : r + m] = v.astype(BF16)
            if xx is not x:
                z2_copy(n, f).start()

    def finish(n, row0, count, total):
        t, u = tower(n), sub(n)
        lanes = pl.ds(al(u * BLK), BLK)
        base = part(n) * rows + row0
        b_row = jnp.where(t == 0, bias[0:1, lanes], bias[1:2, lanes])
        from0 = jnp.where(t == 0, st[0, 0:1, lanes], st[0, 1:2, lanes])
        from1 = jnp.where(t == 0, st[1, 0:1, lanes], st[1, 1:2, lanes])
        for r, m in chunks(count):
            at = pl.ds(al(base + r, 16), m)
            v = total(r, m) + b_row
            sq = v * v
            th = jnp.tanh(ROOT * v * (1.0 + CUBE * sq))
            half = 0.5 * (1.0 + th)
            htmp[r : r + m] = v * half
            slope = half + 0.5 * v * (1.0 - th * th) * (ROOT * (1.0 + 3.0 * CUBE * sq))
            up0, up1 = cot[0, at, lanes].astype(F32), cot[1, at, lanes].astype(F32)
            grad = (from0 * up0 + from1 * up1) * slope
            sacc[u, t] += jnp.sum(grad.reshape(m // 8, 8, BLK), axis=0)
            gat[gpair(n), at, pl.ds(col(z, x), BLK)] = grad.astype(BF16)

    def mix(n, row0, count):
        t, u = tower(n), sub(n)
        lanes = pl.ds(al(u * BLK), BLK)
        base = part(n) * rows + row0

        @pl.when(t == 0)
        def _():
            for r, m in chunks(count):
                hid0[pl.ds(al(base + r, 16), m), lanes] = htmp[r : r + m]

        @pl.when(t == 1)
        def _():
            for r, m in chunks(count):
                at = pl.ds(al(base + r, 16), m)
                h = hid0[at, lanes], htmp[r : r + m]
                for i in (0, 1):
                    up = cot[i, at, lanes].astype(F32)
                    stmp[i, row0 + r : row0 + r + m] = (st[i, 0:1, lanes] * h[0] + st[i, 1:2, lanes] * h[1]).astype(BF16)
                    for j in (0, 1):
                        sacc[u, 2 + 2 * i + j] += jnp.sum((up * h[j]).reshape(m // 8, 8, BLK), axis=0)

    def emit(n):
        @pl.when(tower(n) == 1)
        def _():
            for i in (0, 1):
                @pl.when(n >= n_units // 2 + 2)
                def _():
                    s_copy(n, i).wait()

                sbuf[n % 2, i] = stmp[i].T
                s_copy(n, i).start()

    def z_final(n, f):
        z2_copy(n, f).wait_recv()
        start, size = cuts_z[f]

        def total(r, m):
            r += start
            return zown[r : r + m] + z2_r[n % 2, r : r + m].astype(F32)

        finish(n, rx + start, size, total)
        if not final(n):
            z4_send(n, f)
        mix(n, rx + start, size)

    def z4_send(n, f):
        @pl.when(n >= 1)
        def _():
            z4_copy(n - 1, f).wait_send()

        z4_copy(n, f).start()

    def gx_send(n, f):
        for d in (0, 1):
            gather_hop(gx_copy, n, d, 0, f)
        x5_send(n, z, f)

    def x_final(n, f):
        if f == 0:
            x1_copy(n, z).wait_recv()
        for d in (0, 1):
            @pl.when(far(d) >= 1)
            def _():
                xr_copy(n, d, 2, f).wait_recv()

        start, size = cuts_x[f]

        def total(r, m):
            r += start
            return (
                fwd[n % 2, r : r + m, pl.ds(col(z, x), BLK)]
                + x1_r[n % 2, z, r : r + m].astype(F32)
                + xr_r[n % 2, 0, 2, r : r + m].astype(F32)
                + xr_r[n % 2, 1, 2, r : r + m].astype(F32)
            )

        finish(n, start, size, total)
        if not final(n):
            gx_send(n, f)
        mix(n, start, size)

    def gather_hop(copy, n, d, h, f):
        @pl.when((far(d) >= h) & (far(d) <= 2))
        def _():
            @pl.when(n >= 1)
            def _():
                copy(n - 1, d, h, f).wait_send()

            copy(n, d, h, f).start()

    def x5_send(n, o, f):
        @pl.when(n >= 1)
        def _():
            x5_copy(n - 1, o, x, f).wait_send()

        x5_copy(n, o, x, f).start()

    def gz_first(n, f):
        z4_copy(n, f).wait_recv()
        for d in (0, 1):
            gather_hop(gz_copy, n, d, 0, f)

    def gather_arrive(copy, n, h, forward_x, f):
        for d in (0, 1):
            @pl.when(far(d) >= h + 1)
            def _():
                copy(n, d, h, f).wait_recv()
                if h < 2:
                    gather_hop(copy, n, d, h + 1, f)
                if forward_x:
                    x5_send(n, z - 1 - h if d == 0 else z + 1 + h, f)

    def gathered(n):
        for o in range(NZ):
            for f in (0, 1):
                x5_copy(n, o, 1 - x, f).wait_recv()
        for e in (0, 1):
            @pl.when(n >= 1)
            def _():
                c_copy(n, e).wait_send()

            c_copy(n, e).start()

    def back_pooled(n, q):
        t, s = tower(n), part(n)
        lanes = pl.ds(al(s * rows), rows)
        k = pl.ds(q * dm.third, dm.third)
        acc[k, lanes] += lax.dot_general(
            wb[(n // dm.parts) % 4, k, :],
            gat[gpair(n), pl.ds(al(s * rows, 16), rows), :],
            NT,
            preferred_element_type=F32,
        )
        if q < PIECES - 1:
            return

        @pl.when(sub(n) == dm.subs - 1)
        def _():
            @pl.when((t > 0) | (s > 0))
            def _():
                pg_copy(t, s).wait()

            @pl.loop(0, dm.feats // BLK)
            def _(k):
                at = pl.ds(al(k * BLK), BLK)
                pgb[at] = (acc[at, lanes] * factor(k, s)).astype(BF16)
                acc[at, lanes] = jnp.zeros((BLK, rows), F32)

            pg_copy(t, s).start()

    def y_arrive(p, q):
        k = pl.ds(q * dm.third, dm.third)
        y_copy(p, q).wait_recv()
        for r, m in chunks(dm.third):
            at = pl.ds(q * dm.third + r, m)
            own[p % 2, at] += y_r[p % 2, at].astype(F32)
        for e in (0, 1):
            own_copy(p, q, e).start()

    def back_weight(n, q):
        t, s, p = tower(n), part(n), n // dm.parts
        is_last = final(n)
        k, imgs = pl.ds(q * dm.third, dm.third), pl.ds(al(part(n) * rows), rows)
        if q == 0:
            for e in (0, 1):
                c_copy(n, e).wait_recv()

            @pl.when((s == 0) & (p % dm.subs == 0))
            def _():
                xp_copy(t).wait_recv()

        def grads(yy):
            lanes = pl.ds(col(2 * yy + core, 0), NX * BLK)
            return jnp.dot(xb[t, k, imgs], gat[p % 2, imgs, lanes], preferred_element_type=F32) + jnp.dot(
                xpb[t, k, imgs], gatp[p % 2, imgs, pl.ds(al(yy * NX * BLK), NX * BLK)], preferred_element_type=F32
            )

        @pl.when(s == 0)
        def _():
            if not isinstance(n, int):
                @pl.when(p >= 1)
                def _():
                    y_arrive(p - 1, q)

            @pl.when(p >= 2)
            def _():
                for e in (0, 1):
                    own_copy(p, q, e).wait()

            tacc[k, :] = grads(1 - y)
            own[p % 2, k, :] = grads(y)

        @pl.when(s == 1)
        def _():
            @pl.when(p >= 2)
            def _():
                y_copy(p - 2, q).wait_send()

            y_s[p % 2, k, :] = (tacc[k, :] + grads(1 - y)).astype(BF16)
            if not is_last:
                y_copy(p, q).start()
            own[p % 2, k, :] += grads(y)
            if is_last:
                for copy in last_copies(q):
                    copy.start()

    def sums_send():
        for u in range(dm.subs):
            for j in range(6):
                sum_s[u, j : j + 1] = jnp.sum(sacc[u, j], axis=0, keepdims=True)
            sum_s[u, 6:8] = jnp.zeros((2, BLK), F32)
        for k in (1, 2, 3):
            sum_copy(k).start()

    x_load(0, 0).start()
    for w in range(NZ * NX):
        w_load(0, w).start()
    barrier = pltpu.get_barrier_semaphore()
    peers = [x_dev] + [(wi, lax.rem(bi + k, 4)) for k in (1, 2, 3)]
    for dev in peers:
        pl.semaphore_signal(barrier, inc=1, device_id=dev, device_id_type=MESH)
    for d in (0, 1):
        @pl.when(far(d) <= 2)
        def _():
            pl.semaphore_signal(barrier, inc=1, device_id=z_dev(d), device_id_type=MESH)

    small_img[...] = jnp.concatenate([group[j : j + 1] for j in range(dm.images // BLK)], axis=1).astype(F32)
    for j in range(dm.feats // BLK):
        gap = 1.0 - valid[j : j + 1].astype(F32)
        hole[j * BLK : (j + 1) * BLK] = jnp.broadcast_to(gap, (BLK, BLK)).T
    x_load(0, 0).wait()
    prepare(0, 0)

    for d in (0, 1):
        @pl.when(far(d) == 0)
        def _():
            for s in (0, 1):
                for h in range(3):
                    xr_r[s, d, h] = jnp.zeros((rx, BLK), BF16)
                    zr_r[s, d, h] = jnp.zeros((rz, NX * BLK), BF16)

    pl.semaphore_wait(barrier, jnp.where((z == 0) | (z == NZ - 1), len(peers) + 1, len(peers) + 2))
    for w in range(NZ * NX):
        w_load(0, w).wait()
    x_load(0, 1).start()
    for i in (0, 1):
        cot_load(0, i).start()
    for w in range(NZ * NX):
        w_load(1, w).start()
    for s in (0, 1):
        x_load(1, s).start()

    for k in range(4):
        forward(0, k)
    sacc[...] = jnp.zeros_like(sacc)

    def tick(i, carry):
        a, b, c = i, i - 1, i - 2
        on_a, on_b, on_c = i >= 0, i >= 1, i >= 2
        on_f = i + 1 < n_units
        on_p = i >= 3

        def clear():
            @pl.loop(0, dm.feats // 32)
            def _(k):
                acc[pl.ds(al(k * 32, 32), 32)] = jnp.zeros((32, dm.images), F32)

        def w_start():
            for w in range(NZ * NX):
                w_load(i // 2 + 2, w).start()

        def w_wait():
            for w in range(NZ * NX):
                w_load((i + 1) // 2, w).wait()

        def first_images():
            x_load(0, 1).wait()
            prepare(0, 1)
            xp_copy(0).start()

        def cot_next():
            prepare_cot(i)

            @pl.when(i + 1 < n_units // 2)
            def _():
                for j in (0, 1):
                    cot_load(i + 1, j).start()

        steps = {
            "ws": ((i % 2 == 0) & (i // 2 + 2 < dm.towers * dm.subs), w_start),
            "ww": (on_f & (i % 2 == 1), w_wait),
            "az": (i == 0, clear),
            "p0": (i == 0, first_images),
            "ct": (i < n_units // 2, cot_next),
            "em": (on_b, lambda: emit(b)),
            "gd": (on_c, lambda: gathered(c)),
        }
        for q in range(4):
            steps[f"x1{q}"] = on_a, functools.partial(x1_send, a, q)
            steps[f"f{q}"] = on_f, functools.partial(forward, i + 1, q)
        for h in range(PIECES):
            steps[f"bw{h}"] = on_p, functools.partial(back_weight, i - 3, h)
            steps[f"bp{h}"] = on_c, functools.partial(back_pooled, c, h)
        for f in (0, 1):
            steps[f"zf{f}"] = on_b, functools.partial(z_final, b, f)
            steps[f"xf{f}"] = on_b, functools.partial(x_final, b, f)
            steps[f"zs{f}"] = on_a, functools.partial(z_sum, a, f)
            steps[f"gs{f}"] = on_b, functools.partial(gz_first, b, f)
            for h in range(3):
                steps[f"zr{h}{f}"] = on_a, functools.partial(zr_hop, a, h, f)
                steps[f"xr{h}{f}"] = on_a, functools.partial(xr_hop, a, h, f)
                steps[f"gx{h}{f}"] = on_b, functools.partial(gather_arrive, gx_copy, b, h, True, f)
                steps[f"gz{h}{f}"] = on_c, functools.partial(gather_arrive, gz_copy, c, h, False, f)
        for name in ORDER:
            pl.when(steps[name][0])(steps[name][1])

        for s in (0, 1):
            @pl.when(i == 4 + s)
            def _():
                x_load(1, s).wait()
                prepare(1, s)
                if s:
                    xp_copy(1).start()

        return carry

    lax.fori_loop(0, n_units, tick, 0)

    last, pairs = n_units - 1, dm.towers * dm.subs
    ends = {
        "em": lambda: emit(last),
        "hd": lambda: gathered(last - 1),
        "gd": lambda: gathered(last),
        "ss": sums_send,
    }
    for q in range(PIECES):
        ends[f"ya{q}"] = functools.partial(y_arrive, pairs - 2, q)
        ends[f"bv{q}"] = functools.partial(back_weight, last - 2, q)
        ends[f"bw{q}"] = functools.partial(back_weight, last - 1, q)
        ends[f"bx{q}"] = functools.partial(back_weight, last, q)
        ends[f"hp{q}"] = functools.partial(back_pooled, last - 1, q)
        ends[f"bp{q}"] = functools.partial(back_pooled, last, q)
    for f in (0, 1):
        ends[f"zf{f}"] = functools.partial(z_final, last, f)
        ends[f"xf{f}"] = functools.partial(x_final, last, f)
        ends[f"sz{f}"] = functools.partial(z4_send, last, f)
        ends[f"sx{f}"] = functools.partial(gx_send, last, f)
        ends[f"gs{f}"] = functools.partial(gz_first, last, f)
        for h in range(3):
            ends[f"gx{h}{f}"] = functools.partial(gather_arrive, gx_copy, last, h, True, f)
            ends[f"gz{h}{f}"] = functools.partial(gather_arrive, gz_copy, last, h, False, f)
            ends[f"hz{h}{f}"] = functools.partial(gather_arrive, gz_copy, last - 1, h, False, f)
    for name in DRAIN:
        ends[name]()

    for k in (1, 2, 3):
        sum_copy(k).wait_recv()
    total = sum_s[bi] + sum_r[0] + sum_r[1] + sum_r[2]
    out_b[...] = total[0:2]
    for i in (0, 1):
        out_sg[i] = total[2 + 2 * i : 4 + 2 * i]
        out_sn[i] = st[i, :, pl.ds(al(bi * BLK), BLK)] - step_ref[0] * total[2 + 2 * i : 4 + 2 * i]
    for q in range(PIECES):
        for e in (0, 1):
            own_copy(pairs - 2, q, e).wait()
        for copy in last_copies(q):
            copy.wait()
        y_copy(pairs - 2, q).wait_send()
    pg_copy(1, 1).wait()
    for i in (0, 1):
        s_copy(last - 1, i).wait()
        s_copy(last, i).wait()
    for t in range(dm.towers):
        xp_copy(t).wait_send()
    for k in (1, 2, 3):
        sum_copy(k).wait_send()
    for e in (0, 1):
        c_copy(last, e).wait_send()
    for o in range(NZ):
        x1_copy(last, o).wait_send()
    for f in (0, 1):
        for o in range(NZ):
            x5_copy(last, o, x, f).wait_send()
        z2_copy(last, f).wait_send()
        z4_copy(last, f).wait_send()
        for d in (0, 1):
            for h in range(3):
                @pl.when(far(d) <= h)
                def _():
                    xr_copy(last, d, h, f).wait_send()
                    zr_copy(last, d, h, f).wait_send()

                @pl.when((far(d) >= h) & (far(d) <= 2))
                def _():
                    gx_copy(last, d, h, f).wait_send()
                    gz_copy(last, d, h, f).wait_send()


def carry_out(*refs):
    count = len(refs) // 2
    for src, dst in zip(refs[:count], refs[count:]):
        dst[...] = src[...]


def settle(dm, _, mine, arrived, out, total, sems):
    u, step = dm.subs - 1, dm.third
    copies = []
    for q in range(PIECES):
        k = pl.ds(q * step, step)
        total[k] = mine[k] + arrived[k].astype(F32)
        for e in (0, 1):
            copies.append(
                pltpu.make_async_copy(
                    total.at[k, pl.ds(e * BLK, BLK)],
                    out.at[dm.towers - 1, k, pl.ds(e * dm.own + u * BLK, BLK)],
                    sems.at[q, e],
                )
            )
            copies[-1].start()
    for copy in copies:
        copy.wait()


def fused(pooled, weight, fc_bias, stitch, cotangent, valid_mask, image_group, step_rate):
    dm = Dims(pooled, weight, cotangent)
    towers, feats, images, own = dm.towers, dm.feats, dm.images, dm.own
    rows, rx, rz, cols = dm.rows, dm.rx, dm.rz, dm.cols
    dma = pltpu.SemaphoreType.DMA
    vm = pltpu.VMEM
    scratch = [
        vm((4, feats, cols), BF16),
        vm((towers, images, feats), BF16),
        vm((towers, feats, images), BF16),
        vm((towers, feats, images), BF16),
        vm((feats, BLK), F32),
        vm((1, images), F32),
        vm((2, 2, BLK, rows), BF16),
        vm((2, images, own), BF16),
        vm((2, rows, BLK), BF16),
        vm((2, 2, BLK, rows), BF16),
        vm((feats, images), F32),
        vm((2, rows, cols), F32),
        vm((2, images, cols), BF16),
        vm((2, images, cols // 2), BF16),
        vm((NZ, rx, BLK), BF16),
        vm((2, NZ, rx, BLK), BF16),
        vm((2, 3, rx, BLK), BF16),
        vm((2, 2, 3, rx, BLK), BF16),
        vm((2, 3, rz, NX * BLK), BF16),
        vm((2, 2, 3, rz, NX * BLK), BF16),
        vm((rz, BLK), F32),
        vm((rz, BLK), BF16),
        vm((2, rz, BLK), BF16),
        vm((2, feats, NX * BLK), F32),
        vm((feats, NX * BLK), F32),
        vm((2, feats, NX * BLK), BF16),
        vm((2, feats, NX * BLK), BF16),
        vm((images, own), F32),
        vm((max(rx, rz), BLK), F32),
        vm((feats, rows), BF16),
        vm((dm.subs, 6, 8, BLK), F32),
        vm((dm.subs, 8, BLK), F32),
        vm((3, 8, BLK), F32),
    ] + [
        dma(shape)
        for shape in (
            (4, NZ * NX), (2, 2), (NZ,), (2, NZ), (2, 3, 2), (2, 2, 3, 2), (2, 3, 2), (2, 2, 3, 2), (2,), (2, 2), (2,), (2, 2),
            (2, 3, 2), (2, 2, 3, 2), (2, 3, 2), (2, 2, 3, 2), (NZ, 2), (2, NZ, 2), (2,), (4, 2), (2, PIECES), (2, PIECES), (3,), (3,),
            (2,), (2,), (2, PIECES, 2), (), (2, 2), (2, 2), (PIECES, 2),
        )
    ]
    anyspace = pl.BlockSpec(memory_space=pl.ANY)
    inside = pl.BlockSpec(memory_space=pltpu.VMEM)
    out_shape = [
        jax.ShapeDtypeStruct((2, own, images), BF16),
        jax.ShapeDtypeStruct((towers, feats, images), BF16),
        jax.ShapeDtypeStruct((towers, feats, images), F32),
        jax.ShapeDtypeStruct((2, BLK), F32),
        jax.ShapeDtypeStruct((2, 2, BLK), F32),
        jax.ShapeDtypeStruct((2, 2, BLK), F32),
    ]
    out_specs = [anyspace] * 3 + [inside] * 3
    block = (feats, NX * BLK)
    *results, mine, theirs = pl.pallas_call(
        functools.partial(kernel, dm),
        name="stitch_fc6",
        out_shape=out_shape + [jax.ShapeDtypeStruct(block, F32), jax.ShapeDtypeStruct(block, BF16)],
        in_specs=[pl.BlockSpec(memory_space=pltpu.SMEM)] + [anyspace] * 3 + [inside] * 4,
        out_specs=out_specs + [anyspace] * 2,
        scratch_shapes=scratch,
        compiler_params=pltpu.CompilerParams(collective_id=1, has_side_effects=True, vmem_limit_bytes=61 * 2**20),
        cost_estimate=pl.CostEstimate(
            flops=6 * towers * feats * images * dm.chans, bytes_accessed=60 * 2**20, transcendentals=towers * images * own
        ),
    )(
        step_rate, weight, pooled, cotangent, fc_bias, stitch,
        valid_mask.reshape(feats // BLK, BLK), image_group.reshape(images // BLK, BLK),
    )
    arrived = lax.ppermute(theirs, "batch", [(0, 2), (1, 3), (2, 0), (3, 1)])

    def cut(shape):
        if len(shape.shape) == 3 and shape.shape[1] % (CUTS * 16) == 0:
            return pl.BlockSpec((shape.shape[0], shape.shape[1] // CUTS, shape.shape[2]), lambda c: (0, c, 0))
        return pl.BlockSpec(shape.shape, lambda c: (0,) * len(shape.shape))

    blocks = [cut(shape) for shape in out_shape]
    results = pl.pallas_call(
        carry_out,
        name="carry_out",
        grid=(CUTS,),
        out_shape=out_shape,
        in_specs=blocks,
        out_specs=blocks,
        compiler_params=pltpu.CompilerParams(vmem_limit_bytes=60 * 2**20),
        cost_estimate=pl.CostEstimate(flops=0, bytes_accessed=32 * 2**20, transcendentals=0),
    )(*results)
    weight_grad = pl.pallas_call(
        functools.partial(settle, dm),
        name="settle",
        out_shape=out_shape[2],
        in_specs=[anyspace, inside, inside],
        out_specs=anyspace,
        scratch_shapes=[vm(block, F32), dma((PIECES, 2))],
        input_output_aliases={0: 0},
        compiler_params=pltpu.CompilerParams(vmem_limit_bytes=6 * 2**20),
    )(results[2], mine, arrived)
    return *results[:2], weight_grad, *results[3:]


def gelu_local(values):
    return jax.nn.gelu(values, approximate=True)


def plain(pooled, weight, fc_bias, stitch, cotangent, valid_mask, image_group, step_rate):
    highest = lax.Precision.HIGHEST
    factor = 1.0 - image_group[None, :].astype(F32) * (1.0 - valid_mask[:, None].astype(F32))
    masked = pooled * factor.astype(BF16)[None]
    owned = weight.shape[2] // lax.axis_size("wide")
    summed = lax.psum_scatter(
        jnp.einsum("tkc,tkb->ctb", weight, masked, preferred_element_type=F32), "wide", scatter_dimension=0, tiled=True
    )
    pre_act = summed + jnp.transpose(fc_bias)[:, :, None]
    hidden, gelu_back = jax.vjp(gelu_local, pre_act)
    stitched = jnp.einsum("ijc,cjb->icb", stitch, hidden, precision=highest)
    upstream = cotangent.astype(F32)
    stitch_part = jnp.einsum("icb,cjb->ijc", upstream, hidden, precision=highest)
    hidden_grad = jnp.einsum("ijc,icb->cjb", stitch, upstream, precision=highest)
    pre_grad = gelu_back(hidden_grad)[0]
    bias_part = jnp.transpose(jnp.sum(pre_grad, axis=2))
    pre_low = pre_grad.astype(BF16)
    bias_grad = lax.psum_scatter(bias_part, "batch", scatter_dimension=1, tiled=True)
    stitch_grad = lax.psum_scatter(stitch_part, "batch", scatter_dimension=2, tiled=True)
    portion = lax.all_gather(pre_low, "wide", axis=0, tiled=True)
    input_sum = jnp.einsum("tkc,ctb->tkb", weight, portion, preferred_element_type=F32)
    block_grad = jnp.einsum("tkb,ctb->tkc", masked, portion, preferred_element_type=F32)
    pooled_grad = (input_sum * factor[None]).astype(BF16)
    weight_grad = lax.psum_scatter(block_grad, "batch", scatter_dimension=2, tiled=True)
    share = owned // lax.axis_size("batch")
    stitch_mine = lax.dynamic_slice_in_dim(stitch, lax.axis_index("batch") * share, share, 2)
    stitch_new = stitch_mine - step_rate[0] * stitch_grad
    return stitched.astype(BF16), pooled_grad, weight_grad, bias_grad, stitch_grad, stitch_new


def fits(mesh, pooled, weight, cotangent):
    return (
        (mesh.shape["wide"], mesh.shape["batch"]) == (NZ * NX, 4)
        and pooled.shape[0] == 2
        and cotangent.shape[1] == 4 * BLK
        and weight.shape[2] == NZ * NX * cotangent.shape[1]
        and pooled.shape[2] % 512 == 0
        and pooled.shape[1] % (16 * PIECES) == 0
        and pooled.shape[1] % BLK == 0
    )


def solution(mesh):
    def body(pooled, weight, fc_bias, stitch, cotangent, *rest):
        form = fused if fits(mesh, pooled, weight, cotangent) else plain
        return form(pooled, weight, fc_bias, stitch, cotangent, *rest)

    return jax.shard_map(
        body,
        mesh=mesh,
        in_specs=(
            P(None, "wide", "batch"),
            P(None, "wide", None),
            P(None, "wide"),
            P(None, None, "wide"),
            P(None, "wide", "batch"),
            P("wide"),
            P("batch"),
            P(),
        ),
        out_specs=(
            P(None, "wide", "batch"),
            P(None, "wide", "batch"),
            P(None, "wide", "batch"),
            P(None, ("wide", "batch")),
            P(None, None, ("wide", "batch")),
            P(None, None, ("wide", "batch")),
        ),
        check_vma=False,
    )
```

```python
import functools
import math

import jax
import jax.numpy as jnp
from jax import lax
from jax.experimental import pallas as pl
from jax.experimental.pallas import tpu as pltpu
from jax.sharding import PartitionSpec as P

MESH = pl.DeviceIdType.MESH
BLK = 128
NZ, NX = 4, 2
F32, BF16 = jnp.float32, jnp.bfloat16
NT = (((1,), (1,)), ((), ()))
ROOT = math.sqrt(2.0 / math.pi)
CUBE = 0.044715
PIECES = 3
CUTS = 4
TAILX = 30
DRAIN = (
    "hz00", "hz01", "zf0", "zf1", "sz0", "sz1", "xf0", "xf1", "sx0", "sx1", "bv0", "gs0", "gs1", "hz10", "hz11", "gx00",
    "gx01", "bv1", "gz00", "gz01", "gx10", "gx11", "hz20", "hz21", "bv2", "gz10", "gz11", "gx20", "gx21", "hd", "em",
    "hp0", "hp1", "hp2", "ss", "bw0", "bw1", "bw2", "gz20", "gz21", "gd", "bp0", "bp1", "bp2", "ya0", "bx0", "ya1",
    "bx1", "bx2", "ya2",
)
ORDER = (
    "zr00", "ws", "zf0", "gz00", "bw0", "x10", "xf0", "ww", "p0", "zr01", "zf1", "gz01", "xf1", "x11", "f0",
    "zr10", "gz10", "bw1", "xr00", "gx00", "em", "zr11", "gz11", "f1", "xr01", "gx01", "x12", "f2",
    "zr20", "gz20", "bw2", "ct", "az", "xr10", "gx10", "f3", "zr21", "gz21", "gd", "bp0", "xr11", "gx11", "x13",
    "zs0", "gs0", "xr20", "gx20", "bp1", "zs1", "gs1", "bp2", "xr21", "gx21",
)


class Dims:
    def __init__(self, pooled, weight, cotangent):
        self.towers, self.feats, self.images = pooled.shape
        self.chans = weight.shape[2]
        self.own = cotangent.shape[1]
        self.subs = self.own // BLK
        self.parts = 2
        self.rows = self.images // self.parts
        self.rx = (self.rows * 19 // 32) // 16 * 16
        self.rz = self.rows - self.rx
        self.units = self.towers * self.subs * self.parts
        self.cols = NZ * NX * BLK
        self.third = self.feats // PIECES


def chunks(count, size=64):
    return [(r, min(size, count - r)) for r in range(0, count, size)]


def kernel(
    dm,
    step_ref, w_hbm, p_hbm, c_hbm, bias, st, valid, group,
    s_hbm, pg_hbm, wg_hbm, out_b, out_sg, out_sn, mine_hbm, theirs_hbm,
    wb, xt, xb, xpb, hole, small_img, craw, cot, stmp, sbuf, acc, fwd, gat, gatp,
    x1_s, x1_r, xr_s, xr_r, zr_s, zr_r, zown, z2_s, z2_r,
    own, tacc, y_s, y_r, hid0, htmp, pgb, sacc, sum_s, sum_r,
    m_w, m_ld, m_x1s, m_x1r, m_xrs, m_xrr, m_zrs, m_zrr, m_z2s, m_z2r, m_z4s, m_z4r,
    m_gxs, m_gxr, m_gzs, m_gzr, m_x5s, m_x5r, m_cs, m_cr, m_ys, m_yr, m_ss, m_sr, m_xps, m_xpr, m_own, m_pg,
    m_cot, m_out, m_last,
):
    n_units, rows, rx, rz = dm.units, dm.rows, dm.rx, dm.rz
    mid_x, mid_z = rx // 32 * 16, rz // 32 * 16
    cuts_x = (0, mid_x), (mid_x, rx - mid_x)
    cuts_z = (0, mid_z), (mid_z, rz - mid_z)
    late = rows * TAILX // 32 // 32 * 32
    rest = (rows - late) // 32 * 16
    tail_x = (0, late // 2), (late // 2, late // 2)
    tail_z = (late - rx, rest), (late - rx + rest, rows - late - rest)
    wi, bi = lax.axis_index("wide"), lax.axis_index("batch")
    z, x = wi // NX, wi % NX
    y, core = bi // 2, bi % 2
    x_dev = (z * NX + 1 - x, bi)
    c_dev = (wi, y * 2 + 1 - core)
    y_dev = (wi, (1 - y) * 2 + core)

    def z_dev(d):
        return (wi + NX, bi) if d == 0 else (wi - NX, bi)

    def far(d):
        return z if d == 0 else NZ - 1 - z

    def rc(src, dst, ss, rs, dev):
        return pltpu.make_async_remote_copy(src, dst, ss, rs, device_id=dev, device_id_type=MESH)

    def al(v, k=BLK):
        return v if isinstance(v, int) else pl.multiple_of(v, k)

    def tower(n):
        return n // (dm.subs * dm.parts)

    def sub(n):
        return (n // dm.parts) % dm.subs

    def part(n):
        return n % dm.parts

    def gpair(n):
        return (n // dm.parts) % 2

    def col(o, xx):
        return al((o * NX + xx) * BLK)

    def w_load(p, w):
        t, u = p // dm.subs, p % dm.subs
        return pltpu.make_async_copy(
            w_hbm.at[t, :, pl.ds(al(w * dm.own + u * BLK), BLK)], wb.at[p % 4, :, pl.ds(w * BLK, BLK)], m_w.at[p % 4, w]
        )

    def x_load(t, s):
        lanes = pl.ds(s * rows, rows)
        return pltpu.make_async_copy(p_hbm.at[t, :, lanes], xb.at[t, :, lanes], m_ld.at[t, s])

    def cot_load(n, i):
        return pltpu.make_async_copy(
            c_hbm.at[i, pl.ds(al(sub(n) * BLK), BLK), pl.ds(al(part(n) * rows), rows)], craw.at[n % 2, i], m_cot.at[n % 2, i]
        )

    def s_copy(n, i):
        return pltpu.make_async_copy(
            sbuf.at[n % 2, i], s_hbm.at[i, pl.ds(al(sub(n) * BLK), BLK), pl.ds(al(part(n) * rows), rows)], m_out.at[n % 2, i]
        )

    def xp_copy(t):
        return rc(xb.at[t], xpb.at[t], m_xps.at[t], m_xpr.at[t], c_dev)

    def x1_copy(n, o):
        return rc(x1_s.at[o], x1_r.at[n % 2, o], m_x1s.at[o], m_x1r.at[n % 2, o], x_dev)

    def xr_copy(n, d, h, f):
        cut = pl.ds(*cuts_x[f])
        return rc(xr_s.at[d, h, cut], xr_r.at[n % 2, d, h, cut], m_xrs.at[d, h, f], m_xrr.at[n % 2, d, h, f], z_dev(d))

    def zr_copy(n, d, h, f):
        cut = pl.ds(*cuts_z[f])
        return rc(zr_s.at[d, h, cut], zr_r.at[n % 2, d, h, cut], m_zrs.at[d, h, f], m_zrr.at[n % 2, d, h, f], z_dev(d))

    def z2_copy(n, f):
        cut = pl.ds(*cuts_z[f])
        return rc(z2_s.at[cut], z2_r.at[n % 2, cut], m_z2s.at[f], m_z2r.at[n % 2, f], x_dev)

    def final(n):
        return isinstance(n, int) and n == n_units - 1

    def g_x(n, o, xx, f):
        start, size = tail_x[f] if final(n) else cuts_x[f]
        return gat.at[gpair(n), pl.ds(al(part(n) * rows + start, 16), size), pl.ds(col(o, xx), BLK)]

    def g_z(n, o, xx, width, f):
        start, size = tail_z[f] if final(n) else cuts_z[f]
        return gat.at[gpair(n), pl.ds(al(part(n) * rows + rx + start, 16), size), pl.ds(col(o, xx), width)]

    def z4_copy(n, f):
        blk = g_z(n, z, x, BLK, f)
        return rc(blk, blk, m_z4s.at[f], m_z4r.at[n % 2, f], x_dev)

    def gx_copy(n, d, h, f):
        blk = g_x(n, z - h if d == 0 else z + h, x, f)
        return rc(blk, blk, m_gxs.at[d, h, f], m_gxr.at[n % 2, d, h, f], z_dev(d))

    def gz_copy(n, d, h, f):
        blk = g_z(n, z - h if d == 0 else z + h, 0, NX * BLK, f)
        return rc(blk, blk, m_gzs.at[d, h, f], m_gzr.at[n % 2, d, h, f], z_dev(d))

    def x5_copy(n, o, xx, f):
        blk = g_x(n, o, xx, f)
        return rc(blk, blk, m_x5s.at[o, f], m_x5r.at[n % 2, o, f], x_dev)

    def c_copy(n, e):
        r = pl.ds(al(part(n) * rows, 16), rows)
        return rc(
            gat.at[gpair(n), r, pl.ds(col(2 * e + 1 - core, 0), NX * BLK)],
            gatp.at[gpair(n), r, pl.ds(e * NX * BLK, NX * BLK)],
            m_cs.at[e], m_cr.at[n % 4, e], c_dev,
        )

    def y_copy(p, q):
        k = pl.ds(q * dm.third, dm.third)
        return rc(y_s.at[p % 2, k], y_r.at[p % 2, k], m_ys.at[p % 2, q], m_yr.at[p % 2, q], y_dev)

    def own_copy(p, q, e):
        t, u = p // dm.subs, p % dm.subs
        k = pl.ds(q * dm.third, dm.third)
        return pltpu.make_async_copy(
            own.at[p % 2, k, pl.ds(e * BLK, BLK)],
            wg_hbm.at[t, k, pl.ds(al(e * dm.own + u * BLK), BLK)],
            m_own.at[p % 2, q, e],
        )

    def last_copies(q):
        slot = (dm.towers * dm.subs - 1) % 2
        k = pl.ds(q * dm.third, dm.third)
        return (
            pltpu.make_async_copy(y_s.at[slot, k], theirs_hbm.at[k], m_last.at[q, 0]),
            pltpu.make_async_copy(own.at[slot, k], mine_hbm.at[k], m_last.at[q, 1]),
        )

    def pg_copy(t, s):
        return pltpu.make_async_copy(pgb, pg_hbm.at[t, :, pl.ds(al(s * rows), rows)], m_pg)

    def sum_copy(k):
        to = lax.rem(bi + k, 4)
        return rc(sum_s.at[to], sum_r.at[k - 1], m_ss.at[k - 1], m_sr.at[k - 1], (wi, to))

    def factor(k, s):
        wide_hole = jnp.concatenate([hole[pl.ds(al(k * BLK), BLK)]] * (rows // BLK), axis=1)
        return 1.0 - small_img[:, pl.ds(al(s * rows), rows)] * wide_hole

    def prepare(t, s):
        @pl.loop(0, dm.feats // BLK)
        def _(k):
            at, lanes = pl.ds(al(k * BLK), BLK), pl.ds(s * rows, rows)
            masked = (xb[t, at, lanes].astype(F32) * factor(k, s)).astype(BF16)
            xb[t, at, lanes] = masked
            xt[t, pl.ds(s * rows, rows), at] = masked.T

    def prepare_cot(n):
        for i in (0, 1):
            cot_load(n, i).wait()
            cot[i, pl.ds(al(part(n) * rows), rows), pl.ds(al(sub(n) * BLK), BLK)] = craw[n % 2, i].T

    def forward(n, k):
        fwd[n % 2, :, pl.ds(k * 256, 256)] = jnp.dot(
            xt[tower(n), pl.ds(al(part(n) * rows, 16), rows), :],
            wb[(n // dm.parts) % 4, :, pl.ds(k * 256, 256)],
            preferred_element_type=F32,
        )

    def x1_send(n, q):
        o = (
            jnp.where(z < 2, 3, 0),
            jnp.where(z < 2, 2, 1),
            jnp.where(z < 2, 1 - z, 5 - z),
            z,
        )[q]

        @pl.when(n >= 1)
        def _():
            x1_copy(n, o).wait_send()

        for r, m in chunks(rx):
            x1_s[o, r : r + m] = fwd[n % 2, r : r + m, pl.ds(col(o, 1 - x), BLK)].astype(BF16)
        x1_copy(n, o).start()

    def xr_hop(n, h, f):
        start, size = cuts_x[f]
        for d in (0, 1):
            o = 3 - h + z if d == 0 else h - 3 + z

            @pl.when(far(d) <= h)
            def _():
                if f == 0:
                    x1_copy(n, o).wait_recv()
                if h:
                    @pl.when(far(d) >= 1)
                    def _():
                        xr_copy(n, d, h - 1, f).wait_recv()

                @pl.when(n >= 1)
                def _():
                    xr_copy(n, d, h, f).wait_send()

                for r, m in chunks(size):
                    r += start
                    v = fwd[n % 2, r : r + m, pl.ds(col(o, x), BLK)] + x1_r[n % 2, o, r : r + m].astype(F32)
                    if h:
                        v = v + xr_r[n % 2, d, h - 1, r : r + m].astype(F32)
                    xr_s[d, h, r : r + m] = v.astype(BF16)
                xr_copy(n, d, h, f).start()

    def zr_hop(n, h, f):
        start, size = cuts_z[f]
        for d in (0, 1):
            o = 3 - h + z if d == 0 else h - 3 + z

            @pl.when(far(d) <= h)
            def _():
                if h:
                    @pl.when(far(d) >= 1)
                    def _():
                        zr_copy(n, d, h - 1, f).wait_recv()

                @pl.when(n >= 1)
                def _():
                    zr_copy(n, d, h, f).wait_send()

                for r, m in chunks(size):
                    r += start
                    v = fwd[n % 2, rx + r : rx + r + m, pl.ds(col(o, 0), NX * BLK)]
                    if h:
                        v = v + zr_r[n % 2, d, h - 1, r : r + m].astype(F32)
                    zr_s[d, h, r : r + m] = v.astype(BF16)
                zr_copy(n, d, h, f).start()

    def z_sum(n, f):
        for d in (0, 1):
            @pl.when(far(d) >= 1)
            def _():
                zr_copy(n, d, 2, f).wait_recv()

        @pl.when(n >= 1)
        def _():
            z2_copy(n, f).wait_send()

        start, size = cuts_z[f]
        for xx in (1 - x, x):
            for r, m in chunks(size):
                r += start
                lanes = pl.ds(al(xx * BLK), BLK)
                v = (
                    fwd[n % 2, rx + r : rx + r + m, pl.ds(col(z, xx), BLK)]
                    + zr_r[n % 2, 0, 2, r : r + m, lanes].astype(F32)
                    + zr_r[n % 2, 1, 2, r : r + m, lanes].astype(F32)
                )
                if xx is x:
                    zown[r : r + m] = v
                else:
                    z2_s[r : r + m] = v.astype(BF16)
            if xx is not x:
                z2_copy(n, f).start()

    def finish(n, row0, count, total):
        t, u = tower(n), sub(n)
        lanes = pl.ds(al(u * BLK), BLK)
        base = part(n) * rows + row0
        b_row = jnp.where(t == 0, bias[0:1, lanes], bias[1:2, lanes])
        from0 = jnp.where(t == 0, st[0, 0:1, lanes], st[0, 1:2, lanes])
        from1 = jnp.where(t == 0, st[1, 0:1, lanes], st[1, 1:2, lanes])
        for r, m in chunks(count):
            at = pl.ds(al(base + r, 16), m)
            v = total(r, m) + b_row
            sq = v * v
            th = jnp.tanh(ROOT * v * (1.0 + CUBE * sq))
            half = 0.5 * (1.0 + th)
            htmp[r : r + m] = v * half
            slope = half + 0.5 * v * (1.0 - th * th) * (ROOT * (1.0 + 3.0 * CUBE * sq))
            up0, up1 = cot[0, at, lanes].astype(F32), cot[1, at, lanes].astype(F32)
            grad = (from0 * up0 + from1 * up1) * slope
            sacc[u, t] += jnp.sum(grad.reshape(m // 8, 8, BLK), axis=0)
            gat[gpair(n), at, pl.ds(col(z, x), BLK)] = grad.astype(BF16)

    def mix(n, row0, count):
        t, u = tower(n), sub(n)
        lanes = pl.ds(al(u * BLK), BLK)
        base = part(n) * rows + row0

        @pl.when(t == 0)
        def _():
            for r, m in chunks(count):
                hid0[pl.ds(al(base + r, 16), m), lanes] = htmp[r : r + m]

        @pl.when(t == 1)
        def _():
            for r, m in chunks(count):
                at = pl.ds(al(base + r, 16), m)
                h = hid0[at, lanes], htmp[r : r + m]
                for i in (0, 1):
                    up = cot[i, at, lanes].astype(F32)
                    stmp[i, row0 + r : row0 + r + m] = (st[i, 0:1, lanes] * h[0] + st[i, 1:2, lanes] * h[1]).astype(BF16)
                    for j in (0, 1):
                        sacc[u, 2 + 2 * i + j] += jnp.sum((up * h[j]).reshape(m // 8, 8, BLK), axis=0)

    def emit(n):
        @pl.when(tower(n) == 1)
        def _():
            for i in (0, 1):
                @pl.when(n >= n_units // 2 + 2)
                def _():
                    s_copy(n, i).wait()

                sbuf[n % 2, i] = stmp[i].T
                s_copy(n, i).start()

    def z_final(n, f):
        z2_copy(n, f).wait_recv()
        start, size = cuts_z[f]

        def total(r, m):
            r += start
            return zown[r : r + m] + z2_r[n % 2, r : r + m].astype(F32)

        finish(n, rx + start, size, total)
        if not final(n):
            z4_send(n, f)
        mix(n, rx + start, size)

    def z4_send(n, f):
        @pl.when(n >= 1)
        def _():
            z4_copy(n - 1, f).wait_send()

        z4_copy(n, f).start()

    def gx_send(n, f):
        for d in (0, 1):
            gather_hop(gx_copy, n, d, 0, f)
        x5_send(n, z, f)

    def x_final(n, f):
        if f == 0:
            x1_copy(n, z).wait_recv()
        for d in (0, 1):
            @pl.when(far(d) >= 1)
            def _():
                xr_copy(n, d, 2, f).wait_recv()

        start, size = cuts_x[f]

        def total(r, m):
            r += start
            return (
                fwd[n % 2, r : r + m, pl.ds(col(z, x), BLK)]
                + x1_r[n % 2, z, r : r + m].astype(F32)
                + xr_r[n % 2, 0, 2, r : r + m].astype(F32)
                + xr_r[n % 2, 1, 2, r : r + m].astype(F32)
            )

        finish(n, start, size, total)
        if not final(n):
            gx_send(n, f)
        mix(n, start, size)

    def gather_hop(copy, n, d, h, f):
        @pl.when((far(d) >= h) & (far(d) <= 2))
        def _():
            @pl.when(n >= 1)
            def _():
                copy(n - 1, d, h, f).wait_send()

            copy(n, d, h, f).start()

    def x5_send(n, o, f):
        @pl.when(n >= 1)
        def _():
            x5_copy(n - 1, o, x, f).wait_send()

        x5_copy(n, o, x, f).start()

    def gz_first(n, f):
        z4_copy(n, f).wait_recv()
        for d in (0, 1):
            gather_hop(gz_copy, n, d, 0, f)

    def gather_arrive(copy, n, h, forward_x, f):
        for d in (0, 1):
            @pl.when(far(d) >= h + 1)
            def _():
                copy(n, d, h, f).wait_recv()
                if h < 2:
                    gather_hop(copy, n, d, h + 1, f)
                if forward_x:
                    x5_send(n, z - 1 - h if d == 0 else z + 1 + h, f)

    def gathered(n):
        for o in range(NZ):
            for f in (0, 1):
                x5_copy(n, o, 1 - x, f).wait_recv()
        for e in (0, 1):
            @pl.when(n >= 1)
            def _():
                c_copy(n, e).wait_send()

            c_copy(n, e).start()

    def back_pooled(n, q):
        t, s = tower(n), part(n)
        lanes = pl.ds(al(s * rows), rows)
        k = pl.ds(q * dm.third, dm.third)
        acc[k, lanes] += lax.dot_general(
            wb[(n // dm.parts) % 4, k, :],
            gat[gpair(n), pl.ds(al(s * rows, 16), rows), :],
            NT,
            preferred_element_type=F32,
        )
        if q < PIECES - 1:
            return

        @pl.when(sub(n) == dm.subs - 1)
        def _():
            @pl.when((t > 0) | (s > 0))
            def _():
                pg_copy(t, s).wait()

            @pl.loop(0, dm.feats // BLK)
            def _(k):
                at = pl.ds(al(k * BLK), BLK)
                pgb[at] = (acc[at, lanes] * factor(k, s)).astype(BF16)
                acc[at, lanes] = jnp.zeros((BLK, rows), F32)

            pg_copy(t, s).start()

    def y_arrive(p, q):
        k = pl.ds(q * dm.third, dm.third)
        y_copy(p, q).wait_recv()
        for r, m in chunks(dm.third):
            at = pl.ds(q * dm.third + r, m)
            own[p % 2, at] += y_r[p % 2, at].astype(F32)
        for e in (0, 1):
            own_copy(p, q, e).start()

    def back_weight(n, q):
        t, s, p = tower(n), part(n), n // dm.parts
        is_last = final(n)
        k, imgs = pl.ds(q * dm.third, dm.third), pl.ds(al(part(n) * rows), rows)
        if q == 0:
            for e in (0, 1):
                c_copy(n, e).wait_recv()

            @pl.when((s == 0) & (p % dm.subs == 0))
            def _():
                xp_copy(t).wait_recv()

        def grads(yy):
            lanes = pl.ds(col(2 * yy + core, 0), NX * BLK)
            return jnp.dot(xb[t, k, imgs], gat[p % 2, imgs, lanes], preferred_element_type=F32) + jnp.dot(
                xpb[t, k, imgs], gatp[p % 2, imgs, pl.ds(al(yy * NX * BLK), NX * BLK)], preferred_element_type=F32
            )

        @pl.when(s == 0)
        def _():
            if not isinstance(n, int):
                @pl.when(p >= 1)
                def _():
                    y_arrive(p - 1, q)

            @pl.when(p >= 2)
            def _():
                for e in (0, 1):
                    own_copy(p, q, e).wait()

            tacc[k, :] = grads(1 - y)
            own[p % 2, k, :] = grads(y)

        @pl.when(s == 1)
        def _():
            @pl.when(p >= 2)
            def _():
                y_copy(p - 2, q).wait_send()

            y_s[p % 2, k, :] = (tacc[k, :] + grads(1 - y)).astype(BF16)
            if not is_last:
                y_copy(p, q).start()
            own[p % 2, k, :] += grads(y)
            if is_last:
                for copy in last_copies(q):
                    copy.start()

    def sums_send():
        for u in range(dm.subs):
            for j in range(6):
                sum_s[u, j : j + 1] = jnp.sum(sacc[u, j], axis=0, keepdims=True)
            sum_s[u, 6:8] = jnp.zeros((2, BLK), F32)
        for k in (1, 2, 3):
            sum_copy(k).start()

    x_load(0, 0).start()
    for w in range(NZ * NX):
        w_load(0, w).start()
    barrier = pltpu.get_barrier_semaphore()
    peers = [x_dev] + [(wi, lax.rem(bi + k, 4)) for k in (1, 2, 3)]
    for dev in peers:
        pl.semaphore_signal(barrier, inc=1, device_id=dev, device_id_type=MESH)
    for d in (0, 1):
        @pl.when(far(d) <= 2)
        def _():
            pl.semaphore_signal(barrier, inc=1, device_id=z_dev(d), device_id_type=MESH)

    small_img[...] = jnp.concatenate([group[j : j + 1] for j in range(dm.images // BLK)], axis=1).astype(F32)
    for j in range(dm.feats // BLK):
        gap = 1.0 - valid[j : j + 1].astype(F32)
        hole[j * BLK : (j + 1) * BLK] = jnp.broadcast_to(gap, (BLK, BLK)).T
    x_load(0, 0).wait()
    prepare(0, 0)

    for d in (0, 1):
        @pl.when(far(d) == 0)
        def _():
            for s in (0, 1):
                for h in range(3):
                    xr_r[s, d, h] = jnp.zeros((rx, BLK), BF16)
                    zr_r[s, d, h] = jnp.zeros((rz, NX * BLK), BF16)

    pl.semaphore_wait(barrier, jnp.where((z == 0) | (z == NZ - 1), len(peers) + 1, len(peers) + 2))
    for w in range(NZ * NX):
        w_load(0, w).wait()
    x_load(0, 1).start()
    for i in (0, 1):
        cot_load(0, i).start()
    for w in range(NZ * NX):
        w_load(1, w).start()
    for s in (0, 1):
        x_load(1, s).start()

    for k in range(4):
        forward(0, k)
    sacc[...] = jnp.zeros_like(sacc)

    def tick(i, carry):
        a, b, c = i, i - 1, i - 2
        on_a, on_b, on_c = i >= 0, i >= 1, i >= 2
        on_f = i + 1 < n_units
        on_p = i >= 3

        def clear():
            @pl.loop(0, dm.feats // 32)
            def _(k):
                acc[pl.ds(al(k * 32, 32), 32)] = jnp.zeros((32, dm.images), F32)

        def w_start():
            for w in range(NZ * NX):
                w_load(i // 2 + 2, w).start()

        def w_wait():
            for w in range(NZ * NX):
                w_load((i + 1) // 2, w).wait()

        def first_images():
            x_load(0, 1).wait()
            prepare(0, 1)
            xp_copy(0).start()

        def cot_next():
            prepare_cot(i)

            @pl.when(i + 1 < n_units // 2)
            def _():
                for j in (0, 1):
                    cot_load(i + 1, j).start()

        steps = {
            "ws": ((i % 2 == 0) & (i // 2 + 2 < dm.towers * dm.subs), w_start),
            "ww": (on_f & (i % 2 == 1), w_wait),
            "az": (i == 0, clear),
            "p0": (i == 0, first_images),
            "ct": (i < n_units // 2, cot_next),
            "em": (on_b, lambda: emit(b)),
            "gd": (on_c, lambda: gathered(c)),
        }
        for q in range(4):
            steps[f"x1{q}"] = on_a, functools.partial(x1_send, a, q)
            steps[f"f{q}"] = on_f, functools.partial(forward, i + 1, q)
        for h in range(PIECES):
            steps[f"bw{h}"] = on_p, functools.partial(back_weight, i - 3, h)
            steps[f"bp{h}"] = on_c, functools.partial(back_pooled, c, h)
        for f in (0, 1):
            steps[f"zf{f}"] = on_b, functools.partial(z_final, b, f)
            steps[f"xf{f}"] = on_b, functools.partial(x_final, b, f)
            steps[f"zs{f}"] = on_a, functools.partial(z_sum, a, f)
            steps[f"gs{f}"] = on_b, functools.partial(gz_first, b, f)
            for h in range(3):
                steps[f"zr{h}{f}"] = on_a, functools.partial(zr_hop, a, h, f)
                steps[f"xr{h}{f}"] = on_a, functools.partial(xr_hop, a, h, f)
                steps[f"gx{h}{f}"] = on_b, functools.partial(gather_arrive, gx_copy, b, h, True, f)
                steps[f"gz{h}{f}"] = on_c, functools.partial(gather_arrive, gz_copy, c, h, False, f)
        for name in ORDER:
            pl.when(steps[name][0])(steps[name][1])

        for s in (0, 1):
            @pl.when(i == 4 + s)
            def _():
                x_load(1, s).wait()
                prepare(1, s)
                if s:
                    xp_copy(1).start()

        return carry

    lax.fori_loop(0, n_units, tick, 0)

    last, pairs = n_units - 1, dm.towers * dm.subs
    ends = {
        "em": lambda: emit(last),
        "hd": lambda: gathered(last - 1),
        "gd": lambda: gathered(last),
        "ss": sums_send,
    }
    for q in range(PIECES):
        ends[f"ya{q}"] = functools.partial(y_arrive, pairs - 2, q)
        ends[f"bv{q}"] = functools.partial(back_weight, last - 2, q)
        ends[f"bw{q}"] = functools.partial(back_weight, last - 1, q)
        ends[f"bx{q}"] = functools.partial(back_weight, last, q)
        ends[f"hp{q}"] = functools.partial(back_pooled, last - 1, q)
        ends[f"bp{q}"] = functools.partial(back_pooled, last, q)
    for f in (0, 1):
        ends[f"zf{f}"] = functools.partial(z_final, last, f)
        ends[f"xf{f}"] = functools.partial(x_final, last, f)
        ends[f"sz{f}"] = functools.partial(z4_send, last, f)
        ends[f"sx{f}"] = functools.partial(gx_send, last, f)
        ends[f"gs{f}"] = functools.partial(gz_first, last, f)
        for h in range(3):
            ends[f"gx{h}{f}"] = functools.partial(gather_arrive, gx_copy, last, h, True, f)
            ends[f"gz{h}{f}"] = functools.partial(gather_arrive, gz_copy, last, h, False, f)
            ends[f"hz{h}{f}"] = functools.partial(gather_arrive, gz_copy, last - 1, h, False, f)
    for name in DRAIN:
        ends[name]()

    for k in (1, 2, 3):
        sum_copy(k).wait_recv()
    total = sum_s[bi] + sum_r[0] + sum_r[1] + sum_r[2]
    out_b[...] = total[0:2]
    for i in (0, 1):
        out_sg[i] = total[2 + 2 * i : 4 + 2 * i]
        out_sn[i] = st[i, :, pl.ds(al(bi * BLK), BLK)] - step_ref[0] * total[2 + 2 * i : 4 + 2 * i]
    for q in range(PIECES):
        for e in (0, 1):
            own_copy(pairs - 2, q, e).wait()
        for copy in last_copies(q):
            copy.wait()
        y_copy(pairs - 2, q).wait_send()
    pg_copy(1, 1).wait()
    for i in (0, 1):
        s_copy(last - 1, i).wait()
        s_copy(last, i).wait()
    for t in range(dm.towers):
        xp_copy(t).wait_send()
    for k in (1, 2, 3):
        sum_copy(k).wait_send()
    for e in (0, 1):
        c_copy(last, e).wait_send()
    for o in range(NZ):
        x1_copy(last, o).wait_send()
    for f in (0, 1):
        for o in range(NZ):
            x5_copy(last, o, x, f).wait_send()
        z2_copy(last, f).wait_send()
        z4_copy(last, f).wait_send()
        for d in (0, 1):
            for h in range(3):
                @pl.when(far(d) <= h)
                def _():
                    xr_copy(last, d, h, f).wait_send()
                    zr_copy(last, d, h, f).wait_send()

                @pl.when((far(d) >= h) & (far(d) <= 2))
                def _():
                    gx_copy(last, d, h, f).wait_send()
                    gz_copy(last, d, h, f).wait_send()


def carry_out(*refs):
    count = len(refs) // 2
    for src, dst in zip(refs[:count], refs[count:]):
        dst[...] = src[...]


def settle(dm, _, mine, arrived, out, total, sems):
    u, step = dm.subs - 1, dm.third
    copies = []
    for q in range(PIECES):
        k = pl.ds(q * step, step)
        total[k] = mine[k] + arrived[k].astype(F32)
        for e in (0, 1):
            copies.append(
                pltpu.make_async_copy(
                    total.at[k, pl.ds(e * BLK, BLK)],
                    out.at[dm.towers - 1, k, pl.ds(e * dm.own + u * BLK, BLK)],
                    sems.at[q, e],
                )
            )
            copies[-1].start()
    for copy in copies:
        copy.wait()


def fused(pooled, weight, fc_bias, stitch, cotangent, valid_mask, image_group, step_rate):
    dm = Dims(pooled, weight, cotangent)
    towers, feats, images, own = dm.towers, dm.feats, dm.images, dm.own
    rows, rx, rz, cols = dm.rows, dm.rx, dm.rz, dm.cols
    dma = pltpu.SemaphoreType.DMA
    vm = pltpu.VMEM
    scratch = [
        vm((4, feats, cols), BF16),
        vm((towers, images, feats), BF16),
        vm((towers, feats, images), BF16),
        vm((towers, feats, images), BF16),
        vm((feats, BLK), F32),
        vm((1, images), F32),
        vm((2, 2, BLK, rows), BF16),
        vm((2, images, own), BF16),
        vm((2, rows, BLK), BF16),
        vm((2, 2, BLK, rows), BF16),
        vm((feats, images), F32),
        vm((2, rows, cols), F32),
        vm((2, images, cols), BF16),
        vm((2, images, cols // 2), BF16),
        vm((NZ, rx, BLK), BF16),
        vm((2, NZ, rx, BLK), BF16),
        vm((2, 3, rx, BLK), BF16),
        vm((2, 2, 3, rx, BLK), BF16),
        vm((2, 3, rz, NX * BLK), BF16),
        vm((2, 2, 3, rz, NX * BLK), BF16),
        vm((rz, BLK), F32),
        vm((rz, BLK), BF16),
        vm((2, rz, BLK), BF16),
        vm((2, feats, NX * BLK), F32),
        vm((feats, NX * BLK), F32),
        vm((2, feats, NX * BLK), BF16),
        vm((2, feats, NX * BLK), BF16),
        vm((images, own), F32),
        vm((max(rx, rz), BLK), F32),
        vm((feats, rows), BF16),
        vm((dm.subs, 6, 8, BLK), F32),
        vm((dm.subs, 8, BLK), F32),
        vm((3, 8, BLK), F32),
    ] + [
        dma(shape)
        for shape in (
            (4, NZ * NX), (2, 2), (NZ,), (2, NZ), (2, 3, 2), (2, 2, 3, 2), (2, 3, 2), (2, 2, 3, 2), (2,), (2, 2), (2,), (2, 2),
            (2, 3, 2), (2, 2, 3, 2), (2, 3, 2), (2, 2, 3, 2), (NZ, 2), (2, NZ, 2), (2,), (4, 2), (2, PIECES), (2, PIECES), (3,), (3,),
            (2,), (2,), (2, PIECES, 2), (), (2, 2), (2, 2), (PIECES, 2),
        )
    ]
    anyspace = pl.BlockSpec(memory_space=pl.ANY)
    inside = pl.BlockSpec(memory_space=pltpu.VMEM)
    out_shape = [
        jax.ShapeDtypeStruct((2, own, images), BF16),
        jax.ShapeDtypeStruct((towers, feats, images), BF16),
        jax.ShapeDtypeStruct((towers, feats, images), F32),
        jax.ShapeDtypeStruct((2, BLK), F32),
        jax.ShapeDtypeStruct((2, 2, BLK), F32),
        jax.ShapeDtypeStruct((2, 2, BLK), F32),
    ]
    out_specs = [anyspace] * 3 + [inside] * 3
    block = (feats, NX * BLK)
    *results, mine, theirs = pl.pallas_call(
        functools.partial(kernel, dm),
        name="stitch_fc6",
        out_shape=out_shape + [jax.ShapeDtypeStruct(block, F32), jax.ShapeDtypeStruct(block, BF16)],
        in_specs=[pl.BlockSpec(memory_space=pltpu.SMEM)] + [anyspace] * 3 + [inside] * 4,
        out_specs=out_specs + [anyspace] * 2,
        scratch_shapes=scratch,
        compiler_params=pltpu.CompilerParams(collective_id=1, has_side_effects=True, vmem_limit_bytes=61 * 2**20),
        cost_estimate=pl.CostEstimate(
            flops=6 * towers * feats * images * dm.chans, bytes_accessed=60 * 2**20, transcendentals=towers * images * own
        ),
    )(
        step_rate, weight, pooled, cotangent, fc_bias, stitch,
        valid_mask.reshape(feats // BLK, BLK), image_group.reshape(images // BLK, BLK),
    )
    arrived = lax.ppermute(theirs, "batch", [(0, 2), (1, 3), (2, 0), (3, 1)])

    def cut(shape):
        if len(shape.shape) == 3 and shape.shape[1] % (CUTS * 16) == 0:
            return pl.BlockSpec((shape.shape[0], shape.shape[1] // CUTS, shape.shape[2]), lambda c: (0, c, 0))
        return pl.BlockSpec(shape.shape, lambda c: (0,) * len(shape.shape))

    blocks = [cut(shape) for shape in out_shape]
    results = pl.pallas_call(
        carry_out,
        name="carry_out",
        grid=(CUTS,),
        out_shape=out_shape,
        in_specs=blocks,
        out_specs=blocks,
        compiler_params=pltpu.CompilerParams(vmem_limit_bytes=60 * 2**20),
        cost_estimate=pl.CostEstimate(flops=0, bytes_accessed=32 * 2**20, transcendentals=0),
    )(*results)
    weight_grad = pl.pallas_call(
        functools.partial(settle, dm),
        name="settle",
        out_shape=out_shape[2],
        in_specs=[anyspace, inside, inside],
        out_specs=anyspace,
        scratch_shapes=[vm(block, F32), dma((PIECES, 2))],
        input_output_aliases={0: 0},
        compiler_params=pltpu.CompilerParams(vmem_limit_bytes=6 * 2**20),
    )(results[2], mine, arrived)
    return *results[:2], weight_grad, *results[3:]


def gelu_local(values):
    return jax.nn.gelu(values, approximate=True)


def plain(pooled, weight, fc_bias, stitch, cotangent, valid_mask, image_group, step_rate):
    highest = lax.Precision.HIGHEST
    factor = 1.0 - image_group[None, :].astype(F32) * (1.0 - valid_mask[:, None].astype(F32))
    masked = pooled * factor.astype(BF16)[None]
    owned = weight.shape[2] // lax.axis_size("wide")
    summed = lax.psum_scatter(
        jnp.einsum("tkc,tkb->ctb", weight, masked, preferred_element_type=F32), "wide", scatter_dimension=0, tiled=True
    )
    pre_act = summed + jnp.transpose(fc_bias)[:, :, None]
    hidden, gelu_back = jax.vjp(gelu_local, pre_act)
    stitched = jnp.einsum("ijc,cjb->icb", stitch, hidden, precision=highest)
    upstream = cotangent.astype(F32)
    stitch_part = jnp.einsum("icb,cjb->ijc", upstream, hidden, precision=highest)
    hidden_grad = jnp.einsum("ijc,icb->cjb", stitch, upstream, precision=highest)
    pre_grad = gelu_back(hidden_grad)[0]
    bias_part = jnp.transpose(jnp.sum(pre_grad, axis=2))
    pre_low = pre_grad.astype(BF16)
    bias_grad = lax.psum_scatter(bias_part, "batch", scatter_dimension=1, tiled=True)
    stitch_grad = lax.psum_scatter(stitch_part, "batch", scatter_dimension=2, tiled=True)
    portion = lax.all_gather(pre_low, "wide", axis=0, tiled=True)
    input_sum = jnp.einsum("tkc,ctb->tkb", weight, portion, preferred_element_type=F32)
    block_grad = jnp.einsum("tkb,ctb->tkc", masked, portion, preferred_element_type=F32)
    pooled_grad = (input_sum * factor[None]).astype(BF16)
    weight_grad = lax.psum_scatter(block_grad, "batch", scatter_dimension=2, tiled=True)
    share = owned // lax.axis_size("batch")
    stitch_mine = lax.dynamic_slice_in_dim(stitch, lax.axis_index("batch") * share, share, 2)
    stitch_new = stitch_mine - step_rate[0] * stitch_grad
    return stitched.astype(BF16), pooled_grad, weight_grad, bias_grad, stitch_grad, stitch_new


def fits(mesh, pooled, weight, cotangent):
    return (
        (mesh.shape["wide"], mesh.shape["batch"]) == (NZ * NX, 4)
        and pooled.shape[0] == 2
        and cotangent.shape[1] == 4 * BLK
        and weight.shape[2] == NZ * NX * cotangent.shape[1]
        and pooled.shape[2] % 512 == 0
        and pooled.shape[1] % (16 * PIECES) == 0
        and pooled.shape[1] % BLK == 0
    )


def solution(mesh):
    def body(pooled, weight, fc_bias, stitch, cotangent, *rest):
        form = fused if fits(mesh, pooled, weight, cotangent) else plain
        return form(pooled, weight, fc_bias, stitch, cotangent, *rest)

    return jax.shard_map(
        body,
        mesh=mesh,
        in_specs=(
            P(None, "wide", "batch"),
            P(None, "wide", None),
            P(None, "wide"),
            P(None, None, "wide"),
            P(None, "wide", "batch"),
            P("wide"),
            P("batch"),
            P(),
        ),
        out_specs=(
            P(None, "wide", "batch"),
            P(None, "wide", "batch"),
            P(None, "wide", "batch"),
            P(None, ("wide", "batch")),
            P(None, None, ("wide", "batch")),
            P(None, None, ("wide", "batch")),
        ),
        check_vma=False,
    )
```

```python
import functools
import math

import jax
import jax.numpy as jnp
from jax import lax
from jax.experimental import pallas as pl
from jax.experimental.pallas import tpu as pltpu
from jax.sharding import PartitionSpec as P

MESH = pl.DeviceIdType.MESH
BLK = 128
NZ, NX = 4, 2
F32, BF16 = jnp.float32, jnp.bfloat16
NT = (((1,), (1,)), ((), ()))
ROOT = math.sqrt(2.0 / math.pi)
CUBE = 0.044715
PIECES = 3
CUTS = 4
TAILX = 30
DRAIN = (
    "hz00", "hz01", "zf0", "zf1", "sz0", "sz1", "xf0", "xf1", "sx0", "sx1", "bv0", "gs0", "gs1", "hz10", "hz11", "gx00",
    "gx01", "bv1", "gz00", "gz01", "gx10", "gx11", "hz20", "hz21", "bv2", "gz10", "gz11", "gx20", "gx21", "hd", "em",
    "hp0", "hp1", "hp2", "ss", "bw0", "bw1", "bw2", "gz20", "gz21", "gd", "bp0", "bp1", "bp2", "ya0", "bx0", "ya1",
    "bx1", "bx2", "ya2",
)
ORDER = (
    "x10", "zr00", "ws", "zf0", "gz00", "bw0", "xf0", "ww", "p0", "zr01", "zf1", "gz01", "xf1", "x11", "f0",
    "zr10", "gz10", "bw1", "xr00", "gx00", "em", "zr11", "gz11", "f1", "xr01", "gx01", "x12", "f2",
    "zr20", "gz20", "bw2", "ct", "az", "xr10", "gx10", "f3", "zr21", "gz21", "gd", "bp0", "xr11", "gx11", "x13",
    "zs0", "gs0", "xr20", "gx20", "bp1", "zs1", "gs1", "bp2", "xr21", "gx21",
)


class Dims:
    def __init__(self, pooled, weight, cotangent):
        self.towers, self.feats, self.images = pooled.shape
        self.chans = weight.shape[2]
        self.own = cotangent.shape[1]
        self.subs = self.own // BLK
        self.parts = 2
        self.rows = self.images // self.parts
        self.rx = (self.rows * 19 // 32) // 16 * 16
        self.rz = self.rows - self.rx
        self.units = self.towers * self.subs * self.parts
        self.cols = NZ * NX * BLK
        self.third = self.feats // PIECES


def chunks(count, size=64):
    return [(r, min(size, count - r)) for r in range(0, count, size)]


def kernel(
    dm,
    step_ref, w_hbm, p_hbm, c_hbm, bias, st, valid, group,
    s_hbm, pg_hbm, wg_hbm, out_b, out_sg, out_sn, mine_hbm, theirs_hbm,
    wb, xt, xb, xpb, hole, small_img, craw, cot, stmp, sbuf, acc, fwd, gat, gatp,
    x1_s, x1_r, xr_s, xr_r, zr_s, zr_r, zown, z2_s, z2_r,
    own, tacc, y_s, y_r, hid0, htmp, pgb, sacc, sum_s, sum_r,
    m_w, m_ld, m_x1s, m_x1r, m_xrs, m_xrr, m_zrs, m_zrr, m_z2s, m_z2r, m_z4s, m_z4r,
    m_gxs, m_gxr, m_gzs, m_gzr, m_x5s, m_x5r, m_cs, m_cr, m_ys, m_yr, m_ss, m_sr, m_xps, m_xpr, m_own, m_pg,
    m_cot, m_out, m_last,
):
    n_units, rows, rx, rz = dm.units, dm.rows, dm.rx, dm.rz
    mid_x, mid_z = rx // 32 * 16, rz // 32 * 16
    cuts_x = (0, mid_x), (mid_x, rx - mid_x)
    cuts_z = (0, mid_z), (mid_z, rz - mid_z)
    late = rows * TAILX // 32 // 32 * 32
    rest = (rows - late) // 32 * 16
    tail_x = (0, late // 2), (late // 2, late // 2)
    tail_z = (late - rx, rest), (late - rx + rest, rows - late - rest)
    wi, bi = lax.axis_index("wide"), lax.axis_index("batch")
    z, x = wi // NX, wi % NX
    y, core = bi // 2, bi % 2
    x_dev = (z * NX + 1 - x, bi)
    c_dev = (wi, y * 2 + 1 - core)
    y_dev = (wi, (1 - y) * 2 + core)

    def z_dev(d):
        return (wi + NX, bi) if d == 0 else (wi - NX, bi)

    def far(d):
        return z if d == 0 else NZ - 1 - z

    def rc(src, dst, ss, rs, dev):
        return pltpu.make_async_remote_copy(src, dst, ss, rs, device_id=dev, device_id_type=MESH)

    def al(v, k=BLK):
        return v if isinstance(v, int) else pl.multiple_of(v, k)

    def tower(n):
        return n // (dm.subs * dm.parts)

    def sub(n):
        return (n // dm.parts) % dm.subs

    def part(n):
        return n % dm.parts

    def gpair(n):
        return (n // dm.parts) % 2

    def col(o, xx):
        return al((o * NX + xx) * BLK)

    def w_load(p, w):
        t, u = p // dm.subs, p % dm.subs
        return pltpu.make_async_copy(
            w_hbm.at[t, :, pl.ds(al(w * dm.own + u * BLK), BLK)], wb.at[p % 4, :, pl.ds(w * BLK, BLK)], m_w.at[p % 4, w]
        )

    def x_load(t, s):
        lanes = pl.ds(s * rows, rows)
        return pltpu.make_async_copy(p_hbm.at[t, :, lanes], xb.at[t, :, lanes], m_ld.at[t, s])

    def cot_load(n, i):
        return pltpu.make_async_copy(
            c_hbm.at[i, pl.ds(al(sub(n) * BLK), BLK), pl.ds(al(part(n) * rows), rows)], craw.at[n % 2, i], m_cot.at[n % 2, i]
        )

    def s_copy(n, i):
        return pltpu.make_async_copy(
            sbuf.at[n % 2, i], s_hbm.at[i, pl.ds(al(sub(n) * BLK), BLK), pl.ds(al(part(n) * rows), rows)], m_out.at[n % 2, i]
        )

    def xp_copy(t):
        return rc(xb.at[t], xpb.at[t], m_xps.at[t], m_xpr.at[t], c_dev)

    def x1_copy(n, o):
        return rc(x1_s.at[o], x1_r.at[n % 2, o], m_x1s.at[o], m_x1r.at[n % 2, o], x_dev)

    def xr_copy(n, d, h, f):
        cut = pl.ds(*cuts_x[f])
        return rc(xr_s.at[d, h, cut], xr_r.at[n % 2, d, h, cut], m_xrs.at[d, h, f], m_xrr.at[n % 2, d, h, f], z_dev(d))

    def zr_copy(n, d, h, f):
        cut = pl.ds(*cuts_z[f])
        return rc(zr_s.at[d, h, cut], zr_r.at[n % 2, d, h, cut], m_zrs.at[d, h, f], m_zrr.at[n % 2, d, h, f], z_dev(d))

    def z2_copy(n, f):
        cut = pl.ds(*cuts_z[f])
        return rc(z2_s.at[cut], z2_r.at[n % 2, cut], m_z2s.at[f], m_z2r.at[n % 2, f], x_dev)

    def final(n):
        return isinstance(n, int) and n == n_units - 1

    def g_x(n, o, xx, f):
        start, size = tail_x[f] if final(n) else cuts_x[f]
        return gat.at[gpair(n), pl.ds(al(part(n) * rows + start, 16), size), pl.ds(col(o, xx), BLK)]

    def g_z(n, o, xx, width, f):
        start, size = tail_z[f] if final(n) else cuts_z[f]
        return gat.at[gpair(n), pl.ds(al(part(n) * rows + rx + start, 16), size), pl.ds(col(o, xx), width)]

    def z4_copy(n, f):
        blk = g_z(n, z, x, BLK, f)
        return rc(blk, blk, m_z4s.at[f], m_z4r.at[n % 2, f], x_dev)

    def gx_copy(n, d, h, f):
        blk = g_x(n, z - h if d == 0 else z + h, x, f)
        return rc(blk, blk, m_gxs.at[d, h, f], m_gxr.at[n % 2, d, h, f], z_dev(d))

    def gz_copy(n, d, h, f):
        blk = g_z(n, z - h if d == 0 else z + h, 0, NX * BLK, f)
        return rc(blk, blk, m_gzs.at[d, h, f], m_gzr.at[n % 2, d, h, f], z_dev(d))

    def x5_copy(n, o, xx, f):
        blk = g_x(n, o, xx, f)
        return rc(blk, blk, m_x5s.at[o, f], m_x5r.at[n % 2, o, f], x_dev)

    def c_copy(n, e):
        r = pl.ds(al(part(n) * rows, 16), rows)
        return rc(
            gat.at[gpair(n), r, pl.ds(col(2 * e + 1 - core, 0), NX * BLK)],
            gatp.at[gpair(n), r, pl.ds(e * NX * BLK, NX * BLK)],
            m_cs.at[e], m_cr.at[n % 4, e], c_dev,
        )

    def y_copy(p, q):
        k = pl.ds(q * dm.third, dm.third)
        return rc(y_s.at[p % 2, k], y_r.at[p % 2, k], m_ys.at[p % 2, q], m_yr.at[p % 2, q], y_dev)

    def own_copy(p, q, e):
        t, u = p // dm.subs, p % dm.subs
        k = pl.ds(q * dm.third, dm.third)
        return pltpu.make_async_copy(
            own.at[p % 2, k, pl.ds(e * BLK, BLK)],
            wg_hbm.at[t, k, pl.ds(al(e * dm.own + u * BLK), BLK)],
            m_own.at[p % 2, q, e],
        )

    def last_copies(q):
        slot = (dm.towers * dm.subs - 1) % 2
        k = pl.ds(q * dm.third, dm.third)
        return (
            pltpu.make_async_copy(y_s.at[slot, k], theirs_hbm.at[k], m_last.at[q, 0]),
            pltpu.make_async_copy(own.at[slot, k], mine_hbm.at[k], m_last.at[q, 1]),
        )

    def pg_copy(t, s):
        return pltpu.make_async_copy(pgb, pg_hbm.at[t, :, pl.ds(al(s * rows), rows)], m_pg)

    def sum_copy(k):
        to = lax.rem(bi + k, 4)
        return rc(sum_s.at[to], sum_r.at[k - 1], m_ss.at[k - 1], m_sr.at[k - 1], (wi, to))

    def factor(k, s):
        wide_hole = jnp.concatenate([hole[pl.ds(al(k * BLK), BLK)]] * (rows // BLK), axis=1)
        return 1.0 - small_img[:, pl.ds(al(s * rows), rows)] * wide_hole

    def prepare(t, s):
        @pl.loop(0, dm.feats // BLK)
        def _(k):
            at, lanes = pl.ds(al(k * BLK), BLK), pl.ds(s * rows, rows)
            masked = (xb[t, at, lanes].astype(F32) * factor(k, s)).astype(BF16)
            xb[t, at, lanes] = masked
            xt[t, pl.ds(s * rows, rows), at] = masked.T

    def prepare_cot(n):
        for i in (0, 1):
            cot_load(n, i).wait()
            cot[i, pl.ds(al(part(n) * rows), rows), pl.ds(al(sub(n) * BLK), BLK)] = craw[n % 2, i].T

    def forward(n, k):
        fwd[n % 2, :, pl.ds(k * 256, 256)] = jnp.dot(
            xt[tower(n), pl.ds(al(part(n) * rows, 16), rows), :],
            wb[(n // dm.parts) % 4, :, pl.ds(k * 256, 256)],
            preferred_element_type=F32,
        )

    def x1_send(n, q):
        o = (
            jnp.where(z < 2, 3, 0),
            jnp.where(z < 2, 2, 1),
            jnp.where(z < 2, 1 - z, 5 - z),
            z,
        )[q]

        @pl.when(n >= 1)
        def _():
            x1_copy(n, o).wait_send()

        for r, m in chunks(rx):
            x1_s[o, r : r + m] = fwd[n % 2, r : r + m, pl.ds(col(o, 1 - x), BLK)].astype(BF16)
        x1_copy(n, o).start()

    def xr_hop(n, h, f):
        start, size = cuts_x[f]
        for d in (0, 1):
            o = 3 - h + z if d == 0 else h - 3 + z

            @pl.when(far(d) <= h)
            def _():
                if f == 0:
                    x1_copy(n, o).wait_recv()
                if h:
                    @pl.when(far(d) >= 1)
                    def _():
                        xr_copy(n, d, h - 1, f).wait_recv()

                @pl.when(n >= 1)
                def _():
                    xr_copy(n, d, h, f).wait_send()

                for r, m in chunks(size):
                    r += start
                    v = fwd[n % 2, r : r + m, pl.ds(col(o, x), BLK)] + x1_r[n % 2, o, r : r + m].astype(F32)
                    if h:
                        v = v + xr_r[n % 2, d, h - 1, r : r + m].astype(F32)
                    xr_s[d, h, r : r + m] = v.astype(BF16)
                xr_copy(n, d, h, f).start()

    def zr_hop(n, h, f):
        start, size = cuts_z[f]
        for d in (0, 1):
            o = 3 - h + z if d == 0 else h - 3 + z

            @pl.when(far(d) <= h)
            def _():
                if h:
                    @pl.when(far(d) >= 1)
                    def _():
                        zr_copy(n, d, h - 1, f).wait_recv()

                @pl.when(n >= 1)
                def _():
                    zr_copy(n, d, h, f).wait_send()

                for r, m in chunks(size):
                    r += start
                    v = fwd[n % 2, rx + r : rx + r + m, pl.ds(col(o, 0), NX * BLK)]
                    if h:
                        v = v + zr_r[n % 2, d, h - 1, r : r + m].astype(F32)
                    zr_s[d, h, r : r + m] = v.astype(BF16)
                zr_copy(n, d, h, f).start()

    def z_sum(n, f):
        for d in (0, 1):
            @pl.when(far(d) >= 1)
            def _():
                zr_copy(n, d, 2, f).wait_recv()

        @pl.when(n >= 1)
        def _():
            z2_copy(n, f).wait_send()

        start, size = cuts_z[f]
        for xx in (1 - x, x):
            for r, m in chunks(size):
                r += start
                lanes = pl.ds(al(xx * BLK), BLK)
                v = (
                    fwd[n % 2, rx + r : rx + r + m, pl.ds(col(z, xx), BLK)]
                    + zr_r[n % 2, 0, 2, r : r + m, lanes].astype(F32)
                    + zr_r[n % 2, 1, 2, r : r + m, lanes].astype(F32)
                )
                if xx is x:
                    zown[r : r + m] = v
                else:
                    z2_s[r : r + m] = v.astype(BF16)
            if xx is not x:
                z2_copy(n, f).start()

    def finish(n, row0, count, total):
        t, u = tower(n), sub(n)
        lanes = pl.ds(al(u * BLK), BLK)
        base = part(n) * rows + row0
        b_row = jnp.where(t == 0, bias[0:1, lanes], bias[1:2, lanes])
        from0 = jnp.where(t == 0, st[0, 0:1, lanes], st[0, 1:2, lanes])
        from1 = jnp.where(t == 0, st[1, 0:1, lanes], st[1, 1:2, lanes])
        for r, m in chunks(count):
            at = pl.ds(al(base + r, 16), m)
            v = total(r, m) + b_row
            sq = v * v
            th = jnp.tanh(ROOT * v * (1.0 + CUBE * sq))
            half = 0.5 * (1.0 + th)
            htmp[r : r + m] = v * half
            slope = half + 0.5 * v * (1.0 - th * th) * (ROOT * (1.0 + 3.0 * CUBE * sq))
            up0, up1 = cot[0, at, lanes].astype(F32), cot[1, at, lanes].astype(F32)
            grad = (from0 * up0 + from1 * up1) * slope
            sacc[u, t] += jnp.sum(grad.reshape(m // 8, 8, BLK), axis=0)
            gat[gpair(n), at, pl.ds(col(z, x), BLK)] = grad.astype(BF16)

    def mix(n, row0, count):
        t, u = tower(n), sub(n)
        lanes = pl.ds(al(u * BLK), BLK)
        base = part(n) * rows + row0

        @pl.when(t == 0)
        def _():
            for r, m in chunks(count):
                hid0[pl.ds(al(base + r, 16), m), lanes] = htmp[r : r + m]

        @pl.when(t == 1)
        def _():
            for r, m in chunks(count):
                at = pl.ds(al(base + r, 16), m)
                h = hid0[at, lanes], htmp[r : r + m]
                for i in (0, 1):
                    up = cot[i, at, lanes].astype(F32)
                    stmp[i, row0 + r : row0 + r + m] = (st[i, 0:1, lanes] * h[0] + st[i, 1:2, lanes] * h[1]).astype(BF16)
                    for j in (0, 1):
                        sacc[u, 2 + 2 * i + j] += jnp.sum((up * h[j]).reshape(m // 8, 8, BLK), axis=0)

    def emit(n):
        @pl.when(tower(n) == 1)
        def _():
            for i in (0, 1):
                @pl.when(n >= n_units // 2 + 2)
                def _():
                    s_copy(n, i).wait()

                sbuf[n % 2, i] = stmp[i].T
                s_copy(n, i).start()

    def z_final(n, f):
        z2_copy(n, f).wait_recv()
        start, size = cuts_z[f]

        def total(r, m):
            r += start
            return zown[r : r + m] + z2_r[n % 2, r : r + m].astype(F32)

        finish(n, rx + start, size, total)
        if not final(n):
            z4_send(n, f)
        mix(n, rx + start, size)

    def z4_send(n, f):
        @pl.when(n >= 1)
        def _():
            z4_copy(n - 1, f).wait_send()

        z4_copy(n, f).start()

    def gx_send(n, f):
        for d in (0, 1):
            gather_hop(gx_copy, n, d, 0, f)
        x5_send(n, z, f)

    def x_final(n, f):
        if f == 0:
            x1_copy(n, z).wait_recv()
        for d in (0, 1):
            @pl.when(far(d) >= 1)
            def _():
                xr_copy(n, d, 2, f).wait_recv()

        start, size = cuts_x[f]

        def total(r, m):
            r += start
            return (
                fwd[n % 2, r : r + m, pl.ds(col(z, x), BLK)]
                + x1_r[n % 2, z, r : r + m].astype(F32)
                + xr_r[n % 2, 0, 2, r : r + m].astype(F32)
                + xr_r[n % 2, 1, 2, r : r + m].astype(F32)
            )

        finish(n, start, size, total)
        if not final(n):
            gx_send(n, f)
        mix(n, start, size)

    def gather_hop(copy, n, d, h, f):
        @pl.when((far(d) >= h) & (far(d) <= 2))
        def _():
            @pl.when(n >= 1)
            def _():
                copy(n - 1, d, h, f).wait_send()

            copy(n, d, h, f).start()

    def x5_send(n, o, f):
        @pl.when(n >= 1)
        def _():
            x5_copy(n - 1, o, x, f).wait_send()

        x5_copy(n, o, x, f).start()

    def gz_first(n, f):
        z4_copy(n, f).wait_recv()
        for d in (0, 1):
            gather_hop(gz_copy, n, d, 0, f)

    def gather_arrive(copy, n, h, forward_x, f):
        for d in (0, 1):
            @pl.when(far(d) >= h + 1)
            def _():
                copy(n, d, h, f).wait_recv()
                if h < 2:
                    gather_hop(copy, n, d, h + 1, f)
                if forward_x:
                    x5_send(n, z - 1 - h if d == 0 else z + 1 + h, f)

    def gathered(n):
        for o in range(NZ):
            for f in (0, 1):
                x5_copy(n, o, 1 - x, f).wait_recv()
        for e in (0, 1):
            @pl.when(n >= 1)
            def _():
                c_copy(n, e).wait_send()

            c_copy(n, e).start()

    def back_pooled(n, q):
        t, s = tower(n), part(n)
        lanes = pl.ds(al(s * rows), rows)
        k = pl.ds(q * dm.third, dm.third)
        acc[k, lanes] += lax.dot_general(
            wb[(n // dm.parts) % 4, k, :],
            gat[gpair(n), pl.ds(al(s * rows, 16), rows), :],
            NT,
            preferred_element_type=F32,
        )
        if q < PIECES - 1:
            return

        @pl.when(sub(n) == dm.subs - 1)
        def _():
            @pl.when((t > 0) | (s > 0))
            def _():
                pg_copy(t, s).wait()

            @pl.loop(0, dm.feats // BLK)
            def _(k):
                at = pl.ds(al(k * BLK), BLK)
                pgb[at] = (acc[at, lanes] * factor(k, s)).astype(BF16)
                acc[at, lanes] = jnp.zeros((BLK, rows), F32)

            pg_copy(t, s).start()

    def y_arrive(p, q):
        k = pl.ds(q * dm.third, dm.third)
        y_copy(p, q).wait_recv()
        for r, m in chunks(dm.third):
            at = pl.ds(q * dm.third + r, m)
            own[p % 2, at] += y_r[p % 2, at].astype(F32)
        for e in (0, 1):
            own_copy(p, q, e).start()

    def back_weight(n, q):
        t, s, p = tower(n), part(n), n // dm.parts
        is_last = final(n)
        k, imgs = pl.ds(q * dm.third, dm.third), pl.ds(al(part(n) * rows), rows)
        if q == 0:
            for e in (0, 1):
                c_copy(n, e).wait_recv()

            @pl.when((s == 0) & (p % dm.subs == 0))
            def _():
                xp_copy(t).wait_recv()

        def grads(yy):
            lanes = pl.ds(col(2 * yy + core, 0), NX * BLK)
            return jnp.dot(xb[t, k, imgs], gat[p % 2, imgs, lanes], preferred_element_type=F32) + jnp.dot(
                xpb[t, k, imgs], gatp[p % 2, imgs, pl.ds(al(yy * NX * BLK), NX * BLK)], preferred_element_type=F32
            )

        @pl.when(s == 0)
        def _():
            if not isinstance(n, int):
                @pl.when(p >= 1)
                def _():
                    y_arrive(p - 1, q)

            @pl.when(p >= 2)
            def _():
                for e in (0, 1):
                    own_copy(p, q, e).wait()

            tacc[k, :] = grads(1 - y)
            own[p % 2, k, :] = grads(y)

        @pl.when(s == 1)
        def _():
            @pl.when(p >= 2)
            def _():
                y_copy(p - 2, q).wait_send()

            y_s[p % 2, k, :] = (tacc[k, :] + grads(1 - y)).astype(BF16)
            if not is_last:
                y_copy(p, q).start()
            own[p % 2, k, :] += grads(y)
            if is_last:
                for copy in last_copies(q):
                    copy.start()

    def sums_send():
        for u in range(dm.subs):
            for j in range(6):
                sum_s[u, j : j + 1] = jnp.sum(sacc[u, j], axis=0, keepdims=True)
            sum_s[u, 6:8] = jnp.zeros((2, BLK), F32)
        for k in (1, 2, 3):
            sum_copy(k).start()

    x_load(0, 0).start()
    for w in range(NZ * NX):
        w_load(0, w).start()
    barrier = pltpu.get_barrier_semaphore()
    peers = [x_dev] + [(wi, lax.rem(bi + k, 4)) for k in (1, 2, 3)]
    for dev in peers:
        pl.semaphore_signal(barrier, inc=1, device_id=dev, device_id_type=MESH)
    for d in (0, 1):
        @pl.when(far(d) <= 2)
        def _():
            pl.semaphore_signal(barrier, inc=1, device_id=z_dev(d), device_id_type=MESH)

    small_img[...] = jnp.concatenate([group[j : j + 1] for j in range(dm.images // BLK)], axis=1).astype(F32)
    for j in range(dm.feats // BLK):
        gap = 1.0 - valid[j : j + 1].astype(F32)
        hole[j * BLK : (j + 1) * BLK] = jnp.broadcast_to(gap, (BLK, BLK)).T
    x_load(0, 0).wait()
    prepare(0, 0)

    for d in (0, 1):
        @pl.when(far(d) == 0)
        def _():
            for s in (0, 1):
                for h in range(3):
                    xr_r[s, d, h] = jnp.zeros((rx, BLK), BF16)
                    zr_r[s, d, h] = jnp.zeros((rz, NX * BLK), BF16)

    pl.semaphore_wait(barrier, jnp.where((z == 0) | (z == NZ - 1), len(peers) + 1, len(peers) + 2))
    for w in range(NZ * NX):
        w_load(0, w).wait()
    x_load(0, 1).start()
    for i in (0, 1):
        cot_load(0, i).start()
    for w in range(NZ * NX):
        w_load(1, w).start()
    for s in (0, 1):
        x_load(1, s).start()

    for k in range(4):
        forward(0, k)
    sacc[...] = jnp.zeros_like(sacc)

    def tick(i, carry):
        a, b, c = i, i - 1, i - 2
        on_a, on_b, on_c = i >= 0, i >= 1, i >= 2
        on_f = i + 1 < n_units
        on_p = i >= 3

        def clear():
            @pl.loop(0, dm.feats // 32)
            def _(k):
                acc[pl.ds(al(k * 32, 32), 32)] = jnp.zeros((32, dm.images), F32)

        def w_start():
            for w in range(NZ * NX):
                w_load(i // 2 + 2, w).start()

        def w_wait():
            for w in range(NZ * NX):
                w_load((i + 1) // 2, w).wait()

        def first_images():
            x_load(0, 1).wait()
            prepare(0, 1)
            xp_copy(0).start()

        def cot_next():
            prepare_cot(i)

            @pl.when(i + 1 < n_units // 2)
            def _():
                for j in (0, 1):
                    cot_load(i + 1, j).start()

        steps = {
            "ws": ((i % 2 == 0) & (i // 2 + 2 < dm.towers * dm.subs), w_start),
            "ww": (on_f & (i % 2 == 1), w_wait),
            "az": (i == 0, clear),
            "p0": (i == 0, first_images),
            "ct": (i < n_units // 2, cot_next),
            "em": (on_b, lambda: emit(b)),
            "gd": (on_c, lambda: gathered(c)),
        }
        for q in range(4):
            steps[f"x1{q}"] = on_a, functools.partial(x1_send, a, q)
            steps[f"f{q}"] = on_f, functools.partial(forward, i + 1, q)
        for h in range(PIECES):
            steps[f"bw{h}"] = on_p, functools.partial(back_weight, i - 3, h)
            steps[f"bp{h}"] = on_c, functools.partial(back_pooled, c, h)
        for f in (0, 1):
            steps[f"zf{f}"] = on_b, functools.partial(z_final, b, f)
            steps[f"xf{f}"] = on_b, functools.partial(x_final, b, f)
            steps[f"zs{f}"] = on_a, functools.partial(z_sum, a, f)
            steps[f"gs{f}"] = on_b, functools.partial(gz_first, b, f)
            for h in range(3):
                steps[f"zr{h}{f}"] = on_a, functools.partial(zr_hop, a, h, f)
                steps[f"xr{h}{f}"] = on_a, functools.partial(xr_hop, a, h, f)
                steps[f"gx{h}{f}"] = on_b, functools.partial(gather_arrive, gx_copy, b, h, True, f)
                steps[f"gz{h}{f}"] = on_c, functools.partial(gather_arrive, gz_copy, c, h, False, f)
        for name in ORDER:
            pl.when(steps[name][0])(steps[name][1])

        for s in (0, 1):
            @pl.when(i == 4 + s)
            def _():
                x_load(1, s).wait()
                prepare(1, s)
                if s:
                    xp_copy(1).start()

        return carry

    lax.fori_loop(0, n_units, tick, 0)

    last, pairs = n_units - 1, dm.towers * dm.subs
    ends = {
        "em": lambda: emit(last),
        "hd": lambda: gathered(last - 1),
        "gd": lambda: gathered(last),
        "ss": sums_send,
    }
    for q in range(PIECES):
        ends[f"ya{q}"] = functools.partial(y_arrive, pairs - 2, q)
        ends[f"bv{q}"] = functools.partial(back_weight, last - 2, q)
        ends[f"bw{q}"] = functools.partial(back_weight, last - 1, q)
        ends[f"bx{q}"] = functools.partial(back_weight, last, q)
        ends[f"hp{q}"] = functools.partial(back_pooled, last - 1, q)
        ends[f"bp{q}"] = functools.partial(back_pooled, last, q)
    for f in (0, 1):
        ends[f"zf{f}"] = functools.partial(z_final, last, f)
        ends[f"xf{f}"] = functools.partial(x_final, last, f)
        ends[f"sz{f}"] = functools.partial(z4_send, last, f)
        ends[f"sx{f}"] = functools.partial(gx_send, last, f)
        ends[f"gs{f}"] = functools.partial(gz_first, last, f)
        for h in range(3):
            ends[f"gx{h}{f}"] = functools.partial(gather_arrive, gx_copy, last, h, True, f)
            ends[f"gz{h}{f}"] = functools.partial(gather_arrive, gz_copy, last, h, False, f)
            ends[f"hz{h}{f}"] = functools.partial(gather_arrive, gz_copy, last - 1, h, False, f)
    for name in DRAIN:
        ends[name]()

    for k in (1, 2, 3):
        sum_copy(k).wait_recv()
    total = sum_s[bi] + sum_r[0] + sum_r[1] + sum_r[2]
    out_b[...] = total[0:2]
    for i in (0, 1):
        out_sg[i] = total[2 + 2 * i : 4 + 2 * i]
        out_sn[i] = st[i, :, pl.ds(al(bi * BLK), BLK)] - step_ref[0] * total[2 + 2 * i : 4 + 2 * i]
    for q in range(PIECES):
        for e in (0, 1):
            own_copy(pairs - 2, q, e).wait()
        for copy in last_copies(q):
            copy.wait()
        y_copy(pairs - 2, q).wait_send()
    pg_copy(1, 1).wait()
    for i in (0, 1):
        s_copy(last - 1, i).wait()
        s_copy(last, i).wait()
    for t in range(dm.towers):
        xp_copy(t).wait_send()
    for k in (1, 2, 3):
        sum_copy(k).wait_send()
    for e in (0, 1):
        c_copy(last, e).wait_send()
    for o in range(NZ):
        x1_copy(last, o).wait_send()
    for f in (0, 1):
        for o in range(NZ):
            x5_copy(last, o, x, f).wait_send()
        z2_copy(last, f).wait_send()
        z4_copy(last, f).wait_send()
        for d in (0, 1):
            for h in range(3):
                @pl.when(far(d) <= h)
                def _():
                    xr_copy(last, d, h, f).wait_send()
                    zr_copy(last, d, h, f).wait_send()

                @pl.when((far(d) >= h) & (far(d) <= 2))
                def _():
                    gx_copy(last, d, h, f).wait_send()
                    gz_copy(last, d, h, f).wait_send()


def carry_out(*refs):
    count = len(refs) // 2
    for src, dst in zip(refs[:count], refs[count:]):
        dst[...] = src[...]


def settle(dm, _, mine, arrived, out, total, sems):
    u, step = dm.subs - 1, dm.third
    copies = []
    for q in range(PIECES):
        k = pl.ds(q * step, step)
        total[k] = mine[k] + arrived[k].astype(F32)
        for e in (0, 1):
            copies.append(
                pltpu.make_async_copy(
                    total.at[k, pl.ds(e * BLK, BLK)],
                    out.at[dm.towers - 1, k, pl.ds(e * dm.own + u * BLK, BLK)],
                    sems.at[q, e],
                )
            )
            copies[-1].start()
    for copy in copies:
        copy.wait()


def fused(pooled, weight, fc_bias, stitch, cotangent, valid_mask, image_group, step_rate):
    dm = Dims(pooled, weight, cotangent)
    towers, feats, images, own = dm.towers, dm.feats, dm.images, dm.own
    rows, rx, rz, cols = dm.rows, dm.rx, dm.rz, dm.cols
    dma = pltpu.SemaphoreType.DMA
    vm = pltpu.VMEM
    scratch = [
        vm((4, feats, cols), BF16),
        vm((towers, images, feats), BF16),
        vm((towers, feats, images), BF16),
        vm((towers, feats, images), BF16),
        vm((feats, BLK), F32),
        vm((1, images), F32),
        vm((2, 2, BLK, rows), BF16),
        vm((2, images, own), BF16),
        vm((2, rows, BLK), BF16),
        vm((2, 2, BLK, rows), BF16),
        vm((feats, images), F32),
        vm((2, rows, cols), F32),
        vm((2, images, cols), BF16),
        vm((2, images, cols // 2), BF16),
        vm((NZ, rx, BLK), BF16),
        vm((2, NZ, rx, BLK), BF16),
        vm((2, 3, rx, BLK), BF16),
        vm((2, 2, 3, rx, BLK), BF16),
        vm((2, 3, rz, NX * BLK), BF16),
        vm((2, 2, 3, rz, NX * BLK), BF16),
        vm((rz, BLK), F32),
        vm((rz, BLK), BF16),
        vm((2, rz, BLK), BF16),
        vm((2, feats, NX * BLK), F32),
        vm((feats, NX * BLK), F32),
        vm((2, feats, NX * BLK), BF16),
        vm((2, feats, NX * BLK), BF16),
        vm((images, own), F32),
        vm((max(rx, rz), BLK), F32),
        vm((feats, rows), BF16),
        vm((dm.subs, 6, 8, BLK), F32),
        vm((dm.subs, 8, BLK), F32),
        vm((3, 8, BLK), F32),
    ] + [
        dma(shape)
        for shape in (
            (4, NZ * NX), (2, 2), (NZ,), (2, NZ), (2, 3, 2), (2, 2, 3, 2), (2, 3, 2), (2, 2, 3, 2), (2,), (2, 2), (2,), (2, 2),
            (2, 3, 2), (2, 2, 3, 2), (2, 3, 2), (2, 2, 3, 2), (NZ, 2), (2, NZ, 2), (2,), (4, 2), (2, PIECES), (2, PIECES), (3,), (3,),
            (2,), (2,), (2, PIECES, 2), (), (2, 2), (2, 2), (PIECES, 2),
        )
    ]
    anyspace = pl.BlockSpec(memory_space=pl.ANY)
    inside = pl.BlockSpec(memory_space=pltpu.VMEM)
    out_shape = [
        jax.ShapeDtypeStruct((2, own, images), BF16),
        jax.ShapeDtypeStruct((towers, feats, images), BF16),
        jax.ShapeDtypeStruct((towers, feats, images), F32),
        jax.ShapeDtypeStruct((2, BLK), F32),
        jax.ShapeDtypeStruct((2, 2, BLK), F32),
        jax.ShapeDtypeStruct((2, 2, BLK), F32),
    ]
    out_specs = [anyspace] * 3 + [inside] * 3
    block = (feats, NX * BLK)
    *results, mine, theirs = pl.pallas_call(
        functools.partial(kernel, dm),
        name="stitch_fc6",
        out_shape=out_shape + [jax.ShapeDtypeStruct(block, F32), jax.ShapeDtypeStruct(block, BF16)],
        in_specs=[pl.BlockSpec(memory_space=pltpu.SMEM)] + [anyspace] * 3 + [inside] * 4,
        out_specs=out_specs + [anyspace] * 2,
        scratch_shapes=scratch,
        compiler_params=pltpu.CompilerParams(collective_id=1, has_side_effects=True, vmem_limit_bytes=61 * 2**20),
        cost_estimate=pl.CostEstimate(
            flops=6 * towers * feats * images * dm.chans, bytes_accessed=60 * 2**20, transcendentals=towers * images * own
        ),
    )(
        step_rate, weight, pooled, cotangent, fc_bias, stitch,
        valid_mask.reshape(feats // BLK, BLK), image_group.reshape(images // BLK, BLK),
    )
    arrived = lax.ppermute(theirs, "batch", [(0, 2), (1, 3), (2, 0), (3, 1)])

    def cut(shape):
        if len(shape.shape) == 3 and shape.shape[1] % (CUTS * 16) == 0:
            return pl.BlockSpec((shape.shape[0], shape.shape[1] // CUTS, shape.shape[2]), lambda c: (0, c, 0))
        return pl.BlockSpec(shape.shape, lambda c: (0,) * len(shape.shape))

    blocks = [cut(shape) for shape in out_shape]
    results = pl.pallas_call(
        carry_out,
        name="carry_out",
        grid=(CUTS,),
        out_shape=out_shape,
        in_specs=blocks,
        out_specs=blocks,
        compiler_params=pltpu.CompilerParams(vmem_limit_bytes=60 * 2**20),
        cost_estimate=pl.CostEstimate(flops=0, bytes_accessed=32 * 2**20, transcendentals=0),
    )(*results)
    weight_grad = pl.pallas_call(
        functools.partial(settle, dm),
        name="settle",
        out_shape=out_shape[2],
        in_specs=[anyspace, inside, inside],
        out_specs=anyspace,
        scratch_shapes=[vm(block, F32), dma((PIECES, 2))],
        input_output_aliases={0: 0},
        compiler_params=pltpu.CompilerParams(vmem_limit_bytes=6 * 2**20),
    )(results[2], mine, arrived)
    return *results[:2], weight_grad, *results[3:]


def gelu_local(values):
    return jax.nn.gelu(values, approximate=True)


def plain(pooled, weight, fc_bias, stitch, cotangent, valid_mask, image_group, step_rate):
    highest = lax.Precision.HIGHEST
    factor = 1.0 - image_group[None, :].astype(F32) * (1.0 - valid_mask[:, None].astype(F32))
    masked = pooled * factor.astype(BF16)[None]
    owned = weight.shape[2] // lax.axis_size("wide")
    summed = lax.psum_scatter(
        jnp.einsum("tkc,tkb->ctb", weight, masked, preferred_element_type=F32), "wide", scatter_dimension=0, tiled=True
    )
    pre_act = summed + jnp.transpose(fc_bias)[:, :, None]
    hidden, gelu_back = jax.vjp(gelu_local, pre_act)
    stitched = jnp.einsum("ijc,cjb->icb", stitch, hidden, precision=highest)
    upstream = cotangent.astype(F32)
    stitch_part = jnp.einsum("icb,cjb->ijc", upstream, hidden, precision=highest)
    hidden_grad = jnp.einsum("ijc,icb->cjb", stitch, upstream, precision=highest)
    pre_grad = gelu_back(hidden_grad)[0]
    bias_part = jnp.transpose(jnp.sum(pre_grad, axis=2))
    pre_low = pre_grad.astype(BF16)
    bias_grad = lax.psum_scatter(bias_part, "batch", scatter_dimension=1, tiled=True)
    stitch_grad = lax.psum_scatter(stitch_part, "batch", scatter_dimension=2, tiled=True)
    portion = lax.all_gather(pre_low, "wide", axis=0, tiled=True)
    input_sum = jnp.einsum("tkc,ctb->tkb", weight, portion, preferred_element_type=F32)
    block_grad = jnp.einsum("tkb,ctb->tkc", masked, portion, preferred_element_type=F32)
    pooled_grad = (input_sum * factor[None]).astype(BF16)
    weight_grad = lax.psum_scatter(block_grad, "batch", scatter_dimension=2, tiled=True)
    share = owned // lax.axis_size("batch")
    stitch_mine = lax.dynamic_slice_in_dim(stitch, lax.axis_index("batch") * share, share, 2)
    stitch_new = stitch_mine - step_rate[0] * stitch_grad
    return stitched.astype(BF16), pooled_grad, weight_grad, bias_grad, stitch_grad, stitch_new


def fits(mesh, pooled, weight, cotangent):
    return (
        (mesh.shape["wide"], mesh.shape["batch"]) == (NZ * NX, 4)
        and pooled.shape[0] == 2
        and cotangent.shape[1] == 4 * BLK
        and weight.shape[2] == NZ * NX * cotangent.shape[1]
        and pooled.shape[2] % 512 == 0
        and pooled.shape[1] % (16 * PIECES) == 0
        and pooled.shape[1] % BLK == 0
    )


def solution(mesh):
    def body(pooled, weight, fc_bias, stitch, cotangent, *rest):
        form = fused if fits(mesh, pooled, weight, cotangent) else plain
        return form(pooled, weight, fc_bias, stitch, cotangent, *rest)

    return jax.shard_map(
        body,
        mesh=mesh,
        in_specs=(
            P(None, "wide", "batch"),
            P(None, "wide", None),
            P(None, "wide"),
            P(None, None, "wide"),
            P(None, "wide", "batch"),
            P("wide"),
            P("batch"),
            P(),
        ),
        out_specs=(
            P(None, "wide", "batch"),
            P(None, "wide", "batch"),
            P(None, "wide", "batch"),
            P(None, ("wide", "batch")),
            P(None, None, ("wide", "batch")),
            P(None, None, ("wide", "batch")),
        ),
        check_vma=False,
    )
```
